256 devices in a mesh: grp: 32 (over x, z), rep: 8 (over y, core).
Axes of the slice: x: 4, y: 4, z: 8, core: 2. Of those that a mesh axis runs over, the one named last changes fastest.
Arguments:
- frames: bfloat16 [8, 2048, 1280], P('rep', 'grp'), may hold values from -6 to 6
- destination: int32 [8, 2048, 1], P('rep', 'grp'), may hold values from 0 to 31; in each aligned block of 64 rows (0 to 63, 64 to 127, ..., all dimensions but the last counted through in order) at most 4 rows name the same one
- plan: int32 [8, 32], P('rep'), may hold values from 0 to 7, never falling along the last dimension, each value on 1 to 8 neighbouring positions
- norm_gain: float32 [1280], replicated, may hold values from 0.5 to 1.5
- w_qkv: bfloat16 [1280, 3072], P(None, 'rep'), as said below
- w_out: bfloat16 [1024, 1280], P('rep'), may hold values from -0.1875 to 0.1875
Outputs:
- attended: bfloat16 [8, 2048, 1280], P('rep', 'grp')
The draws below stay inside these ranges and needn't reach their ends.
Inputs may be any that keep to these rules, and one draw needn't show every extreme that they name: `destination`: within the rows of one device no device is named more than 4 times, and in some draw blocks one is named exactly 4 times; every device of the replica is named by some row. `plan`: never falls along the devices; each group is 1 to 8 consecutive devices and one group has exactly 8. `w_qkv`: columns hold queries, keys and values in that order.
All inputs are finite; a program needn't handle non-finite values.
Results may differ from the reference program's by a relative error of at most 0.012.
The reference program's roundings to bfloat16 on the way (of `slots`, `normed`, `qkv`, `weights`, `context` and `projected`) count: a program that leaves them out, or rounds other values in their place, can miss the bound.
Values may be sent and summed in bfloat16 or wider, within the bound.
A program may use at most 64 MiB of HBM per device.

```python
import math
import jax
import jax.numpy as jnp
import numpy as np
from jax import lax

D = 1280
HEADS = 16
HEAD_DIM = 64
ROWS_DEV = 64
HD = 1024
CAP = 4
MOST = 8
GROUPS = 8
TOKENS = 2048
N_GRP = 32
N_REP = 8


def draw_w_qkv(key, part):
    key = jax.random.fold_in(key, 11)
    first = jax.random.fold_in(key, 0)
    second = jax.random.fold_in(key, 1)
    fourth = jax.random.fold_in(key, 3)
    scale = D ** (-0.5)
    query = jax.random.normal(first, (D, HD), jnp.float32) * (3.0 * scale)
    keys = jax.random.normal(second, (D, HD), jnp.float32) * scale
    vals = jax.random.normal(fourth, (D, HD), jnp.float32) * scale
    return jnp.concatenate([query, keys, vals], axis=1).astype(jnp.bfloat16)


def steps_of(own_key, extent, cuts, low, high):
    gain = 1.0
    for dim, shards_of in cuts:
        heights = jax.random.uniform(jax.random.fold_in(jax.random.fold_in(own_key, 6), dim), (shards_of,), jnp.float32, low / len(cuts), high / len(cuts))
        gain = gain * jnp.repeat(jnp.exp(heights), extent[dim] // shards_of).reshape((-1,) + (1,) * (len(extent) - 1 - dim))
    return gain


def length_profile(count, total, most, slope):
    loads = [(1 << 20) // math.isqrt(grade ** slope) + 1 for grade in range(2, count + 1)]
    spare, counts = total - most - (count - 1), [1] * (count - 1)
    while spare > 0:
        movable = [i for i in range(count - 1) if counts[i] < most]
        mass, remaining = sum([loads[i] for i in movable]), spare
        for i in movable:
            more = min(most - counts[i], max(1, remaining * loads[i] // mass), spare)
            counts[i] = counts[i] + more
            spare = spare - more
    return np.array([most] + counts)


def uneven(rng, count, total, bound, slope):
    if count == 2:
        one = jax.random.randint(rng, (), max(1, total - bound), min(bound, total - 1) + 1)
        return jnp.stack([one, total - one])
    lengths = jnp.asarray(length_profile(count, total, bound, slope), jnp.int32)
    twos = (count - 1) // 2
    donor, sink = lengths[1:1 + 2 * twos:2], lengths[2:2 + 2 * twos:2]
    room = jnp.minimum(donor - 1, bound - sink)
    moved = jax.random.randint(jax.random.fold_in(rng, 1), (twos,), 0, 1 << 20) % (room + 1)
    lengths = lengths.at[1:1 + 2 * twos:2].set(donor - moved).at[2:2 + 2 * twos:2].set(sink + moved)
    return lengths[jax.random.permutation(jax.random.fold_in(rng, 2), count)]


def shared_out(own_key, own, number, rows, count, top, most, skew):
    sequence = jax.random.permutation(own_key, count)
    crowded, usual = load_shares(count, rows * top, most, skew, True), load_shares(count, rows * top, most, skew, False)
    places = jnp.arange(count)

    def named(tallies, rotation):
        used = int((tallies > 0).sum())
        fixed = max(1, used // 4)
        passed = fixed + (places - fixed + rotation * (used - fixed)) % max(1, count - fixed)
        return jnp.zeros((count,), jnp.int32).at[sequence[jnp.where(places < fixed, places, passed)]].set(jnp.asarray(tallies, jnp.int32))

    tallies = jnp.where(number % 4 == 0, named(crowded, number // 4), named(usual, number - number // 4 - 1))
    mixed = jax.random.permutation(jax.random.fold_in(own, 3), count)
    source_of, receiver = mixed[0:count // 2 * 2:2], mixed[1:count // 2 * 2:2]
    margin = jnp.minimum(tallies[source_of] - 1, most - tallies[receiver]) // 2
    margin = jnp.where((source_of == sequence[0]) | (receiver == sequence[0]) | (tallies[receiver] == 0), 0, jnp.maximum(margin, 0))
    passed = jax.random.randint(jax.random.fold_in(own, 4), (count // 2,), 0, 1 << 20) % (margin + 1)
    tallies = tallies.at[source_of].add(-passed).at[receiver].add(passed)
    items = jnp.searchsorted(jnp.cumsum(tallies), jnp.arange(rows * top), side="right").astype(jnp.int32)
    grid = items.reshape(top, rows).T
    grid = grid[jax.random.permutation(jax.random.fold_in(own, 1), rows)]
    rotation = jax.random.randint(jax.random.fold_in(own, 2), (rows, 1), 0, top)
    return jnp.take_along_axis(grid, (jnp.arange(top)[None, :] + rotation) % top, axis=1)


def load_shares(count, total, bound, slope, full):
    portions = [(1 << 20) // math.isqrt(rank ** slope) + 1 for rank in range(1, count + 1)]
    largest = bound if full else min(bound, max(-(-total // count), total * portions[0] // sum(portions)))
    least = 1 if total - largest >= count - 1 else 0
    holding, rest = [largest] + [least] * (count - 1), total - largest - least * (count - 1)
    while rest > 0:
        movable = [i for i in range(1, count) if holding[i] < largest] or [i for i in range(1, count) if holding[i] < bound]
        whole, remaining = sum([portions[i] for i in movable]), rest
        for i in movable:
            addition = min(bound - holding[i], max(1, remaining * portions[i] // whole), rest)
            holding[i] = holding[i] + addition
            rest = rest - addition
    return np.array(holding)


def scatter_about(own_key, extent, deviation, bound, cuts=(), kind=jnp.bfloat16):
    entries = deviation * jax.random.normal(own_key, extent, jnp.float32)
    if cuts:
        entries = entries * steps_of(own_key, extent, cuts, -0.22, 0.18)
    return jnp.clip(entries, -bound, bound).astype(kind)


def setup_inputs(seed: int = 0) -> dict:
    key_list = jax.random.split(jax.random.key(seed), 7)
    frames = scatter_about(key_list[0], (N_REP, TOKENS, D), 1.0, 6.0, ((0, 8), (1, 32)))
    destination_keys = jax.random.split(jax.random.fold_in(key_list[1], 1), N_REP * TOKENS // ROWS_DEV)
    destination_turns = jax.random.permutation(jax.random.fold_in(key_list[1], 3), N_REP * TOKENS // ROWS_DEV)
    destination = jax.vmap(lambda own, number: shared_out(jax.random.fold_in(key_list[1], 2), own, number, ROWS_DEV, N_GRP, 1, CAP, 2))(destination_keys, destination_turns).reshape((N_REP, TOKENS, 1))
    plan = jax.vmap(lambda own: jnp.searchsorted(jnp.cumsum(uneven(own, GROUPS, N_GRP, MOST, 2)), jnp.arange(N_GRP), side="right"))(jax.random.split(key_list[2], N_REP)).reshape((N_REP, N_GRP)).astype(jnp.int32)
    norm_gain = jnp.clip(1.0 + 0.1 * jax.random.normal(key_list[3], (D,), jnp.float32), 0.5, 1.5)
    w_qkv = draw_w_qkv(jax.random.fold_in(key_list[6], 71), 0)
    w_out = scatter_about(key_list[5], (HD, D), HD ** -0.5, 0.1875, ((0, 8),))
    return dict(frames=frames, destination=destination, plan=plan, norm_gain=norm_gain, w_qkv=w_qkv, w_out=w_out)


def one_replica(x, dest, groups, norm_gain, w_qkv, w_out):
    slots_dev = N_GRP * CAP
    target = dest[:, 0].astype(jnp.int32)
    source = (jnp.arange(TOKENS) // ROWS_DEV).astype(jnp.int32)
    own_hot = (target[:, None] == jnp.arange(N_GRP, dtype=jnp.int32)[None, :]).astype(jnp.int32)
    blocks = own_hot.reshape(N_GRP, ROWS_DEV, N_GRP)
    counted = jnp.cumsum(blocks, axis=1)
    rank = lax.optimization_barrier(jnp.sum((counted - 1) * blocks, axis=2)).reshape(TOKENS).astype(jnp.int32)
    index = (target * slots_dev + source * CAP + rank).astype(jnp.int32)
    total = N_GRP * slots_dev
    slots = jnp.zeros((total, D), jnp.bfloat16).at[index].set(x)
    live = jnp.zeros((total,), jnp.int32).at[index].set(1)
    values = slots.astype(jnp.float32)
    mean = lax.optimization_barrier(jnp.mean(values, axis=1, keepdims=True))
    centered = values - mean
    variance = lax.optimization_barrier(jnp.mean(centered * centered, axis=1, keepdims=True))
    normed = (centered * lax.rsqrt(variance + 1e-05) * norm_gain[None, :]).astype(jnp.bfloat16)
    qkv = jnp.dot(normed, w_qkv, preferred_element_type=jnp.float32).astype(jnp.bfloat16)
    query = qkv[:, :HD]
    keys = jnp.concatenate([qkv[:, HD:2 * HD], jnp.zeros((MOST * slots_dev, HD), jnp.bfloat16)], axis=0)
    vals = jnp.concatenate([qkv[:, 2 * HD:], jnp.zeros((MOST * slots_dev, HD), jnp.bfloat16)], axis=0)
    live_pad = jnp.concatenate([live, jnp.zeros((MOST * slots_dev,), jnp.int32)])
    group_pad = jnp.concatenate([groups.astype(jnp.int32), jnp.full((MOST,), -1, jnp.int32)])
    width = MOST * slots_dev

    def per_device(device):
        mine = groups[device]
        start = jnp.sum((groups < mine).astype(jnp.int32)).astype(jnp.int32)
        first = (start * slots_dev).astype(jnp.int32)
        q_rows = lax.dynamic_slice_in_dim(query, (device * slots_dev).astype(jnp.int32), slots_dev, 0)
        k_rows = lax.dynamic_slice_in_dim(keys, first, width, 0)
        v_rows = lax.dynamic_slice_in_dim(vals, first, width, 0)
        live_rows = lax.dynamic_slice_in_dim(live_pad, first, width, 0)
        key_device = (start + jnp.arange(width, dtype=jnp.int32) // slots_dev).astype(jnp.int32)
        allowed = (live_rows == 1) & (group_pad[key_device] == mine)
        qf = q_rows.astype(jnp.float32).reshape(slots_dev, HEADS, HEAD_DIM)
        kf = k_rows.astype(jnp.float32).reshape(width, HEADS, HEAD_DIM)
        vf = v_rows.astype(jnp.float32).reshape(width, HEADS, HEAD_DIM)
        score = jnp.einsum('shd,khd->hsk', qf, kf) * HEAD_DIM ** (-0.5)
        score = jnp.where(allowed[None, None, :], score, -jnp.inf)
        top = lax.optimization_barrier(jnp.max(score, axis=2, keepdims=True))
        weights = jnp.exp(score - top)
        norm_sum = lax.optimization_barrier(jnp.sum(weights, axis=2))
        rounded = weights.astype(jnp.bfloat16).astype(jnp.float32)
        context = jnp.einsum('hsk,khd->hsd', rounded, vf) / norm_sum[:, :, None]
        return jnp.transpose(context, (1, 0, 2)).reshape(slots_dev, HD).astype(jnp.bfloat16)
    context = lax.map(per_device, jnp.arange(N_GRP, dtype=jnp.int32)).reshape(total, HD)
    projected = jnp.dot(context, w_out, preferred_element_type=jnp.float32).astype(jnp.bfloat16)
    return projected[index]

def reference(frames, destination, plan, norm_gain, w_qkv, w_out):

    def replica(items):
        return one_replica(items[0], items[1], items[2], norm_gain, w_qkv, w_out)
    return lax.map(replica, (frames, destination, plan))
```

```python
import math

import jax
import jax.numpy as jnp
from jax import lax
from jax.experimental import pallas as pl
from jax.experimental.pallas import tpu as pltpu
from jax.sharding import PartitionSpec as P

MESH = pl.DeviceIdType.MESH
NT = (((1,), (1,)), ((), ()))
BF = jnp.bfloat16
F32 = jnp.float32
D = 1280
ROWS = 64
HALF = 32
FR, DE, PL, GA, WL, WOL = 0, 1, 2, 3, 4, 5
XS, XR = 6, 10
WS, WR = 14, 15
OS, OR = 16, 20
FS, FRV = 24, 25
SBS = 26
QR = 27
GS, GR = 30, 31
PS, PR = 32, 35
CS, CR = 38, 39
NSEM = 40


def halves(block):
    return jnp.concatenate([block[:, 64:], block[:, :64]], axis=1)


def kernel(
    frames, dest, plan, gain, w_qkv, w_out, out,
    raw, dest_v, plan_v, gain_v, xb, w, wo, sb, own_g, rb, gb, vd, co, cb, spare,
    sem, line_x, line_s, line_y,
):
    g = lax.axis_index("grp")
    r = lax.axis_index("rep")
    x, z = lax.div(g, 8), lax.rem(g, 8)
    y, c = lax.div(r, 2), lax.rem(r, 2)
    cls = lax.rem(z, 2)
    slot = lax.div(z, 2) * 4 + x

    def at(tx, ty, tz, tc):
        return (tx * 8 + tz, ty * 2 + tc)

    def along_x(i):
        return at(lax.rem(x + i, 4), y, z, c)

    def along_y(i):
        return at(x, lax.rem(y + i, 4), z, c)

    sibling = at(x, y, z, 1 - c)

    def remote(src, dst, ssem, rsem, target):
        return pltpu.make_async_remote_copy(
            src_ref=src, dst_ref=dst, send_sem=sem.at[ssem], recv_sem=sem.at[rsem],
            device_id=target, device_id_type=MESH,
        )

    def local(src, dst, s):
        return pltpu.make_async_copy(src, dst, sem.at[s])

    def push(src, dst, ssem, rsem, tx, ty, tz, tc, dummy):
        same = (tx == x) & (ty == y) & (tz == z) & (tc == c)

        @pl.when(jnp.logical_not(same))
        def _():
            remote(src, dst, ssem, rsem, at(tx, ty, tz, tc)).start()

        @pl.when(same)
        def _():
            local(src, dst, rsem).start()
            local(src, spare.at[dummy], ssem).start()

    def drain(ref, s):
        local(ref, ref, s).wait()

    loads = [
        local(frames.at[0], raw, FR),
        local(dest.at[0], dest_v, DE),
        local(plan, plan_v, PL),
        local(gain, gain_v, GA),
        local(w_qkv, w.at[c], WL),
        local(w_out, wo.at[c, y], WOL),
    ]
    for load in loads:
        load.start()

    barrier = pltpu.get_barrier_semaphore()
    partners = [sibling] + [along_y(i) for i in (1, 2, 3)] + [along_x(i) for i in (1, 2, 3)]
    partners += [at(x, y, lax.rem(z + i, 8), c) for i in range(1, 8)]
    for partner in partners:
        pl.semaphore_signal(barrier, inc=1, device_id=partner, device_id_type=MESH)

    loads[0].wait()
    loads[3].wait()
    values = raw[...].astype(F32)
    mean = jnp.mean(values, axis=1, keepdims=True)
    centered = values - mean
    variance = jnp.mean(centered * centered, axis=1, keepdims=True)
    xb[0] = (centered * lax.rsqrt(variance + 1e-05) * gain_v[...]).astype(BF)

    pl.semaphore_wait(barrier, len(partners))

    for i in (1, 3, 2):
        remote(xb.at[0], xb.at[i], XS + i, XR + i, along_y(4 - i)).start()
    remote(w_qkv, w.at[c], WS, WR, sibling).start()
    for i in (1, 2, 3):
        pl.semaphore_signal(line_x, inc=1, device_id=along_x(i), device_id_type=MESH)

    loads[1].wait()
    loads[2].wait()
    hot = dest_v[...] == lax.broadcasted_iota(jnp.int32, (ROWS, 32), 1)
    group = jnp.sum(jnp.where(hot, plan_v[...].astype(F32), 0.0), axis=1, keepdims=True)
    low = lax.broadcasted_iota(jnp.int32, (1, 128), 1) < 64
    own_g[...] = jnp.where(low, group[:HALF], group[HALF:]).astype(BF)

    def project(i):
        block = xb[i]
        for s in range(2):
            part = jnp.dot(block, w[s], preferred_element_type=F32)
            for p in range(3):
                two = part[:, 128 * p : 128 * p + 128]
                top, bottom = two[:HALF], two[HALF:]
                sb[i, 6 * s + 2 * p] = jnp.where(low, top, halves(bottom)).astype(BF)
                sb[i, 6 * s + 2 * p + 1] = jnp.where(low, halves(top), bottom).astype(BF)

    def scatter(i):
        tz = lax.rem(y + i, 4) + 4 * c

        def one(j, carry):
            sub = 3 * y + lax.div(j, 4)
            kind, block = lax.div(sub, 4), lax.rem(sub, 4)
            ty = block + 1 - 2 * lax.rem(block, 2)
            push(
                sb.at[i, j], rb.at[kind, cls, pl.ds(slot * HALF, HALF)], SBS, QR + kind,
                lax.rem(j, 4), ty, tz, cls, 0,
            )
            return carry

        lax.fori_loop(0, 12, one, 0)

    loads[4].wait()
    remote(w_qkv, w.at[1 - c], WS, WR, sibling).wait_recv()
    project(0)

    pl.semaphore_wait(line_x, 3)
    pl.semaphore_signal(line_s, inc=1, device_id=sibling, device_id_type=MESH)
    pl.semaphore_wait(line_s, 1)
    for i in (1, 2, 3):
        pl.semaphore_signal(line_y, inc=1, device_id=along_y(i), device_id_type=MESH)
    pl.semaphore_wait(line_y, 3)

    def tell(j, carry):
        push(
            own_g, gb.at[cls, pl.ds(slot * HALF, HALF)], GS, GR,
            lax.rem(j, 4), lax.div(j, 4), y + 4 * c, cls, 1,
        )
        return carry

    lax.fori_loop(0, 16, tell, 0)
    scatter(0)
    for i in (1, 3, 2):
        remote(xb.at[0], xb.at[i], XS + i, XR + i, along_y(4 - i)).wait_recv()
        project(i)
        scatter(i)
    loads[5].wait()
    for i in (1, 3, 2):
        remote(
            wo.at[c, y], wo.at[c, y], OS + i, OR + i, along_y(4 - i)
        ).start()

    mine = [rb.at[1, c], rb.at[2, c], gb.at[c]]
    theirs = [rb.at[1, 1 - c], rb.at[2, 1 - c], gb.at[1 - c]]
    for n, s in enumerate((QR + 1, QR + 2, GR)):
        drain(mine[n], s)
        remote(mine[n], mine[n], PS + n, PR + n, sibling).start()
    drain(rb.at[0, c], QR)
    for n in range(3):
        drain(theirs[n], PR + n)

    first = lax.broadcasted_iota(jnp.int32, (8, 128), 1)
    groups = gb[...].reshape(1024, 128)
    key_low = lax.dot_general(
        jnp.where(first == 0, 1.0, 0.0).astype(BF), groups, NT, preferred_element_type=F32
    )[0:1]
    key_high = lax.dot_general(
        jnp.where(first == 64, 1.0, 0.0).astype(BF), groups, NT, preferred_element_type=F32
    )[0:1]
    vals = rb[2].reshape(1024, 128)
    vals_turned = halves(vals)
    vd[0:1024, :] = jnp.where(low, vals, vals_turned)
    vd[1024:2048, :] = jnp.where(low, vals_turned, vals)
    head = (y + 1 - 2 * lax.rem(y, 2)) * 4 + x
    owner_y, owner_c = lax.rem(z, 4), lax.div(z, 4)
    scale = 0.125 * math.log2(math.e)

    def attend(n, carry):
        m = lax.rem(lax.div(z, 2) + 2 + n * 3, 4)
        rows = pl.ds(pl.multiple_of(m * 128, 128), 128)
        q = rb[0, c, rows, :]
        turned = halves(q)
        none = jnp.zeros_like(q)
        q_low = jnp.concatenate([jnp.where(low, q, none), jnp.where(low, turned, none)], axis=0)
        q_high = jnp.concatenate([jnp.where(low, none, turned), jnp.where(low, none, q)], axis=0)
        gq = gb[c, rows, :].astype(F32)
        gq = jnp.concatenate([gq[:, 0:1], gq[:, 64:65]], axis=0)
        keys = rb[1].reshape(1024, 128)
        s_low = lax.dot_general(q_low, keys, NT, preferred_element_type=F32)
        s_high = lax.dot_general(q_high, keys, NT, preferred_element_type=F32)
        s_low = jnp.where(gq == key_low, s_low, -jnp.inf)
        s_high = jnp.where(gq == key_high, s_high, -jnp.inf)
        top = jnp.maximum(
            jnp.max(s_low, axis=1, keepdims=True), jnp.max(s_high, axis=1, keepdims=True)
        )
        p_low = jnp.exp2((s_low - top) * scale)
        p_high = jnp.exp2((s_high - top) * scale)
        total = jnp.sum(p_low, axis=1, keepdims=True) + jnp.sum(p_high, axis=1, keepdims=True)
        context = jnp.dot(p_low.astype(BF), vd[0:1024, :], preferred_element_type=F32)
        context += jnp.dot(p_high.astype(BF), vd[1024:2048, :], preferred_element_type=F32)
        context = context / total
        co[rows, :] = jnp.where(low, context[:128], context[128:]).astype(BF)
        for i in range(4):
            push(
                co.at[pl.ds(m * 128 + HALF * i, HALF)],
                cb.at[lax.div(x, 2), lax.div(head, 4), lax.rem(x, 2)],
                CS, CR, i, owner_y, 2 * m + c, owner_c, 2,
            )
        return carry

    lax.fori_loop(0, 4, attend, 0)

    for i in (1, 2, 3):
        remote(wo.at[c, y], wo.at[c, lax.rem(y + i, 4)], OS + i, OR + i, along_y(4 - i)).wait_recv()
    remote(wo.at[c], wo.at[c], FS, FRV, sibling).start()

    drain(cb, CR)
    pieces = []
    for tc in range(2):
        for ty in range(4):
            even, odd = cb[tc, ty, 0], cb[tc, ty, 1]
            pieces.append(
                jnp.concatenate(
                    [jnp.where(low, even, halves(odd)), jnp.where(low, halves(even), odd)], axis=0
                )
            )
    context = jnp.concatenate(pieces, axis=1)
    remote(wo.at[c], wo.at[1 - c], FS, FRV, sibling).wait_recv()
    for n in range(5):
        cols = slice(256 * n, 256 * n + 256)
        weights = wo[:, :, :, cols].reshape(1024, 256)
        out[0, :, cols] = jnp.dot(context, weights, preferred_element_type=F32).astype(BF)

    for i in (1, 2, 3):
        remote(xb.at[0], xb.at[i], XS + i, XR + i, along_y(4 - i)).wait_send()
        remote(wo.at[c, y], wo.at[c, y], OS + i, OR + i, along_y(4 - i)).wait_send()
    remote(w_qkv, w.at[c], WS, WR, sibling).wait_send()
    remote(wo.at[c], wo.at[c], FS, FRV, sibling).wait_send()
    drain(sb, SBS)
    for n in range(3):
        remote(mine[n], mine[n], PS + n, PR + n, sibling).wait_send()
    drain(gb.at[c], GS)
    drain(co, CS)


def shards(frames, destination, plan, norm_gain, w_qkv, w_out):
    any_space = pl.BlockSpec(memory_space=pl.ANY)
    return pl.pallas_call(
        kernel,
        out_shape=jax.ShapeDtypeStruct((1, ROWS, D), BF),
        in_specs=[any_space] * 6,
        out_specs=pl.BlockSpec(memory_space=pltpu.VMEM),
        scratch_shapes=[
            pltpu.VMEM((ROWS, D), BF),
            pltpu.VMEM((ROWS, 1), jnp.int32),
            pltpu.VMEM((1, 32), jnp.int32),
            pltpu.VMEM((1, D), F32),
            pltpu.VMEM((4, ROWS, D), BF),
            pltpu.VMEM((2, D, 384), BF),
            pltpu.VMEM((2, 4, 128, D), BF),
            pltpu.VMEM((4, 12, HALF, 128), BF),
            pltpu.VMEM((HALF, 128), BF),
            pltpu.VMEM((3, 2, 512, 128), BF),
            pltpu.VMEM((2, 512, 128), BF),
            pltpu.VMEM((2048, 128), BF),
            pltpu.VMEM((512, 128), BF),
            pltpu.VMEM((2, 4, 2, HALF, 128), BF),
            pltpu.VMEM((3, HALF, 128), BF),
            pltpu.SemaphoreType.DMA((NSEM,)),
            pltpu.SemaphoreType.REGULAR,
            pltpu.SemaphoreType.REGULAR,
            pltpu.SemaphoreType.REGULAR,
        ],
        compiler_params=pltpu.CompilerParams(
            collective_id=0, has_side_effects=True, vmem_limit_bytes=48 * 2**20
        ),
        name="attend",
    )(frames, destination, plan, norm_gain.reshape(1, D), w_qkv, w_out)


def solution(mesh):
    in_specs = (
        P("rep", "grp", None),
        P("rep", "grp", None),
        P("rep", None),
        P(),
        P(None, "rep"),
        P("rep", None),
    )
    out_specs = P("rep", "grp", None)
    return jax.shard_map(shards, mesh=mesh, in_specs=in_specs, out_specs=out_specs, check_vma=False)
```

```python
import math

import jax
import jax.numpy as jnp
from jax import lax
from jax.experimental import pallas as pl
from jax.experimental.pallas import tpu as pltpu
from jax.sharding import PartitionSpec as P

MESH = pl.DeviceIdType.MESH
NT = (((1,), (1,)), ((), ()))
BF = jnp.bfloat16
F32 = jnp.float32
D = 1280
ROWS = 64
HALF = 32
FR, DE, PL, GA, WL, WOL = 0, 1, 2, 3, 4, 5
XS, XR = 6, 10
WS, WR = 14, 15
OS, OR = 16, 20
FS, FT = 24, 28
SBS = 32
QR = 33
GS, GR = 36, 37
PS, PR = 38, 41
CS, CR = 44, 45
NSEM = 46


def halves(block):
    return jnp.concatenate([block[:, 64:], block[:, :64]], axis=1)


def kernel(
    frames, dest, plan, gain, w_qkv, w_out, out,
    raw, dest_v, plan_v, gain_v, xb, w, wo, sb, own_g, rb, gb, vd, co, cb, acc, top_v, sum_v,
    spare, spare_g, sem, line_x, line_y,
):
    g = lax.axis_index("grp")
    r = lax.axis_index("rep")
    x, z = lax.div(g, 8), lax.rem(g, 8)
    y, c = lax.div(r, 2), lax.rem(r, 2)
    cls = lax.rem(z, 2)
    slot = lax.div(z, 2) * 4 + x

    def at(tx, ty, tz, tc):
        return (tx * 8 + tz, ty * 2 + tc)

    def turn_x(i):
        return lax.rem(x + i, 4)

    def along_y(i):
        return at(x, lax.rem(y + i, 4), z, c)

    sibling = at(x, y, z, 1 - c)

    def remote(src, dst, ssem, rsem, target):
        return pltpu.make_async_remote_copy(
            src_ref=src, dst_ref=dst, send_sem=sem.at[ssem], recv_sem=sem.at[rsem],
            device_id=target, device_id_type=MESH,
        )

    def local(src, dst, s):
        return pltpu.make_async_copy(src, dst, sem.at[s])

    def push(src, dst, ssem, rsem, tx, ty, tz, tc, dummy):
        if dummy is None:
            remote(src, dst, ssem, rsem, at(tx, ty, tz, tc)).start()
            return
        same = (ty == y) & (tz == z) & (tc == c)

        @pl.when(jnp.logical_not(same))
        def _():
            remote(src, dst, ssem, rsem, at(tx, ty, tz, tc)).start()

        @pl.when(same)
        def _():
            local(src, dst, rsem).start()
            local(src, dummy, ssem).start()

    def drain(ref, s):
        local(ref, ref, s).wait()

    loads = [
        local(frames.at[0], raw, FR),
        local(dest, dest_v, DE),
        local(plan, plan_v, PL),
        local(gain, gain_v, GA),
        local(w_qkv, w.at[c], WL),
        local(w_out, wo.at[c, y], WOL),
    ]
    for load in loads:
        load.start()

    barrier = pltpu.get_barrier_semaphore()
    plane = [at(turn_x(i), y, z, c) for i in (1, 2, 3)]
    plane += [at(turn_x(i), y, z, 1 - c) for i in range(4)]
    partners = [along_y(i) for i in (1, 2, 3)] + plane
    partners += [at(x, y, lax.rem(z + i, 8), c) for i in range(1, 8)]
    for partner in partners:
        pl.semaphore_signal(barrier, inc=1, device_id=partner, device_id_type=MESH)

    low = lax.broadcasted_iota(jnp.int32, (1, 128), 1) < 64
    loads[1].wait()
    loads[2].wait()
    row32 = lax.broadcasted_iota(jnp.int32, (32, 32), 0)
    col32 = lax.broadcasted_iota(jnp.int32, (32, 32), 1)
    plan_rows = jnp.sum(
        jnp.where(row32 == col32, plan_v[...].astype(F32), 0.0), axis=1, keepdims=True
    )
    hot = dest_v[...] == lax.broadcasted_iota(jnp.int32, (32, ROWS), 0)
    group = jnp.sum(jnp.where(hot, plan_rows, 0.0), axis=0, keepdims=True)
    own_g[...] = jnp.concatenate([group, group], axis=1)

    loads[0].wait()
    loads[3].wait()
    values = raw[...].astype(F32)
    mean = jnp.mean(values, axis=1, keepdims=True)
    centered = values - mean
    variance = jnp.mean(centered * centered, axis=1, keepdims=True)
    xb[0] = (centered * lax.rsqrt(variance + 1e-05) * gain_v[...][None, :]).astype(BF)

    pl.semaphore_wait(barrier, len(partners))

    for i in (1, 3, 2):
        remote(xb.at[0], xb.at[i], XS + i, XR + i, along_y(4 - i)).start()
    remote(w_qkv, w.at[c], WS, WR, sibling).start()
    for partner in plane:
        pl.semaphore_signal(line_x, inc=1, device_id=partner, device_id_type=MESH)

    def project(i, s):
        part = jnp.dot(xb[i], w[s], preferred_element_type=F32)
        for p in range(3):
            two = part[:, 128 * p : 128 * p + 128]
            upper, lower = two[:HALF], two[HALF:]
            sb[i, 6 * s + 2 * p] = jnp.where(low, upper, halves(lower)).astype(BF)
            sb[i, 6 * s + 2 * p + 1] = jnp.where(low, halves(upper), lower).astype(BF)

    def scatter(i):
        tz = lax.rem(y + i, 4) + 4 * c
        for s in range(3):
            sub = 3 * y + s
            kind, block = lax.div(sub, 4), lax.rem(sub, 4)
            ty = block + 1 - 2 * lax.rem(block, 2)
            for k in (2, 1, 3, 0):
                push(
                    sb.at[i, 4 * s + turn_x(k)], rb.at[kind, cls, pl.ds(slot * HALF, HALF)],
                    SBS, QR + kind, turn_x(k), ty, tz, cls, None if k else spare.at[0],
                )

    loads[4].wait()
    project(0, c)
    pl.semaphore_wait(line_x, len(plane))
    for i in (1, 2, 3):
        pl.semaphore_signal(line_y, inc=1, device_id=along_y(i), device_id_type=MESH)
    remote(w_qkv, w.at[1 - c], WS, WR, sibling).wait_recv()
    project(0, 1 - c)
    pl.semaphore_wait(line_y, 3)

    scatter(0)
    for k in (2, 1, 3, 0):
        for i in (2, 1, 3, 0):
            push(
                own_g, gb.at[cls, slot], GS, GR, turn_x(k), lax.rem(y + i, 4), y + 4 * c, cls,
                None if k or i else spare_g,
            )
    for i in (1, 3, 2):
        remote(xb.at[0], xb.at[i], XS + i, XR + i, along_y(4 - i)).wait_recv()
        project(i, 0)
        project(i, 1)
        scatter(i)
    loads[5].wait()
    for i in (1, 3, 2):
        remote(wo.at[c, y], wo.at[c, y], OS + i, OR + i, along_y(4 - i)).start()

    def to_sibling(i):
        ty = lax.rem(y + i, 4)
        return remote(wo.at[c, ty], wo.at[c, ty], FS + i, FT + i, sibling)

    to_sibling(0).start()

    mine = [rb.at[1, c], rb.at[2, c], gb.at[c]]
    theirs = [rb.at[1, 1 - c], rb.at[2, 1 - c], gb.at[1 - c]]
    for n, s in ((2, GR), (0, QR + 1), (1, QR + 2)):
        drain(mine[n], s)
        remote(mine[n], mine[n], PS + n, PR + n, sibling).start()
    drain(rb.at[0, c], QR)

    lane = lax.broadcasted_iota(jnp.int32, (1, 512), 1)
    depth = lax.broadcasted_iota(jnp.int32, (128, 512), 0)
    source = lax.broadcasted_iota(jnp.int32, (16, 512), 0) == lax.div(lane, HALF)

    def key_groups(half):
        table = jnp.concatenate([gb[half, n] for n in range(16)], axis=0).astype(BF)
        both = []
        for base in (0, HALF):
            spread = jnp.where(depth == lax.rem(lane, HALF) + base, 1.0, 0.0).astype(BF)
            wide = jnp.dot(table, spread, preferred_element_type=F32)
            both.append(jnp.sum(jnp.where(source, wide, 0.0), axis=0, keepdims=True))
        return both

    def spread_values(half):
        vals = rb[2, half]
        turned = halves(vals)
        vd[half, 0:512, :] = jnp.where(low, vals, turned)
        vd[half, 512:1024, :] = jnp.where(low, turned, vals)

    head = (y + 1 - 2 * lax.rem(y, 2)) * 4 + x
    owner_y, owner_c = lax.rem(z, 4), lax.div(z, 4)
    scale = 0.125 * math.log2(math.e)
    row = lax.rem(lax.broadcasted_iota(jnp.int32, (128, 128), 0), HALF)
    col = lax.broadcasted_iota(jnp.int32, (128, 128), 1)

    def chunk(n):
        return lax.rem(lax.div(z, 2) + 2 + n * 3, 4)

    def scores(m, half, key_low, key_high):
        rows = pl.ds(pl.multiple_of(m * 128, 128), 128)
        q = rb[0, c, rows, :]
        turned = halves(q)
        none = jnp.zeros_like(q)
        q_low = jnp.concatenate([jnp.where(low, q, none), jnp.where(low, turned, none)], axis=0)
        q_high = jnp.concatenate([jnp.where(low, none, turned), jnp.where(low, none, q)], axis=0)
        mine_g = jnp.concatenate(
            [jnp.broadcast_to(gb[c, 4 * m + n], (HALF, 128)) for n in range(4)], axis=0
        )
        gq = jnp.concatenate(
            [
                jnp.sum(jnp.where(col == row + base, mine_g, 0.0), axis=1, keepdims=True)
                for base in (0, HALF)
            ],
            axis=0,
        )
        keys = rb[1, half]
        s_low = lax.dot_general(q_low, keys, NT, preferred_element_type=F32)
        s_high = lax.dot_general(q_high, keys, NT, preferred_element_type=F32)
        s_low = jnp.where(gq == key_low, s_low, -jnp.inf)
        s_high = jnp.where(gq == key_high, s_high, -jnp.inf)
        top = jnp.maximum(
            jnp.max(s_low, axis=1, keepdims=True), jnp.max(s_high, axis=1, keepdims=True)
        )
        return s_low, s_high, top

    def weigh(s_low, s_high, top, half):
        p_low = jnp.exp2((s_low - top) * scale)
        p_high = jnp.exp2((s_high - top) * scale)
        total = jnp.sum(p_low, axis=1, keepdims=True) + jnp.sum(p_high, axis=1, keepdims=True)
        mixed = jnp.dot(p_low.astype(BF), vd[half, 0:512, :], preferred_element_type=F32)
        mixed += jnp.dot(p_high.astype(BF), vd[half, 512:1024, :], preferred_element_type=F32)
        return total, mixed

    key_low, key_high = key_groups(c)
    spread_values(c)

    def first_half(n, carry):
        s_low, s_high, top = scores(chunk(n), c, key_low, key_high)
        total, mixed = weigh(s_low, s_high, top, c)
        top_v[n] = top
        sum_v[n] = total
        acc[n] = mixed
        return carry

    lax.fori_loop(0, 4, first_half, 0)

    for n in range(3):
        drain(theirs[n], PR + n)
    other_low, other_high = key_groups(1 - c)
    spread_values(1 - c)

    def second_half(n, carry):
        m = chunk(n)
        s_low, s_high, top = scores(m, 1 - c, other_low, other_high)
        before = top_v[n]
        top = jnp.maximum(before, top)
        total, mixed = weigh(s_low, s_high, top, 1 - c)
        factor = jnp.exp2((before - top) * scale)
        context = (acc[n] * factor + mixed) / (sum_v[n] * factor + total)
        co[pl.ds(pl.multiple_of(m * 128, 128), 128), :] = jnp.where(
            low, context[:128], context[128:]
        ).astype(BF)
        for k in (2, 1, 3, 0):
            push(
                co.at[pl.ds(m * 128 + HALF * turn_x(k), HALF)],
                cb.at[lax.div(x, 2), lax.div(head, 4), lax.rem(x, 2)],
                CS, CR, turn_x(k), owner_y, 2 * m + c, owner_c, None if k else spare.at[1],
            )
        return carry

    lax.fori_loop(0, 4, second_half, 0)

    for i in (1, 3, 2):
        remote(wo.at[c, y], wo.at[c, lax.rem(y + i, 4)], OS + i, OR + i, along_y(4 - i)).wait_recv()
        to_sibling(i).start()

    drain(cb, CR)
    pieces = []
    for tc in range(2):
        for ty in range(4):
            even, odd = cb[tc, ty, 0], cb[tc, ty, 1]
            pieces.append(
                jnp.concatenate(
                    [jnp.where(low, even, halves(odd)), jnp.where(low, halves(even), odd)], axis=0
                )
            )
    context = jnp.concatenate(pieces, axis=1)
    for i in range(4):
        ty = lax.rem(y + i, 4)
        remote(wo.at[c, ty], wo.at[1 - c, ty], FS + i, FT + i, sibling).wait_recv()
    for n in range(5):
        cols = slice(256 * n, 256 * n + 256)
        weights = wo[:, :, :, cols].reshape(1024, 256)
        out[0, :, cols] = jnp.dot(context, weights, preferred_element_type=F32).astype(BF)

    for i in (1, 2, 3):
        remote(xb.at[0], xb.at[i], XS + i, XR + i, along_y(4 - i)).wait_send()
        remote(wo.at[c, y], wo.at[c, y], OS + i, OR + i, along_y(4 - i)).wait_send()
    remote(w_qkv, w.at[c], WS, WR, sibling).wait_send()
    for i in range(4):
        to_sibling(i).wait_send()
    drain(sb, SBS)
    for n in range(3):
        remote(mine[n], mine[n], PS + n, PR + n, sibling).wait_send()
    drain(gb.at[c], GS)
    drain(co, CS)


SCRATCH = [
    pltpu.VMEM((ROWS, D), BF),
    pltpu.VMEM((1, ROWS), jnp.int32),
    pltpu.VMEM((1, 32), jnp.int32),
    pltpu.VMEM((D,), F32),
    pltpu.VMEM((4, ROWS, D), BF),
    pltpu.VMEM((2, D, 384), BF),
    pltpu.VMEM((2, 4, 128, D), BF),
    pltpu.VMEM((4, 12, HALF, 128), BF),
    pltpu.VMEM((1, 128), F32),
    pltpu.VMEM((3, 2, 512, 128), BF),
    pltpu.VMEM((2, 16, 1, 128), F32),
    pltpu.VMEM((2, 1024, 128), BF),
    pltpu.VMEM((512, 128), BF),
    pltpu.VMEM((2, 4, 2, HALF, 128), BF),
    pltpu.VMEM((4, 256, 128), F32),
    pltpu.VMEM((4, 256, 1), F32),
    pltpu.VMEM((4, 256, 1), F32),
    pltpu.VMEM((2, HALF, 128), BF),
    pltpu.VMEM((1, 128), F32),
    pltpu.SemaphoreType.DMA((NSEM,)),
    pltpu.SemaphoreType.REGULAR,
    pltpu.SemaphoreType.REGULAR,
]


def shards(frames, destination, plan, norm_gain, w_qkv, w_out):
    any_space = pl.BlockSpec(memory_space=pl.ANY)
    return pl.pallas_call(
        kernel,
        out_shape=jax.ShapeDtypeStruct((1, ROWS, D), BF),
        in_specs=[any_space] * 6,
        out_specs=pl.BlockSpec(memory_space=pltpu.VMEM),
        scratch_shapes=SCRATCH,
        compiler_params=pltpu.CompilerParams(
            collective_id=0, has_side_effects=True, vmem_limit_bytes=60 * 2**20
        ),
        name="attend",
    )(frames, destination.reshape(1, ROWS), plan, norm_gain, w_qkv, w_out)


def solution(mesh):
    in_specs = (
        P("rep", "grp", None),
        P("rep", "grp", None),
        P("rep", None),
        P(),
        P(None, "rep"),
        P("rep", None),
    )
    out_specs = P("rep", "grp", None)
    return jax.shard_map(shards, mesh=mesh, in_specs=in_specs, out_specs=out_specs, check_vma=False)
```

```python
import math

import jax
import jax.numpy as jnp
from jax import lax
from jax.experimental import pallas as pl
from jax.experimental.pallas import tpu as pltpu
from jax.sharding import PartitionSpec as P

MESH = pl.DeviceIdType.MESH
NT = (((1,), (1,)), ((), ()))
BF = jnp.bfloat16
F32 = jnp.float32
D = 1280
ROWS = 64
HALF = 32
FR, DE, PL, GA, WL, WOL = 0, 1, 2, 3, 4, 5
XS, XR = 6, 10
WS, WR = 14, 15
OS, OR = 16, 20
FS, FT = 24, 28
SBS = 32
QR = 33
GS, GR = 36, 37
PS, PR = 38, 41
CS, CR = 44, 45
NSEM = 46


def halves(block):
    return jnp.concatenate([block[:, 64:], block[:, :64]], axis=1)


def kernel(
    frames, dest, plan, gain, w_qkv, w_out, out,
    raw, dest_v, plan_v, gain_v, xb, w, wo, sb, own_g, rb, gb, key_mark, query_mark, vd, co, cb, acc, top_v,
    sum_v, spare, spare_g, sem, line_x, line_y,
):
    g = lax.axis_index("grp")
    r = lax.axis_index("rep")
    x, z = lax.div(g, 8), lax.rem(g, 8)
    y, c = lax.div(r, 2), lax.rem(r, 2)
    cls = lax.rem(z, 2)
    slot = lax.div(z, 2) * 4 + x

    def at(tx, ty, tz, tc):
        return (tx * 8 + tz, ty * 2 + tc)

    def turn_x(i):
        return lax.rem(x + i, 4)

    def along_y(i):
        return at(x, lax.rem(y + i, 4), z, c)

    sibling = at(x, y, z, 1 - c)

    def remote(src, dst, ssem, rsem, target):
        return pltpu.make_async_remote_copy(
            src_ref=src, dst_ref=dst, send_sem=sem.at[ssem], recv_sem=sem.at[rsem],
            device_id=target, device_id_type=MESH,
        )

    def local(src, dst, s):
        return pltpu.make_async_copy(src, dst, sem.at[s])

    def push(src, dst, ssem, rsem, tx, ty, tz, tc, dummy):
        if dummy is None:
            remote(src, dst, ssem, rsem, at(tx, ty, tz, tc)).start()
            return
        same = (ty == y) & (tz == z) & (tc == c)

        @pl.when(jnp.logical_not(same))
        def _():
            remote(src, dst, ssem, rsem, at(tx, ty, tz, tc)).start()

        @pl.when(same)
        def _():
            local(src, dst, rsem).start()
            local(src, dummy, ssem).start()

    def drain(ref, s):
        local(ref, ref, s).wait()

    loads = [
        local(frames.at[0], raw, FR),
        local(dest, dest_v, DE),
        local(plan, plan_v, PL),
        local(gain, gain_v, GA),
        local(w_qkv, w.at[c], WL),
        local(w_out, wo.at[c, y], WOL),
    ]
    for load in loads:
        load.start()

    barrier = pltpu.get_barrier_semaphore()
    plane = [at(turn_x(i), y, z, c) for i in (1, 2, 3)]
    plane += [at(turn_x(i), y, z, 1 - c) for i in range(4)]
    partners = [along_y(i) for i in (1, 2, 3)] + plane
    partners += [at(x, y, lax.rem(z + i, 8), c) for i in range(1, 8)]
    for partner in partners:
        pl.semaphore_signal(barrier, inc=1, device_id=partner, device_id_type=MESH)

    low = lax.broadcasted_iota(jnp.int32, (1, 128), 1) < 64
    loads[1].wait()
    loads[2].wait()
    row32 = lax.broadcasted_iota(jnp.int32, (32, 32), 0)
    col32 = lax.broadcasted_iota(jnp.int32, (32, 32), 1)
    plan_rows = jnp.sum(
        jnp.where(row32 == col32, plan_v[...].astype(F32), 0.0), axis=1, keepdims=True
    )
    hot = dest_v[...] == lax.broadcasted_iota(jnp.int32, (32, ROWS), 0)
    group = jnp.sum(jnp.where(hot, plan_rows, 0.0), axis=0, keepdims=True)
    own_g[...] = jnp.concatenate([group, group], axis=1)

    loads[0].wait()
    loads[3].wait()
    values = raw[...].astype(F32)
    mean = jnp.mean(values, axis=1, keepdims=True)
    centered = values - mean
    variance = jnp.mean(centered * centered, axis=1, keepdims=True)
    xb[0] = (centered * lax.rsqrt(variance + 1e-05) * gain_v[...][None, :]).astype(BF)

    pl.semaphore_wait(barrier, len(partners))

    for i in (1, 3, 2):
        remote(xb.at[0], xb.at[i], XS + i, XR + i, along_y(4 - i)).start()
    remote(w_qkv, w.at[c], WS, WR, sibling).start()
    for partner in plane:
        pl.semaphore_signal(line_x, inc=1, device_id=partner, device_id_type=MESH)

    def project(i, s):
        part = jnp.dot(xb[i], w[s], preferred_element_type=F32)
        for p in range(3):
            two = part[:, 128 * p : 128 * p + 128]
            upper, lower = two[:HALF], two[HALF:]
            sb[i, 6 * s + 2 * p] = jnp.where(low, upper, halves(lower)).astype(BF)
            sb[i, 6 * s + 2 * p + 1] = jnp.where(low, halves(upper), lower).astype(BF)

    def scatter(i):
        tz = lax.rem(y + i, 4) + 4 * c
        for s in range(3):
            sub = 3 * y + s
            kind, block = lax.div(sub, 4), lax.rem(sub, 4)
            ty = block + 1 - 2 * lax.rem(block, 2)
            for k in (2, 1, 3, 0):
                push(
                    sb.at[i, 4 * s + turn_x(k)], rb.at[kind, cls, pl.ds(slot * HALF, HALF)],
                    SBS, QR + kind, turn_x(k), ty, tz, cls, None if k else spare.at[0],
                )

    loads[4].wait()
    project(0, c)
    pl.semaphore_wait(line_x, len(plane))
    for i in (1, 2, 3):
        pl.semaphore_signal(line_y, inc=1, device_id=along_y(i), device_id_type=MESH)
    remote(w_qkv, w.at[1 - c], WS, WR, sibling).wait_recv()
    project(0, 1 - c)
    pl.semaphore_wait(line_y, 3)

    scatter(0)
    for k in (2, 1, 3, 0):
        for i in (2, 1, 3, 0):
            push(
                own_g, gb.at[cls, slot], GS, GR, turn_x(k), lax.rem(y + i, 4), y + 4 * c, cls,
                None if k or i else spare_g,
            )
    for i in (1, 3, 2):
        remote(xb.at[0], xb.at[i], XS + i, XR + i, along_y(4 - i)).wait_recv()
        project(i, 0)
        project(i, 1)
        scatter(i)
    loads[5].wait()
    for i in (1, 3, 2):
        remote(wo.at[c, y], wo.at[c, y], OS + i, OR + i, along_y(4 - i)).start()

    def to_sibling(i):
        ty = lax.rem(y + i, 4)
        return remote(wo.at[c, ty], wo.at[c, ty], FS + i, FT + i, sibling)

    to_sibling(0).start()

    mine = [rb.at[1, c], rb.at[2, c], gb.at[c]]
    theirs = [rb.at[1, 1 - c], rb.at[2, 1 - c], gb.at[1 - c]]

    def swap(n, s):
        drain(mine[n], s)
        remote(mine[n], mine[n], PS + n, PR + n, sibling).start()

    lane = lax.broadcasted_iota(jnp.int32, (1, 128), 1)
    lane_group = jnp.where(lane < 64, lax.rem(lax.div(lane, 4), 8), -1).astype(F32)
    row = lax.rem(lax.broadcasted_iota(jnp.int32, (128, 128), 0), HALF)
    col = lax.broadcasted_iota(jnp.int32, (128, 128), 1)

    def group_columns(half, m):
        table = jnp.concatenate(
            [jnp.broadcast_to(gb[half, 4 * m + n], (HALF, 128)) for n in range(4)], axis=0
        )
        return [
            jnp.sum(jnp.where(col == row + base, table, 0.0), axis=1, keepdims=True)
            for base in (0, HALF)
        ]

    def mark_keys(half, m):
        for_low, for_high = group_columns(half, m)
        hit = jnp.where(lane < 32, for_low, for_high) == lane_group
        key_mark[half, 128 * m : 128 * m + 128, :] = jnp.where(hit, 1.0, 0.0).astype(BF)
        if half is not c:
            return
        group = jnp.concatenate([for_low, for_high], axis=0)
        miss = jnp.where(group == lane_group, 0.0, -(2.0**127))
        query_mark[0, m] = jnp.where(lane < 32, miss, 0.0).astype(BF)
        query_mark[1, m] = jnp.where((lane >= 32) & (lane < 64), miss, 0.0).astype(BF)

    swap(2, GR)
    for m in range(4):
        mark_keys(c, m)
    drain(theirs[2], PR + 2)
    for m in range(4):
        mark_keys(1 - c, m)
    swap(0, QR + 1)
    swap(1, QR + 2)
    drain(rb.at[0, c], QR)

    def spread_values(half):
        vals = rb[2, half]
        turned = halves(vals)
        vd[half, 0:512, :] = jnp.where(low, vals, turned)
        vd[half, 512:1024, :] = jnp.where(low, turned, vals)

    head = (y + 1 - 2 * lax.rem(y, 2)) * 4 + x
    owner_y, owner_c = lax.rem(z, 4), lax.div(z, 4)
    scale = 0.125 * math.log2(math.e)

    def chunk(n):
        return lax.rem(lax.div(z, 2) + 2 + n * 3, 4)

    def scores(m, half):
        q = rb[0, c, pl.ds(pl.multiple_of(m * 128, 128), 128), :]
        turned = halves(q)
        none = jnp.zeros_like(q)
        q_low = jnp.concatenate([jnp.where(low, q, none), jnp.where(low, turned, none)], axis=0)
        q_high = jnp.concatenate([jnp.where(low, none, turned), jnp.where(low, none, q)], axis=0)
        keys = jnp.concatenate([rb[1, half], key_mark[half]], axis=1)
        both = [
            lax.dot_general(
                jnp.concatenate([part, query_mark[n, m]], axis=1), keys, NT,
                preferred_element_type=F32,
            )
            for n, part in enumerate((q_low, q_high))
        ]
        top = jnp.maximum(
            jnp.max(both[0], axis=1, keepdims=True), jnp.max(both[1], axis=1, keepdims=True)
        )
        return both[0], both[1], top

    def weigh(s_low, s_high, top, half):
        p_low = jnp.exp2((s_low - top) * scale)
        p_high = jnp.exp2((s_high - top) * scale)
        total = jnp.sum(p_low, axis=1, keepdims=True) + jnp.sum(p_high, axis=1, keepdims=True)
        mixed = jnp.dot(p_low.astype(BF), vd[half, 0:512, :], preferred_element_type=F32)
        mixed += jnp.dot(p_high.astype(BF), vd[half, 512:1024, :], preferred_element_type=F32)
        return total, mixed

    spread_values(c)
    for n in range(4):
        s_low, s_high, top = scores(chunk(n), c)
        total, mixed = weigh(s_low, s_high, top, c)
        top_v[n] = top
        sum_v[n] = total
        acc[n] = mixed

    drain(theirs[0], PR)
    drain(theirs[1], PR + 1)
    spread_values(1 - c)
    for n in range(4):
        m = chunk(n)
        s_low, s_high, top = scores(m, 1 - c)
        before = top_v[n]
        top = jnp.maximum(before, top)
        total, mixed = weigh(s_low, s_high, top, 1 - c)
        factor = jnp.exp2((before - top) * scale)
        context = (acc[n] * factor + mixed) / (sum_v[n] * factor + total)
        co[pl.ds(pl.multiple_of(m * 128, 128), 128), :] = jnp.where(
            low, context[:128], context[128:]
        ).astype(BF)
        for k in (2, 1, 3, 0):
            push(
                co.at[pl.ds(m * 128 + HALF * turn_x(k), HALF)],
                cb.at[lax.div(x, 2), lax.div(head, 4), lax.rem(x, 2)],
                CS, CR, turn_x(k), owner_y, 2 * m + c, owner_c, None if k else spare.at[1],
            )

    for i in (1, 3, 2):
        remote(wo.at[c, y], wo.at[c, lax.rem(y + i, 4)], OS + i, OR + i, along_y(4 - i)).wait_recv()
        to_sibling(i).start()

    drain(cb, CR)
    pieces = []
    for tc in range(2):
        for ty in range(4):
            even, odd = cb[tc, ty, 0], cb[tc, ty, 1]
            pieces.append(
                jnp.concatenate(
                    [jnp.where(low, even, halves(odd)), jnp.where(low, halves(even), odd)], axis=0
                )
            )
    context = jnp.concatenate(pieces, axis=1)
    for i in range(4):
        ty = lax.rem(y + i, 4)
        remote(wo.at[c, ty], wo.at[1 - c, ty], FS + i, FT + i, sibling).wait_recv()
    for n in range(5):
        cols = slice(256 * n, 256 * n + 256)
        weights = wo[:, :, :, cols].reshape(1024, 256)
        out[0, :, cols] = jnp.dot(context, weights, preferred_element_type=F32).astype(BF)

    for i in (1, 2, 3):
        remote(xb.at[0], xb.at[i], XS + i, XR + i, along_y(4 - i)).wait_send()
        remote(wo.at[c, y], wo.at[c, y], OS + i, OR + i, along_y(4 - i)).wait_send()
    remote(w_qkv, w.at[c], WS, WR, sibling).wait_send()
    for i in range(4):
        to_sibling(i).wait_send()
    drain(sb, SBS)
    for n in range(3):
        remote(mine[n], mine[n], PS + n, PR + n, sibling).wait_send()
    drain(gb.at[c], GS)
    drain(co, CS)


SCRATCH = [
    pltpu.VMEM((ROWS, D), BF),
    pltpu.VMEM((1, ROWS), jnp.int32),
    pltpu.VMEM((1, 32), jnp.int32),
    pltpu.VMEM((D,), F32),
    pltpu.VMEM((4, ROWS, D), BF),
    pltpu.VMEM((2, D, 384), BF),
    pltpu.VMEM((2, 4, 128, D), BF),
    pltpu.VMEM((4, 12, HALF, 128), BF),
    pltpu.VMEM((1, 128), F32),
    pltpu.VMEM((3, 2, 512, 128), BF),
    pltpu.VMEM((2, 16, 1, 128), F32),
    pltpu.VMEM((2, 512, 128), BF),
    pltpu.VMEM((2, 4, 256, 128), BF),
    pltpu.VMEM((2, 1024, 128), BF),
    pltpu.VMEM((512, 128), BF),
    pltpu.VMEM((2, 4, 2, HALF, 128), BF),
    pltpu.VMEM((4, 256, 128), F32),
    pltpu.VMEM((4, 256, 1), F32),
    pltpu.VMEM((4, 256, 1), F32),
    pltpu.VMEM((2, HALF, 128), BF),
    pltpu.VMEM((1, 128), F32),
    pltpu.SemaphoreType.DMA((NSEM,)),
    pltpu.SemaphoreType.REGULAR,
    pltpu.SemaphoreType.REGULAR,
]


def shards(frames, destination, plan, norm_gain, w_qkv, w_out):
    any_space = pl.BlockSpec(memory_space=pl.ANY)
    return pl.pallas_call(
        kernel,
        out_shape=jax.ShapeDtypeStruct((1, ROWS, D), BF),
        in_specs=[any_space] * 6,
        out_specs=pl.BlockSpec(memory_space=pltpu.VMEM),
        scratch_shapes=SCRATCH,
        compiler_params=pltpu.CompilerParams(
            collective_id=0, has_side_effects=True, vmem_limit_bytes=60 * 2**20
        ),
        name="attend",
    )(frames, destination.reshape(1, ROWS), plan, norm_gain, w_qkv, w_out)


def solution(mesh):
    in_specs = (
        P("rep", "grp", None),
        P("rep", "grp", None),
        P("rep", None),
        P(),
        P(None, "rep"),
        P("rep", None),
    )
    out_specs = P("rep", "grp", None)
    return jax.shard_map(shards, mesh=mesh, in_specs=in_specs, out_specs=out_specs, check_vma=False)
```

```python
import math

import jax
import jax.numpy as jnp
from jax import lax
from jax.experimental import pallas as pl
from jax.experimental.pallas import tpu as pltpu
from jax.sharding import PartitionSpec as P

MESH = pl.DeviceIdType.MESH
NT = (((1,), (1,)), ((), ()))
BF = jnp.bfloat16
F32 = jnp.float32
D = 1280
ROWS = 64
HALF = 32
FR, DE, PL, GA, WL, WOL = 0, 1, 2, 3, 4, 5
XS, XR = 6, 12
WS, WR = 18, 19
OS, OR = 20, 24
QS, QV = 28, 32
FS, FT = 36, 40
SBS = 44
QR = 45
GS, GR = 48, 49
PS, PR = 50, 53
CS, CR = 56, 57
NSEM = 58


def halves(block):
    return jnp.concatenate([block[:, 64:], block[:, :64]], axis=1)


def kernel(
    frames, dest, plan, gain, w_qkv, w_out, out,
    raw, dest_v, plan_v, gain_v, xb, w, wo, sb, own_g, rb, gb, key_mark, query_mark, vd, co, cb, acc, top_v,
    sum_v, spare, spare_g, sem, line_x, line_y, line_z,
):
    g = lax.axis_index("grp")
    r = lax.axis_index("rep")
    x, z = lax.div(g, 8), lax.rem(g, 8)
    y, c = lax.div(r, 2), lax.rem(r, 2)
    cls = lax.rem(z, 2)
    slot = lax.div(z, 2) * 4 + x

    def at(tx, ty, tz, tc):
        return (tx * 8 + tz, ty * 2 + tc)

    def turn_x(i):
        return lax.rem(x + i, 4)

    def along_x(i):
        return at(turn_x(i), y, z, c)

    def along_y(i):
        return at(x, lax.rem(y + i, 4), z, c)

    def along_z(i):
        return at(x, y, lax.rem(z + i, 8), c)

    sibling = at(x, y, z, 1 - c)

    def remote(src, dst, ssem, rsem, target):
        return pltpu.make_async_remote_copy(
            src_ref=src, dst_ref=dst, send_sem=sem.at[ssem], recv_sem=sem.at[rsem],
            device_id=target, device_id_type=MESH,
        )

    def local(src, dst, s):
        return pltpu.make_async_copy(src, dst, sem.at[s])

    def push(src, dst, ssem, rsem, tx, ty, tz, tc, dummy):
        if dummy is None:
            remote(src, dst, ssem, rsem, at(tx, ty, tz, tc)).start()
            return
        same = (ty == y) & (tz == z) & (tc == c)

        @pl.when(jnp.logical_not(same))
        def _():
            remote(src, dst, ssem, rsem, at(tx, ty, tz, tc)).start()

        @pl.when(same)
        def _():
            local(src, dst, rsem).start()
            local(src, dummy, ssem).start()

    def drain(ref, s):
        local(ref, ref, s).wait()

    loads = [
        local(frames.at[0], raw, FR),
        local(dest, dest_v, DE),
        local(plan, plan_v, PL),
        local(gain, gain_v, GA),
        local(w_qkv, w.at[c], WL),
        local(w_out, wo.at[c, y], WOL),
    ]
    for load in loads:
        load.start()

    barrier = pltpu.get_barrier_semaphore()
    plane = [at(turn_x(i), y, z, c) for i in (1, 2, 3)]
    plane += [at(turn_x(i), y, z, 1 - c) for i in range(4)]
    partners = [along_y(i) for i in (1, 2, 3)] + plane
    partners += [along_z(i) for i in (1, 2, 6, 7)]
    for partner in partners:
        pl.semaphore_signal(barrier, inc=1, device_id=partner, device_id_type=MESH)

    low = lax.broadcasted_iota(jnp.int32, (1, 128), 1) < 64
    loads[1].wait()
    loads[2].wait()
    row32 = lax.broadcasted_iota(jnp.int32, (32, 32), 0)
    col32 = lax.broadcasted_iota(jnp.int32, (32, 32), 1)
    plan_rows = jnp.sum(
        jnp.where(row32 == col32, plan_v[...].astype(F32), 0.0), axis=1, keepdims=True
    )
    hot = dest_v[...] == lax.broadcasted_iota(jnp.int32, (32, ROWS), 0)
    group = jnp.sum(jnp.where(hot, plan_rows, 0.0), axis=0, keepdims=True)
    own_g[...] = jnp.concatenate([group, group], axis=1)

    loads[0].wait()
    loads[3].wait()
    values = raw[...].astype(F32)
    mean = jnp.mean(values, axis=1, keepdims=True)
    centered = values - mean
    variance = jnp.mean(centered * centered, axis=1, keepdims=True)
    xb[0] = (centered * lax.rsqrt(variance + 1e-05) * gain_v[...][None, :]).astype(BF)

    pl.semaphore_wait(barrier, len(partners))

    upper, lower = pl.ds(0, HALF), pl.ds(HALF, HALF)

    def row_copy(n):
        block, to, part, source = (
            (1, 3, upper, 0), (3, 1, lower, 0), (1, 3, lower, 0), (3, 1, upper, 0),
            (2, 3, upper, 1), (2, 1, lower, 3),
        )[n]
        return remote(xb.at[source, part], xb.at[block, part], XS + n, XR + n, along_y(to))

    for n in range(4):
        row_copy(n).start()
    remote(w_qkv, w.at[c], WS, WR, sibling).start()
    for i in (2, 6):
        pl.semaphore_signal(line_z, inc=1, device_id=along_z(i), device_id_type=MESH)

    def project(i, s):
        part = jnp.dot(xb[i], w[s], preferred_element_type=F32)
        for p in range(3):
            two = part[:, 128 * p : 128 * p + 128]
            first, last = two[:HALF], two[HALF:]
            sb[i, 6 * s + 2 * p] = jnp.where(low, first, halves(last)).astype(BF)
            sb[i, 6 * s + 2 * p + 1] = jnp.where(low, halves(first), last).astype(BF)

    def scatter(i):
        tz = lax.rem(y + i, 4) + 4 * c
        for s in range(3):
            sub = 3 * y + s
            kind, block = lax.div(sub, 4), lax.rem(sub, 4)
            ty = block + 1 - 2 * lax.rem(block, 2)
            for k in (2, 1, 3, 0):
                push(
                    sb.at[i, 4 * s + turn_x(k)], rb.at[kind, cls, pl.ds(slot * HALF, HALF)],
                    SBS, QR + kind, turn_x(k), ty, tz, cls, None if k else spare.at[0],
                )

    loads[4].wait()
    project(0, c)
    pl.semaphore_wait(line_z, 2)
    for partner in plane:
        pl.semaphore_signal(line_x, inc=1, device_id=partner, device_id_type=MESH)
    for n in (0, 1):
        row_copy(n).wait_recv()
        row_copy(4 + n).start()
    pl.semaphore_wait(line_x, len(plane))
    for i in (1, 2, 3):
        pl.semaphore_signal(line_y, inc=1, device_id=along_y(i), device_id_type=MESH)
    remote(w_qkv, w.at[1 - c], WS, WR, sibling).wait_recv()
    project(0, 1 - c)
    pl.semaphore_wait(line_y, 3)

    scatter(0)
    for k in (2, 1, 3, 0):
        for i in (2, 1, 3, 0):
            push(
                own_g, gb.at[cls, slot], GS, GR, turn_x(k), lax.rem(y + i, 4), y + 4 * c, cls,
                None if k or i else spare_g,
            )
    for i, arrivals in ((1, (2,)), (3, (3,)), (2, (4, 5))):
        for n in arrivals:
            row_copy(n).wait_recv()
        project(i, 0)
        project(i, 1)
        scatter(i)
    loads[5].wait()
    opposite = lax.rem(y + 2, 4)

    def quarter(ty, tx):
        return wo.at[c, ty, pl.ds(pl.multiple_of(tx * HALF, HALF), HALF)]

    def shard_copy(i):
        ref = quarter(y, x) if i == 2 else wo.at[c, y]
        return remote(ref, ref, OS + i, OR + i, along_y(4 - i))

    def quarter_copy(i):
        ref = quarter(opposite, x)
        return remote(ref, ref, QS + i, QV + i, along_x(i))

    for i in (2, 1, 3):
        shard_copy(i).start()

    def to_sibling(i):
        ty = lax.rem(y + i, 4)
        return remote(wo.at[c, ty], wo.at[c, ty], FS + i, FT + i, sibling)

    to_sibling(0).start()

    mine = [rb.at[1, c], rb.at[2, c], gb.at[c]]
    theirs = [rb.at[1, 1 - c], rb.at[2, 1 - c], gb.at[1 - c]]

    def swap(n, s):
        drain(mine[n], s)
        remote(mine[n], mine[n], PS + n, PR + n, sibling).start()

    lane = lax.broadcasted_iota(jnp.int32, (1, 128), 1)
    lane_group = jnp.where(lane < 64, lax.rem(lax.div(lane, 4), 8), -1).astype(F32)
    row = lax.rem(lax.broadcasted_iota(jnp.int32, (128, 128), 0), HALF)
    col = lax.broadcasted_iota(jnp.int32, (128, 128), 1)

    def group_columns(half, m):
        table = jnp.concatenate(
            [jnp.broadcast_to(gb[half, 4 * m + n], (HALF, 128)) for n in range(4)], axis=0
        )
        return [
            jnp.sum(jnp.where(col == row + base, table, 0.0), axis=1, keepdims=True)
            for base in (0, HALF)
        ]

    def mark_keys(half, m):
        for_low, for_high = group_columns(half, m)
        hit = jnp.where(lane < 32, for_low, for_high) == lane_group
        key_mark[half, 128 * m : 128 * m + 128, :] = jnp.where(hit, 1.0, 0.0).astype(BF)
        if half is not c:
            return
        group = jnp.concatenate([for_low, for_high], axis=0)
        miss = jnp.where(group == lane_group, 0.0, -(2.0**127))
        query_mark[0, m] = jnp.where(lane < 32, miss, 0.0).astype(BF)
        query_mark[1, m] = jnp.where((lane >= 32) & (lane < 64), miss, 0.0).astype(BF)

    swap(2, GR)
    for m in range(4):
        mark_keys(c, m)
    drain(theirs[2], PR + 2)
    for m in range(4):
        mark_keys(1 - c, m)
    shard_copy(2).wait_recv()
    for i in (1, 2, 3):
        quarter_copy(i).start()
    swap(0, QR + 1)
    swap(1, QR + 2)
    drain(rb.at[0, c], QR)

    def spread_values(half):
        vals = rb[2, half]
        turned = halves(vals)
        vd[half, 0:512, :] = jnp.where(low, vals, turned)
        vd[half, 512:1024, :] = jnp.where(low, turned, vals)

    head = (y + 1 - 2 * lax.rem(y, 2)) * 4 + x
    owner_y, owner_c = lax.rem(z, 4), lax.div(z, 4)
    scale = 0.125 * math.log2(math.e)

    def chunk(n):
        return lax.rem(lax.div(z, 2) + 2 + n * 3, 4)

    def scores(m, half):
        q = rb[0, c, pl.ds(pl.multiple_of(m * 128, 128), 128), :]
        turned = halves(q)
        none = jnp.zeros_like(q)
        q_low = jnp.concatenate([jnp.where(low, q, none), jnp.where(low, turned, none)], axis=0)
        q_high = jnp.concatenate([jnp.where(low, none, turned), jnp.where(low, none, q)], axis=0)
        keys = jnp.concatenate([rb[1, half], key_mark[half]], axis=1)
        both = [
            lax.dot_general(
                jnp.concatenate([part, query_mark[n, m]], axis=1), keys, NT,
                preferred_element_type=F32,
            )
            for n, part in enumerate((q_low, q_high))
        ]
        top = jnp.maximum(
            jnp.max(both[0], axis=1, keepdims=True), jnp.max(both[1], axis=1, keepdims=True)
        )
        return both[0], both[1], top

    def weigh(s_low, s_high, top, half):
        p_low = jnp.exp2((s_low - top) * scale)
        p_high = jnp.exp2((s_high - top) * scale)
        total = jnp.sum(p_low, axis=1, keepdims=True) + jnp.sum(p_high, axis=1, keepdims=True)
        mixed = jnp.dot(p_low.astype(BF), vd[half, 0:512, :], preferred_element_type=F32)
        mixed += jnp.dot(p_high.astype(BF), vd[half, 512:1024, :], preferred_element_type=F32)
        return total, mixed

    spread_values(c)
    for n in range(4):
        s_low, s_high, top = scores(chunk(n), c)
        total, mixed = weigh(s_low, s_high, top, c)
        top_v[n] = top
        sum_v[n] = total
        acc[n] = mixed

    drain(theirs[0], PR)
    drain(theirs[1], PR + 1)
    spread_values(1 - c)
    for n in range(4):
        m = chunk(n)
        s_low, s_high, top = scores(m, 1 - c)
        before = top_v[n]
        top = jnp.maximum(before, top)
        total, mixed = weigh(s_low, s_high, top, 1 - c)
        factor = jnp.exp2((before - top) * scale)
        context = (acc[n] * factor + mixed) / (sum_v[n] * factor + total)
        co[pl.ds(pl.multiple_of(m * 128, 128), 128), :] = jnp.where(
            low, context[:128], context[128:]
        ).astype(BF)
        for k in (2, 1, 3, 0):
            push(
                co.at[pl.ds(m * 128 + HALF * turn_x(k), HALF)],
                cb.at[lax.div(x, 2), lax.div(head, 4), lax.rem(x, 2)],
                CS, CR, turn_x(k), owner_y, 2 * m + c, owner_c, None if k else spare.at[1],
            )

    for i in (1, 3, 2):
        if i == 2:
            for k in (1, 2, 3):
                quarter_copy(k).wait_recv()
        else:
            shard_copy(i).wait_recv()
        to_sibling(i).start()

    drain(cb, CR)
    pieces = []
    for tc in range(2):
        for ty in range(4):
            even, odd = cb[tc, ty, 0], cb[tc, ty, 1]
            pieces.append(
                jnp.concatenate(
                    [jnp.where(low, even, halves(odd)), jnp.where(low, halves(even), odd)], axis=0
                )
            )
    context = jnp.concatenate(pieces, axis=1)
    for i in range(4):
        ty = lax.rem(y + i, 4)
        remote(wo.at[c, ty], wo.at[1 - c, ty], FS + i, FT + i, sibling).wait_recv()
    for n in range(5):
        cols = slice(256 * n, 256 * n + 256)
        weights = wo[:, :, :, cols].reshape(1024, 256)
        out[0, :, cols] = jnp.dot(context, weights, preferred_element_type=F32).astype(BF)

    for n in range(6):
        row_copy(n).wait_send()
    for i in (1, 2, 3):
        shard_copy(i).wait_send()
        quarter_copy(i).wait_send()
    remote(w_qkv, w.at[c], WS, WR, sibling).wait_send()
    for i in range(4):
        to_sibling(i).wait_send()
    drain(sb, SBS)
    for n in range(3):
        remote(mine[n], mine[n], PS + n, PR + n, sibling).wait_send()
    drain(gb.at[c], GS)
    drain(co, CS)


SCRATCH = [
    pltpu.VMEM((ROWS, D), BF),
    pltpu.VMEM((1, ROWS), jnp.int32),
    pltpu.VMEM((1, 32), jnp.int32),
    pltpu.VMEM((D,), F32),
    pltpu.VMEM((4, ROWS, D), BF),
    pltpu.VMEM((2, D, 384), BF),
    pltpu.VMEM((2, 4, 128, D), BF),
    pltpu.VMEM((4, 12, HALF, 128), BF),
    pltpu.VMEM((1, 128), F32),
    pltpu.VMEM((3, 2, 512, 128), BF),
    pltpu.VMEM((2, 16, 1, 128), F32),
    pltpu.VMEM((2, 512, 128), BF),
    pltpu.VMEM((2, 4, 256, 128), BF),
    pltpu.VMEM((2, 1024, 128), BF),
    pltpu.VMEM((512, 128), BF),
    pltpu.VMEM((2, 4, 2, HALF, 128), BF),
    pltpu.VMEM((4, 256, 128), F32),
    pltpu.VMEM((4, 256, 1), F32),
    pltpu.VMEM((4, 256, 1), F32),
    pltpu.VMEM((2, HALF, 128), BF),
    pltpu.VMEM((1, 128), F32),
    pltpu.SemaphoreType.DMA((NSEM,)),
    pltpu.SemaphoreType.REGULAR,
    pltpu.SemaphoreType.REGULAR,
    pltpu.SemaphoreType.REGULAR,
]


def shards(frames, destination, plan, norm_gain, w_qkv, w_out):
    any_space = pl.BlockSpec(memory_space=pl.ANY)
    return pl.pallas_call(
        kernel,
        out_shape=jax.ShapeDtypeStruct((1, ROWS, D), BF),
        in_specs=[any_space] * 6,
        out_specs=pl.BlockSpec(memory_space=pltpu.VMEM),
        scratch_shapes=SCRATCH,
        compiler_params=pltpu.CompilerParams(
            collective_id=0, has_side_effects=True, vmem_limit_bytes=60 * 2**20
        ),
        name="attend",
    )(frames, destination.reshape(1, ROWS), plan, norm_gain, w_qkv, w_out)


def solution(mesh):
    in_specs = (
        P("rep", "grp", None),
        P("rep", "grp", None),
        P("rep", None),
        P(),
        P(None, "rep"),
        P("rep", None),
    )
    out_specs = P("rep", "grp", None)
    return jax.shard_map(shards, mesh=mesh, in_specs=in_specs, out_specs=out_specs, check_vma=False)
```

```python
import math

import jax
import jax.numpy as jnp
from jax import lax
from jax.experimental import pallas as pl
from jax.experimental.pallas import tpu as pltpu
from jax.sharding import PartitionSpec as P

MESH = pl.DeviceIdType.MESH
NT = (((1,), (1,)), ((), ()))
BF = jnp.bfloat16
F32 = jnp.float32
D = 1280
ROWS = 64
HALF = 32
FR, DE, PL, GA, WL, WOL = 0, 1, 2, 3, 4, 5
XS, XR = 6, 12
WS, WR = 18, 19
OS, OR = 20, 24
QS, QV = 28, 32
FS, FT = 36, 40
SBS = 44
QR = 45
GS, GR = 48, 49
PS, PR = 50, 53
CS, CR = 56, 57
NSEM = 58


def halves(block):
    return jnp.concatenate([block[:, 64:], block[:, :64]], axis=1)


def kernel(
    frames, dest, plan, gain, w_qkv, w_out, out, wo,
    raw, dest_v, plan_v, gain_v, xb, w, sb, own_g, rb, gb, key_mark, query_mark, vd, co, cb, acc, top_v,
    sum_v, spare, spare_g, sem, line_x, line_y, line_z,
):
    g = lax.axis_index("grp")
    r = lax.axis_index("rep")
    x, z = lax.div(g, 8), lax.rem(g, 8)
    y, c = lax.div(r, 2), lax.rem(r, 2)
    cls = lax.rem(z, 2)
    slot = lax.div(z, 2) * 4 + x

    def at(tx, ty, tz, tc):
        return (tx * 8 + tz, ty * 2 + tc)

    def turn_x(i):
        return lax.rem(x + i, 4)

    def along_x(i):
        return at(turn_x(i), y, z, c)

    def along_y(i):
        return at(x, lax.rem(y + i, 4), z, c)

    def along_z(i):
        return at(x, y, lax.rem(z + i, 8), c)

    sibling = at(x, y, z, 1 - c)

    def remote(src, dst, ssem, rsem, target):
        return pltpu.make_async_remote_copy(
            src_ref=src, dst_ref=dst, send_sem=sem.at[ssem], recv_sem=sem.at[rsem],
            device_id=target, device_id_type=MESH,
        )

    def local(src, dst, s):
        return pltpu.make_async_copy(src, dst, sem.at[s])

    def push(src, dst, ssem, rsem, tx, ty, tz, tc, dummy):
        if dummy is None:
            remote(src, dst, ssem, rsem, at(tx, ty, tz, tc)).start()
            return
        same = (ty == y) & (tz == z) & (tc == c)

        @pl.when(jnp.logical_not(same))
        def _():
            remote(src, dst, ssem, rsem, at(tx, ty, tz, tc)).start()

        @pl.when(same)
        def _():
            local(src, dst, rsem).start()
            local(src, dummy, ssem).start()

    def drain(ref, s):
        local(ref, ref, s).wait()

    loads = [
        local(frames.at[0], raw, FR),
        local(dest, dest_v, DE),
        local(plan, plan_v, PL),
        local(gain, gain_v, GA),
        local(w_qkv, w.at[c], WL),
        local(w_out, wo.at[c, y], WOL),
    ]
    for load in loads:
        load.start()

    barrier = pltpu.get_barrier_semaphore()
    plane = [at(turn_x(i), y, z, c) for i in (1, 2, 3)]
    plane += [at(turn_x(i), y, z, 1 - c) for i in range(4)]
    partners = [along_y(i) for i in (1, 2, 3)] + plane
    partners += [along_z(i) for i in (1, 2, 6, 7)]
    for partner in partners:
        pl.semaphore_signal(barrier, inc=1, device_id=partner, device_id_type=MESH)

    low = lax.broadcasted_iota(jnp.int32, (1, 128), 1) < 64
    loads[1].wait()
    loads[2].wait()
    row32 = lax.broadcasted_iota(jnp.int32, (32, 32), 0)
    col32 = lax.broadcasted_iota(jnp.int32, (32, 32), 1)
    plan_rows = jnp.sum(
        jnp.where(row32 == col32, plan_v[...].astype(F32), 0.0), axis=1, keepdims=True
    )
    hot = dest_v[...] == lax.broadcasted_iota(jnp.int32, (32, ROWS), 0)
    group = jnp.sum(jnp.where(hot, plan_rows, 0.0), axis=0, keepdims=True)
    own_g[...] = jnp.concatenate([group, group], axis=1)

    loads[0].wait()
    loads[3].wait()
    values = raw[...].astype(F32)
    mean = jnp.mean(values, axis=1, keepdims=True)
    centered = values - mean
    variance = jnp.mean(centered * centered, axis=1, keepdims=True)
    xb[0] = (centered * lax.rsqrt(variance + 1e-05) * gain_v[...][None, :]).astype(BF)

    pl.semaphore_wait(barrier, len(partners))

    upper, lower = pl.ds(0, HALF), pl.ds(HALF, HALF)

    def row_copy(n):
        block, to, part, source = (
            (1, 3, upper, 0), (3, 1, lower, 0), (1, 3, lower, 0), (3, 1, upper, 0),
            (2, 3, upper, 1), (2, 1, lower, 3),
        )[n]
        return remote(xb.at[source, part], xb.at[block, part], XS + n, XR + n, along_y(to))

    for n in range(4):
        row_copy(n).start()
    remote(w_qkv, w.at[c], WS, WR, sibling).start()
    for i in (2, 6):
        pl.semaphore_signal(line_z, inc=1, device_id=along_z(i), device_id_type=MESH)

    def project(i, s):
        part = jnp.dot(xb[i], w[s], preferred_element_type=F32)
        for p in range(3):
            two = part[:, 128 * p : 128 * p + 128]
            first, last = two[:HALF], two[HALF:]
            sb[i, 6 * s + 2 * p] = jnp.where(low, first, halves(last)).astype(BF)
            sb[i, 6 * s + 2 * p + 1] = jnp.where(low, halves(first), last).astype(BF)

    def scatter(i):
        tz = lax.rem(y + i, 4) + 4 * c
        for s in range(3):
            sub = 3 * y + s
            kind, block = lax.div(sub, 4), lax.rem(sub, 4)
            ty = block + 1 - 2 * lax.rem(block, 2)
            for k in (2, 1, 3, 0):
                push(
                    sb.at[i, 4 * s + turn_x(k)], rb.at[kind, cls, pl.ds(slot * HALF, HALF)],
                    SBS, QR + kind, turn_x(k), ty, tz, cls, None if k else spare.at[0],
                )

    loads[4].wait()
    project(0, c)
    pl.semaphore_wait(line_z, 2)
    for partner in plane:
        pl.semaphore_signal(line_x, inc=1, device_id=partner, device_id_type=MESH)
    for n in (0, 1):
        row_copy(n).wait_recv()
        row_copy(4 + n).start()
    pl.semaphore_wait(line_x, len(plane))
    for i in (1, 2, 3):
        pl.semaphore_signal(line_y, inc=1, device_id=along_y(i), device_id_type=MESH)
    remote(w_qkv, w.at[1 - c], WS, WR, sibling).wait_recv()
    project(0, 1 - c)
    pl.semaphore_wait(line_y, 3)

    scatter(0)
    for k in (2, 1, 3, 0):
        for i in (2, 1, 3, 0):
            push(
                own_g, gb.at[cls, slot], GS, GR, turn_x(k), lax.rem(y + i, 4), y + 4 * c, cls,
                None if k or i else spare_g,
            )
    for i, arrivals in ((1, (2,)), (3, (3,)), (2, (4, 5))):
        for n in arrivals:
            row_copy(n).wait_recv()
        project(i, 0)
        project(i, 1)
        scatter(i)
    loads[5].wait()
    opposite = lax.rem(y + 2, 4)

    def quarter(ty, tx):
        return wo.at[c, ty, pl.ds(pl.multiple_of(tx * HALF, HALF), HALF)]

    def shard_copy(i):
        ref = quarter(y, x) if i == 2 else wo.at[c, y]
        return remote(ref, ref, OS + i, OR + i, along_y(4 - i))

    def quarter_copy(i):
        ref = quarter(opposite, x)
        return remote(ref, ref, QS + i, QV + i, along_x(i))

    for i in (2, 1, 3):
        shard_copy(i).start()

    def to_sibling(i):
        ty = lax.rem(y + i, 4)
        return remote(wo.at[c, ty], wo.at[c, ty], FS + i, FT + i, sibling)

    to_sibling(0).start()

    mine = [rb.at[1, c], rb.at[2, c], gb.at[c]]
    theirs = [rb.at[1, 1 - c], rb.at[2, 1 - c], gb.at[1 - c]]

    def swap(n, s):
        drain(mine[n], s)
        remote(mine[n], mine[n], PS + n, PR + n, sibling).start()

    lane = lax.broadcasted_iota(jnp.int32, (1, 128), 1)
    lane_group = jnp.where(lane < 64, lax.rem(lax.div(lane, 4), 8), -1).astype(F32)
    row = lax.rem(lax.broadcasted_iota(jnp.int32, (128, 128), 0), HALF)
    col = lax.broadcasted_iota(jnp.int32, (128, 128), 1)

    def group_columns(half, m):
        table = jnp.concatenate(
            [jnp.broadcast_to(gb[half, 4 * m + n], (HALF, 128)) for n in range(4)], axis=0
        )
        return [
            jnp.sum(jnp.where(col == row + base, table, 0.0), axis=1, keepdims=True)
            for base in (0, HALF)
        ]

    def mark_keys(half, m):
        for_low, for_high = group_columns(half, m)
        hit = jnp.where(lane < 32, for_low, for_high) == lane_group
        key_mark[half, 128 * m : 128 * m + 128, :] = jnp.where(hit, 1.0, 0.0).astype(BF)
        if half is not c:
            return
        group = jnp.concatenate([for_low, for_high], axis=0)
        miss = jnp.where(group == lane_group, 0.0, -(2.0**127))
        query_mark[0, m] = jnp.where(lane < 32, miss, 0.0).astype(BF)
        query_mark[1, m] = jnp.where((lane >= 32) & (lane < 64), miss, 0.0).astype(BF)

    swap(2, GR)
    for m in range(4):
        mark_keys(c, m)
    drain(theirs[2], PR + 2)
    for m in range(4):
        mark_keys(1 - c, m)
    shard_copy(2).wait_recv()
    for i in (1, 2, 3):
        quarter_copy(i).start()
    swap(0, QR + 1)
    swap(1, QR + 2)
    drain(rb.at[0, c], QR)

    def spread_values(half):
        vals = rb[2, half]
        turned = halves(vals)
        vd[half, 0:512, :] = jnp.where(low, vals, turned)
        vd[half, 512:1024, :] = jnp.where(low, turned, vals)

    head = (y + 1 - 2 * lax.rem(y, 2)) * 4 + x
    owner_y, owner_c = lax.rem(z, 4), lax.div(z, 4)
    scale = 0.125 * math.log2(math.e)

    def scores(m, half):
        q = rb[0, c, 128 * m : 128 * m + 128, :]
        turned = halves(q)
        none = jnp.zeros_like(q)
        q_low = jnp.concatenate([jnp.where(low, q, none), jnp.where(low, turned, none)], axis=0)
        q_high = jnp.concatenate([jnp.where(low, none, turned), jnp.where(low, none, q)], axis=0)
        keys = jnp.concatenate([rb[1, half], key_mark[half]], axis=1)
        both = [
            lax.dot_general(
                jnp.concatenate([part, query_mark[n, m]], axis=1), keys, NT,
                preferred_element_type=F32,
            )
            for n, part in enumerate((q_low, q_high))
        ]
        top = jnp.maximum(
            jnp.max(both[0], axis=1, keepdims=True), jnp.max(both[1], axis=1, keepdims=True)
        )
        return both[0], both[1], top

    def weigh(s_low, s_high, top, half):
        p_low = jnp.exp2((s_low - top) * scale)
        p_high = jnp.exp2((s_high - top) * scale)
        total = jnp.sum(p_low, axis=1, keepdims=True) + jnp.sum(p_high, axis=1, keepdims=True)
        mixed = jnp.dot(p_low.astype(BF), vd[half, 0:512, :], preferred_element_type=F32)
        mixed += jnp.dot(p_high.astype(BF), vd[half, 512:1024, :], preferred_element_type=F32)
        return total, mixed

    def first_part(m):
        s_low, s_high, top = scores(m, c)
        total, mixed = weigh(s_low, s_high, top, c)
        top_v[m] = top
        sum_v[m] = total
        acc[m] = mixed

    def second_part(m):
        s_low, s_high, top = scores(m, 1 - c)
        before = top_v[m]
        top = jnp.maximum(before, top)
        total, mixed = weigh(s_low, s_high, top, 1 - c)
        factor = jnp.exp2((before - top) * scale)
        context = (acc[m] * factor + mixed) / (sum_v[m] * factor + total)
        co[128 * m : 128 * m + 128, :] = jnp.where(low, context[:128], context[128:]).astype(BF)
        for k in (2, 1, 3, 0):
            push(
                co.at[pl.ds(128 * m + HALF * turn_x(k), HALF)],
                cb.at[lax.div(x, 2), lax.div(head, 4), lax.rem(x, 2)],
                CS, CR, turn_x(k), owner_y, 2 * m + c, owner_c, None if k else spare.at[1],
            )

    spread_values(c)
    for m in range(3):
        first_part(m)
    drain(theirs[0], PR)
    drain(theirs[1], PR + 1)
    spread_values(1 - c)
    for m in range(3):
        second_part(m)
    first_part(3)
    second_part(3)

    for i in (1, 3, 2):
        if i == 2:
            for k in (1, 2, 3):
                quarter_copy(k).wait_recv()
        else:
            shard_copy(i).wait_recv()
        to_sibling(i).start()

    drain(cb, CR)
    for tc in range(2):
        for ty in range(4):
            even, odd = cb[tc, ty, 0], cb[tc, ty, 1]
            both = jnp.concatenate(
                [jnp.where(low, even, halves(odd)), jnp.where(low, halves(even), odd)], axis=0
            )
            out[:, 512 * tc + 128 * ty : 512 * tc + 128 * ty + 128] = both
    for i in range(4):
        ty = lax.rem(y + i, 4)
        remote(wo.at[c, ty], wo.at[1 - c, ty], FS + i, FT + i, sibling).wait_recv()

    for n in range(6):
        row_copy(n).wait_send()
    for i in (1, 2, 3):
        shard_copy(i).wait_send()
        quarter_copy(i).wait_send()
    remote(w_qkv, w.at[c], WS, WR, sibling).wait_send()
    for i in range(4):
        to_sibling(i).wait_send()
    drain(sb, SBS)
    for n in range(3):
        remote(mine[n], mine[n], PS + n, PR + n, sibling).wait_send()
    drain(gb.at[c], GS)
    drain(co, CS)


SCRATCH = [
    pltpu.VMEM((ROWS, D), BF),
    pltpu.VMEM((1, ROWS), jnp.int32),
    pltpu.VMEM((1, 32), jnp.int32),
    pltpu.VMEM((D,), F32),
    pltpu.VMEM((4, ROWS, D), BF),
    pltpu.VMEM((2, D, 384), BF),
    pltpu.VMEM((4, 12, HALF, 128), BF),
    pltpu.VMEM((1, 128), F32),
    pltpu.VMEM((3, 2, 512, 128), BF),
    pltpu.VMEM((2, 16, 1, 128), F32),
    pltpu.VMEM((2, 512, 128), BF),
    pltpu.VMEM((2, 4, 256, 128), BF),
    pltpu.VMEM((2, 1024, 128), BF),
    pltpu.VMEM((512, 128), BF),
    pltpu.VMEM((2, 4, 2, HALF, 128), BF),
    pltpu.VMEM((4, 256, 128), F32),
    pltpu.VMEM((4, 256, 1), F32),
    pltpu.VMEM((4, 256, 1), F32),
    pltpu.VMEM((2, HALF, 128), BF),
    pltpu.VMEM((1, 128), F32),
    pltpu.SemaphoreType.DMA((NSEM,)),
    pltpu.SemaphoreType.REGULAR,
    pltpu.SemaphoreType.REGULAR,
    pltpu.SemaphoreType.REGULAR,
]


def shards(frames, destination, plan, norm_gain, w_qkv, w_out):
    any_space = pl.BlockSpec(memory_space=pl.ANY)
    context, weights = pl.pallas_call(
        kernel,
        out_shape=(
            jax.ShapeDtypeStruct((ROWS, 1024), BF),
            jax.ShapeDtypeStruct((2, 4, 128, D), BF),
        ),
        in_specs=[any_space] * 6,
        out_specs=(pl.BlockSpec(memory_space=pltpu.VMEM), any_space),
        scratch_shapes=SCRATCH,
        compiler_params=pltpu.CompilerParams(
            collective_id=0, has_side_effects=True, vmem_limit_bytes=60 * 2**20
        ),
        name="attend",
    )(frames, destination.reshape(1, ROWS), plan, norm_gain, w_qkv, w_out)
    projected = jnp.dot(context, weights.reshape(1024, D), preferred_element_type=F32)
    return projected.astype(BF)[None]


def solution(mesh):
    in_specs = (
        P("rep", "grp", None),
        P("rep", "grp", None),
        P("rep", None),
        P(),
        P(None, "rep"),
        P("rep", None),
    )
    out_specs = P("rep", "grp", None)
    return jax.shard_map(shards, mesh=mesh, in_specs=in_specs, out_specs=out_specs, check_vma=False)
```

```python
import math

import jax
import jax.numpy as jnp
from jax import lax
from jax.experimental import pallas as pl
from jax.experimental.pallas import tpu as pltpu
from jax.sharding import PartitionSpec as P

MESH = pl.DeviceIdType.MESH
NT = (((1,), (1,)), ((), ()))
BF = jnp.bfloat16
F32 = jnp.float32
D = 1280
ROWS = 64
HALF = 32
FR, DE, PL, GA, WL, WOL = 0, 1, 2, 3, 4, 5
XS, XR = 6, 12
WS, WR = 18, 19
OS, OR = 20, 24
QS, QV = 28, 32
FS, FT = 36, 40
SBS = 44
QR = 45
GS, GR = 48, 49
PS, PR = 50, 53
CS, CR = 56, 57
NSEM = 58


def halves(block):
    return jnp.concatenate([block[:, 64:], block[:, :64]], axis=1)


def kernel(
    frames, dest, plan, gain, w_qkv, w_out, out,
    raw, dest_v, plan_v, gain_v, xb, w, wo, sb, own_g, rb, gb, key_mark, query_mark, vd, co, cb, acc, top_v,
    sum_v, spare, spare_g, sem, line_x, line_y, line_z,
):
    g = lax.axis_index("grp")
    r = lax.axis_index("rep")
    x, z = lax.div(g, 8), lax.rem(g, 8)
    y, c = lax.div(r, 2), lax.rem(r, 2)
    cls = lax.rem(z, 2)
    slot = lax.div(z, 2) * 4 + x

    def at(tx, ty, tz, tc):
        return (tx * 8 + tz, ty * 2 + tc)

    def turn_x(i):
        return lax.rem(x + i, 4)

    def along_x(i):
        return at(turn_x(i), y, z, c)

    def along_y(i):
        return at(x, lax.rem(y + i, 4), z, c)

    def along_z(i):
        return at(x, y, lax.rem(z + i, 8), c)

    sibling = at(x, y, z, 1 - c)

    def remote(src, dst, ssem, rsem, target):
        return pltpu.make_async_remote_copy(
            src_ref=src, dst_ref=dst, send_sem=sem.at[ssem], recv_sem=sem.at[rsem],
            device_id=target, device_id_type=MESH,
        )

    def local(src, dst, s):
        return pltpu.make_async_copy(src, dst, sem.at[s])

    def push(src, dst, ssem, rsem, tx, ty, tz, tc, dummy):
        if dummy is None:
            remote(src, dst, ssem, rsem, at(tx, ty, tz, tc)).start()
            return
        same = (ty == y) & (tz == z) & (tc == c)

        @pl.when(jnp.logical_not(same))
        def _():
            remote(src, dst, ssem, rsem, at(tx, ty, tz, tc)).start()

        @pl.when(same)
        def _():
            local(src, dst, rsem).start()
            local(src, dummy, ssem).start()

    def drain(ref, s):
        local(ref, ref, s).wait()

    loads = [
        local(frames.at[0], raw, FR),
        local(dest, dest_v, DE),
        local(plan, plan_v, PL),
        local(gain, gain_v, GA),
        local(w_qkv, w.at[c], WL),
        local(w_out, wo.at[c, y], WOL),
    ]
    for load in loads:
        load.start()

    barrier = pltpu.get_barrier_semaphore()
    plane = [at(turn_x(i), y, z, c) for i in (1, 2, 3)]
    plane += [at(turn_x(i), y, z, 1 - c) for i in range(4)]
    partners = [along_y(i) for i in (1, 2, 3)] + plane
    partners += [along_z(i) for i in (1, 2, 6, 7)]
    for partner in partners:
        pl.semaphore_signal(barrier, inc=1, device_id=partner, device_id_type=MESH)

    low = lax.broadcasted_iota(jnp.int32, (1, 128), 1) < 64
    loads[1].wait()
    loads[2].wait()
    row32 = lax.broadcasted_iota(jnp.int32, (32, 32), 0)
    col32 = lax.broadcasted_iota(jnp.int32, (32, 32), 1)
    plan_rows = jnp.sum(
        jnp.where(row32 == col32, plan_v[...].astype(F32), 0.0), axis=1, keepdims=True
    )
    hot = dest_v[...] == lax.broadcasted_iota(jnp.int32, (32, ROWS), 0)
    group = jnp.sum(jnp.where(hot, plan_rows, 0.0), axis=0, keepdims=True)
    own_g[...] = jnp.concatenate([group, group], axis=1)

    loads[0].wait()
    loads[3].wait()
    values = raw[...].astype(F32)
    mean = jnp.mean(values, axis=1, keepdims=True)
    centered = values - mean
    variance = jnp.mean(centered * centered, axis=1, keepdims=True)
    xb[0] = (centered * lax.rsqrt(variance + 1e-05) * gain_v[...][None, :]).astype(BF)

    pl.semaphore_wait(barrier, len(partners))

    upper, lower = pl.ds(0, HALF), pl.ds(HALF, HALF)

    def row_copy(n):
        block, to, part, source = (
            (1, 3, upper, 0), (3, 1, lower, 0), (1, 3, lower, 0), (3, 1, upper, 0),
            (2, 3, upper, 1), (2, 1, lower, 3),
        )[n]
        return remote(xb.at[source, part], xb.at[block, part], XS + n, XR + n, along_y(to))

    for n in range(4):
        row_copy(n).start()
    remote(w_qkv, w.at[c], WS, WR, sibling).start()
    for i in (2, 6):
        pl.semaphore_signal(line_z, inc=1, device_id=along_z(i), device_id_type=MESH)

    def project(i, s):
        part = jnp.dot(xb[i], w[s], preferred_element_type=F32)
        for p in range(3):
            two = part[:, 128 * p : 128 * p + 128]
            first, last = two[:HALF], two[HALF:]
            sb[i, 6 * s + 2 * p] = jnp.where(low, first, halves(last)).astype(BF)
            sb[i, 6 * s + 2 * p + 1] = jnp.where(low, halves(first), last).astype(BF)

    def scatter(i):
        tz = lax.rem(y + i, 4) + 4 * c
        for s in range(3):
            sub = 3 * y + s
            kind, block = lax.div(sub, 4), lax.rem(sub, 4)
            ty = block + 1 - 2 * lax.rem(block, 2)
            for k in (2, 1, 3, 0):
                push(
                    sb.at[i, 4 * s + turn_x(k)], rb.at[kind, cls, pl.ds(slot * HALF, HALF)],
                    SBS, QR + kind, turn_x(k), ty, tz, cls, None if k else spare.at[0],
                )

    loads[4].wait()
    project(0, c)
    pl.semaphore_wait(line_z, 2)
    for partner in plane:
        pl.semaphore_signal(line_x, inc=1, device_id=partner, device_id_type=MESH)
    for n in (0, 1):
        row_copy(n).wait_recv()
        row_copy(4 + n).start()
    pl.semaphore_wait(line_x, len(plane))
    for i in (1, 2, 3):
        pl.semaphore_signal(line_y, inc=1, device_id=along_y(i), device_id_type=MESH)
    remote(w_qkv, w.at[1 - c], WS, WR, sibling).wait_recv()
    project(0, 1 - c)
    pl.semaphore_wait(line_y, 3)

    scatter(0)
    for k in (2, 1, 3, 0):
        for i in (2, 1, 3, 0):
            push(
                own_g, gb.at[cls, slot], GS, GR, turn_x(k), lax.rem(y + i, 4), y + 4 * c, cls,
                None if k or i else spare_g,
            )
    for i, arrivals in ((1, (2,)), (3, (3,)), (2, (4, 5))):
        for n in arrivals:
            row_copy(n).wait_recv()
        project(i, 0)
        project(i, 1)
        scatter(i)
    loads[5].wait()
    opposite = lax.rem(y + 2, 4)

    def quarter(ty, tx):
        return wo.at[c, ty, pl.ds(pl.multiple_of(tx * HALF, HALF), HALF)]

    def shard_copy(i):
        ref = quarter(y, x) if i == 2 else wo.at[c, y]
        return remote(ref, ref, OS + i, OR + i, along_y(4 - i))

    def quarter_copy(i):
        ref = quarter(opposite, x)
        return remote(ref, ref, QS + i, QV + i, along_x(i))

    for i in (2, 1, 3):
        shard_copy(i).start()

    def to_sibling(i):
        ty = lax.rem(y + i, 4)
        return remote(wo.at[c, ty], wo.at[c, ty], FS + i, FT + i, sibling)

    to_sibling(0).start()

    mine = [rb.at[1, c], rb.at[2, c], gb.at[c]]
    theirs = [rb.at[1, 1 - c], rb.at[2, 1 - c], gb.at[1 - c]]

    def swap(n, s):
        drain(mine[n], s)
        remote(mine[n], mine[n], PS + n, PR + n, sibling).start()

    lane = lax.broadcasted_iota(jnp.int32, (1, 128), 1)
    lane_group = jnp.where(lane < 64, lax.rem(lax.div(lane, 4), 8), -1).astype(F32)
    row = lax.rem(lax.broadcasted_iota(jnp.int32, (128, 128), 0), HALF)
    col = lax.broadcasted_iota(jnp.int32, (128, 128), 1)

    def group_columns(half, m):
        table = jnp.concatenate(
            [jnp.broadcast_to(gb[half, 4 * m + n], (HALF, 128)) for n in range(4)], axis=0
        )
        return [
            jnp.sum(jnp.where(col == row + base, table, 0.0), axis=1, keepdims=True)
            for base in (0, HALF)
        ]

    def mark_keys(half, m):
        for_low, for_high = group_columns(half, m)
        hit = jnp.where(lane < 32, for_low, for_high) == lane_group
        key_mark[half, 128 * m : 128 * m + 128, :] = jnp.where(hit, 1.0, 0.0).astype(BF)
        if half is not c:
            return
        group = jnp.concatenate([for_low, for_high], axis=0)
        miss = jnp.where(group == lane_group, 0.0, -(2.0**127))
        query_mark[0, m] = jnp.where(lane < 32, miss, 0.0).astype(BF)
        query_mark[1, m] = jnp.where((lane >= 32) & (lane < 64), miss, 0.0).astype(BF)

    swap(2, GR)
    for m in range(4):
        mark_keys(c, m)
    drain(theirs[2], PR + 2)
    for m in range(4):
        mark_keys(1 - c, m)
    shard_copy(2).wait_recv()
    for i in (1, 2, 3):
        quarter_copy(i).start()
    swap(0, QR + 1)
    swap(1, QR + 2)
    drain(rb.at[0, c], QR)

    def spread_values(half):
        vals = rb[2, half]
        turned = halves(vals)
        vd[half, 0:512, :] = jnp.where(low, vals, turned)
        vd[half, 512:1024, :] = jnp.where(low, turned, vals)

    head = (y + 1 - 2 * lax.rem(y, 2)) * 4 + x
    owner_y, owner_c = lax.rem(z, 4), lax.div(z, 4)
    scale = 0.125 * math.log2(math.e)

    def scores(m, half):
        q = rb[0, c, 128 * m : 128 * m + 128, :]
        turned = halves(q)
        none = jnp.zeros_like(q)
        q_low = jnp.concatenate([jnp.where(low, q, none), jnp.where(low, turned, none)], axis=0)
        q_high = jnp.concatenate([jnp.where(low, none, turned), jnp.where(low, none, q)], axis=0)
        keys = jnp.concatenate([rb[1, half], key_mark[half]], axis=1)
        both = [
            lax.dot_general(
                jnp.concatenate([part, query_mark[n, m]], axis=1), keys, NT,
                preferred_element_type=F32,
            )
            for n, part in enumerate((q_low, q_high))
        ]
        top = jnp.maximum(
            jnp.max(both[0], axis=1, keepdims=True), jnp.max(both[1], axis=1, keepdims=True)
        )
        return both[0], both[1], top

    def weigh(s_low, s_high, top, half):
        p_low = jnp.exp2((s_low - top) * scale)
        p_high = jnp.exp2((s_high - top) * scale)
        total = jnp.sum(p_low, axis=1, keepdims=True) + jnp.sum(p_high, axis=1, keepdims=True)
        mixed = jnp.dot(p_low.astype(BF), vd[half, 0:512, :], preferred_element_type=F32)
        mixed += jnp.dot(p_high.astype(BF), vd[half, 512:1024, :], preferred_element_type=F32)
        return total, mixed

    def first_part(m):
        s_low, s_high, top = scores(m, c)
        total, mixed = weigh(s_low, s_high, top, c)
        top_v[m] = top
        sum_v[m] = total
        acc[m] = mixed

    def second_part(m):
        s_low, s_high, top = scores(m, 1 - c)
        before = top_v[m]
        top = jnp.maximum(before, top)
        total, mixed = weigh(s_low, s_high, top, 1 - c)
        factor = jnp.exp2((before - top) * scale)
        context = (acc[m] * factor + mixed) / (sum_v[m] * factor + total)
        co[128 * m : 128 * m + 128, :] = jnp.where(low, context[:128], context[128:]).astype(BF)
        for k in (2, 1, 3, 0):
            push(
                co.at[pl.ds(128 * m + HALF * turn_x(k), HALF)],
                cb.at[lax.div(x, 2), lax.div(head, 4), lax.rem(x, 2)],
                CS, CR, turn_x(k), owner_y, 2 * m + c, owner_c, None if k else spare.at[1],
            )

    spread_values(c)
    for m in range(3):
        first_part(m)
    drain(theirs[0], PR)
    drain(theirs[1], PR + 1)
    spread_values(1 - c)
    for m in range(3):
        second_part(m)
    first_part(3)
    second_part(3)

    for i in (1, 3, 2):
        if i == 2:
            for k in (1, 2, 3):
                quarter_copy(k).wait_recv()
        else:
            shard_copy(i).wait_recv()
        to_sibling(i).start()

    drain(cb, CR)
    pieces = []
    for tc in range(2):
        for ty in range(4):
            even, odd = cb[tc, ty, 0], cb[tc, ty, 1]
            pieces.append(
                jnp.concatenate(
                    [jnp.where(low, even, halves(odd)), jnp.where(low, halves(even), odd)], axis=0
                )
            )
    context = jnp.concatenate(pieces, axis=1)
    for i in range(4):
        ty = lax.rem(y + i, 4)
        remote(wo.at[c, ty], wo.at[1 - c, ty], FS + i, FT + i, sibling).wait_recv()
    for n in range(5):
        cols = slice(256 * n, 256 * n + 256)
        weights = wo[:, :, :, cols].reshape(1024, 256)
        out[0, :, cols] = jnp.dot(context, weights, preferred_element_type=F32).astype(BF)

    for n in range(6):
        row_copy(n).wait_send()
    for i in (1, 2, 3):
        shard_copy(i).wait_send()
        quarter_copy(i).wait_send()
    remote(w_qkv, w.at[c], WS, WR, sibling).wait_send()
    for i in range(4):
        to_sibling(i).wait_send()
    drain(sb, SBS)
    for n in range(3):
        remote(mine[n], mine[n], PS + n, PR + n, sibling).wait_send()
    drain(gb.at[c], GS)
    drain(co, CS)


SCRATCH = [
    pltpu.VMEM((ROWS, D), BF),
    pltpu.VMEM((1, ROWS), jnp.int32),
    pltpu.VMEM((1, 32), jnp.int32),
    pltpu.VMEM((D,), F32),
    pltpu.VMEM((4, ROWS, D), BF),
    pltpu.VMEM((2, D, 384), BF),
    pltpu.VMEM((2, 4, 128, D), BF),
    pltpu.VMEM((4, 12, HALF, 128), BF),
    pltpu.VMEM((1, 128), F32),
    pltpu.VMEM((3, 2, 512, 128), BF),
    pltpu.VMEM((2, 16, 1, 128), F32),
    pltpu.VMEM((2, 512, 128), BF),
    pltpu.VMEM((2, 4, 256, 128), BF),
    pltpu.VMEM((2, 1024, 128), BF),
    pltpu.VMEM((512, 128), BF),
    pltpu.VMEM((2, 4, 2, HALF, 128), BF),
    pltpu.VMEM((4, 256, 128), F32),
    pltpu.VMEM((4, 256, 1), F32),
    pltpu.VMEM((4, 256, 1), F32),
    pltpu.VMEM((2, HALF, 128), BF),
    pltpu.VMEM((1, 128), F32),
    pltpu.SemaphoreType.DMA((NSEM,)),
    pltpu.SemaphoreType.REGULAR,
    pltpu.SemaphoreType.REGULAR,
    pltpu.SemaphoreType.REGULAR,
]


def shards(frames, destination, plan, norm_gain, w_qkv, w_out):
    any_space = pl.BlockSpec(memory_space=pl.ANY)
    return pl.pallas_call(
        kernel,
        out_shape=jax.ShapeDtypeStruct((1, ROWS, D), BF),
        in_specs=[any_space] * 6,
        out_specs=pl.BlockSpec(memory_space=pltpu.VMEM),
        scratch_shapes=SCRATCH,
        compiler_params=pltpu.CompilerParams(
            collective_id=0, has_side_effects=True, vmem_limit_bytes=60 * 2**20
        ),
        name="attend",
    )(frames, destination.reshape(1, ROWS), plan, norm_gain, w_qkv, w_out)


def solution(mesh):
    in_specs = (
        P("rep", "grp", None),
        P("rep", "grp", None),
        P("rep", None),
        P(),
        P(None, "rep"),
        P("rep", None),
    )
    out_specs = P("rep", "grp", None)
    return jax.shard_map(shards, mesh=mesh, in_specs=in_specs, out_specs=out_specs, check_vma=False)
```

```python
import math

import jax
import jax.numpy as jnp
from jax import lax
from jax.experimental import pallas as pl
from jax.experimental.pallas import tpu as pltpu
from jax.sharding import PartitionSpec as P

MESH = pl.DeviceIdType.MESH
NT = (((1,), (1,)), ((), ()))
BF = jnp.bfloat16
F32 = jnp.float32
D = 1280
ROWS = 64
HALF = 32
FR, DE, PL, GA, WL, WOL = 0, 1, 2, 3, 4, 5
XS, XR = 6, 12
WS, WR = 18, 19
OS, OR = 20, 24
QS, QV = 28, 32
FS, FT = 36, 40
SBS = 44
QR = 45
GS, GR = 48, 49
PS, PR = 50, 53
CS, CR = 56, 57
RS = 58
NSEM = 63


def halves(block):
    return jnp.concatenate([block[:, 64:], block[:, :64]], axis=1)


def kernel(
    frames, dest, plan, gain, w_qkv, w_out, out,
    raw, dest_v, plan_v, gain_v, xb, w, wo, sb, own_g, rb, gb, key_mark, query_mark, vd, co, cb, acc, top_v,
    sum_v, spare, spare_g, result, sem, line_x, line_y, line_z,
):
    g = lax.axis_index("grp")
    r = lax.axis_index("rep")
    x, z = lax.div(g, 8), lax.rem(g, 8)
    y, c = lax.div(r, 2), lax.rem(r, 2)
    cls = lax.rem(z, 2)
    slot = lax.div(z, 2) * 4 + x

    def at(tx, ty, tz, tc):
        return (tx * 8 + tz, ty * 2 + tc)

    def turn_x(i):
        return lax.rem(x + i, 4)

    def along_x(i):
        return at(turn_x(i), y, z, c)

    def along_y(i):
        return at(x, lax.rem(y + i, 4), z, c)

    def along_z(i):
        return at(x, y, lax.rem(z + i, 8), c)

    sibling = at(x, y, z, 1 - c)

    def remote(src, dst, ssem, rsem, target):
        return pltpu.make_async_remote_copy(
            src_ref=src, dst_ref=dst, send_sem=sem.at[ssem], recv_sem=sem.at[rsem],
            device_id=target, device_id_type=MESH,
        )

    def local(src, dst, s):
        return pltpu.make_async_copy(src, dst, sem.at[s])

    def push(src, dst, ssem, rsem, tx, ty, tz, tc, dummy):
        if dummy is None:
            remote(src, dst, ssem, rsem, at(tx, ty, tz, tc)).start()
            return
        same = (ty == y) & (tz == z) & (tc == c)

        @pl.when(jnp.logical_not(same))
        def _():
            remote(src, dst, ssem, rsem, at(tx, ty, tz, tc)).start()

        @pl.when(same)
        def _():
            local(src, dst, rsem).start()
            local(src, dummy, ssem).start()

    def drain(ref, s):
        local(ref, ref, s).wait()

    loads = [
        local(frames.at[0], raw, FR),
        local(dest, dest_v, DE),
        local(plan, plan_v, PL),
        local(gain, gain_v, GA),
        local(w_qkv, w.at[c], WL),
        local(w_out, wo.at[c, y], WOL),
    ]
    for load in loads:
        load.start()

    barrier = pltpu.get_barrier_semaphore()
    plane = [at(turn_x(i), y, z, c) for i in (1, 2, 3)]
    plane += [at(turn_x(i), y, z, 1 - c) for i in range(4)]
    partners = [along_y(i) for i in (1, 2, 3)] + plane
    partners += [along_z(i) for i in (1, 2, 6, 7)]
    for partner in partners:
        pl.semaphore_signal(barrier, inc=1, device_id=partner, device_id_type=MESH)

    low = lax.broadcasted_iota(jnp.int32, (1, 128), 1) < 64
    loads[0].wait()
    loads[3].wait()
    values = raw[...].astype(F32)
    mean = jnp.mean(values, axis=1, keepdims=True)
    centered = values - mean
    variance = jnp.mean(centered * centered, axis=1, keepdims=True)
    xb[0] = (centered * lax.rsqrt(variance + 1e-05) * gain_v[...][None, :]).astype(BF)

    pl.semaphore_wait(barrier, len(partners))

    upper, lower = pl.ds(0, HALF), pl.ds(HALF, HALF)

    def row_copy(n):
        block, to, part, source = (
            (1, 3, upper, 0), (3, 1, lower, 0), (1, 3, lower, 0), (3, 1, upper, 0),
            (2, 3, upper, 1), (2, 1, lower, 3),
        )[n]
        return remote(xb.at[source, part], xb.at[block, part], XS + n, XR + n, along_y(to))

    for i in (2, 6):
        pl.semaphore_signal(line_z, inc=1, device_id=along_z(i), device_id_type=MESH)
    for n in range(4):
        row_copy(n).start()
    remote(w_qkv, w.at[c], WS, WR, sibling).start()

    loads[1].wait()
    loads[2].wait()
    row32 = lax.broadcasted_iota(jnp.int32, (32, 32), 0)
    col32 = lax.broadcasted_iota(jnp.int32, (32, 32), 1)
    plan_rows = jnp.sum(
        jnp.where(row32 == col32, plan_v[...].astype(F32), 0.0), axis=1, keepdims=True
    )
    hot = dest_v[...] == lax.broadcasted_iota(jnp.int32, (32, ROWS), 0)
    group = jnp.sum(jnp.where(hot, plan_rows, 0.0), axis=0, keepdims=True)
    own_g[...] = jnp.concatenate([group, group], axis=1)

    def project(i, s):
        part = jnp.dot(xb[i], w[s], preferred_element_type=F32)
        for p in range(3):
            two = part[:, 128 * p : 128 * p + 128]
            first, last = two[:HALF], two[HALF:]
            sb[i, 6 * s + 2 * p] = jnp.where(low, first, halves(last)).astype(BF)
            sb[i, 6 * s + 2 * p + 1] = jnp.where(low, halves(first), last).astype(BF)

    def scatter(i, blocks):
        tz = lax.rem(y + i, 4) + 4 * c
        for s in blocks:
            sub = 3 * y + s
            kind, block = lax.div(sub, 4), lax.rem(sub, 4)
            ty = block + 1 - 2 * lax.rem(block, 2)
            for k in (2, 1, 3, 0):
                push(
                    sb.at[i, 4 * s + turn_x(k)], rb.at[kind, cls, pl.ds(slot * HALF, HALF)],
                    SBS, QR + kind, turn_x(k), ty, tz, cls, None if k else spare.at[0],
                )

    loads[4].wait()
    project(0, c)
    pl.semaphore_wait(line_z, 2)
    for partner in plane:
        pl.semaphore_signal(line_x, inc=1, device_id=partner, device_id_type=MESH)
    pl.semaphore_wait(line_x, len(plane))
    for i in (1, 2, 3):
        pl.semaphore_signal(line_y, inc=1, device_id=along_y(i), device_id_type=MESH)
    for n in (0, 1):
        row_copy(n).wait_recv()
        row_copy(4 + n).start()
    remote(w_qkv, w.at[1 - c], WS, WR, sibling).wait_recv()
    project(0, 1 - c)
    scatter(0, (1,))
    pl.semaphore_wait(line_y, 3)
    scatter(0, (0, 2))
    for k in (2, 1, 3, 0):
        for i in (2, 1, 3, 0):
            push(
                own_g, gb.at[cls, slot], GS, GR, turn_x(k), lax.rem(y + i, 4), y + 4 * c, cls,
                None if k or i else spare_g,
            )
    for i, arrivals in ((1, (2,)), (3, (3,)), (2, (4, 5))):
        for n in arrivals:
            row_copy(n).wait_recv()
        project(i, 0)
        project(i, 1)
        scatter(i, (0, 2, 1))
    loads[5].wait()
    opposite = lax.rem(y + 2, 4)

    def quarter(ty, tx):
        return wo.at[c, ty, pl.ds(pl.multiple_of(tx * HALF, HALF), HALF)]

    def shard_copy(i):
        ref = quarter(y, x) if i == 2 else wo.at[c, y]
        return remote(ref, ref, OS + i, OR + i, along_y(4 - i))

    def quarter_copy(i):
        ref = quarter(opposite, x)
        return remote(ref, ref, QS + i, QV + i, along_x(i))

    for i in (2, 1, 3):
        shard_copy(i).start()

    def to_sibling(i):
        ty = lax.rem(y + i, 4)
        return remote(wo.at[c, ty], wo.at[c, ty], FS + i, FT + i, sibling)

    to_sibling(0).start()

    mine = [rb.at[1, c], rb.at[2, c], gb.at[c]]
    theirs = [rb.at[1, 1 - c], rb.at[2, 1 - c], gb.at[1 - c]]

    def swap(n, s):
        drain(mine[n], s)
        remote(mine[n], mine[n], PS + n, PR + n, sibling).start()

    lane = lax.broadcasted_iota(jnp.int32, (1, 128), 1)
    lane_group = jnp.where(lane < 64, lax.rem(lax.div(lane, 4), 8), -1).astype(F32)
    row = lax.rem(lax.broadcasted_iota(jnp.int32, (128, 128), 0), HALF)
    col = lax.broadcasted_iota(jnp.int32, (128, 128), 1)

    def group_columns(half, m):
        table = jnp.concatenate(
            [jnp.broadcast_to(gb[half, 4 * m + n], (HALF, 128)) for n in range(4)], axis=0
        )
        return [
            jnp.sum(jnp.where(col == row + base, table, 0.0), axis=1, keepdims=True)
            for base in (0, HALF)
        ]

    def mark_keys(half, m):
        for_low, for_high = group_columns(half, m)
        hit = jnp.where(lane < 32, for_low, for_high) == lane_group
        key_mark[half, 128 * m : 128 * m + 128, :] = jnp.where(hit, 1.0, 0.0).astype(BF)
        if half is not c:
            return
        group = jnp.concatenate([for_low, for_high], axis=0)
        miss = jnp.where(group == lane_group, 0.0, -(2.0**127))
        query_mark[0, m] = jnp.where(lane < 32, miss, 0.0).astype(BF)
        query_mark[1, m] = jnp.where((lane >= 32) & (lane < 64), miss, 0.0).astype(BF)

    swap(2, GR)
    for m in range(4):
        mark_keys(c, m)
    drain(theirs[2], PR + 2)
    for m in range(4):
        mark_keys(1 - c, m)
    swap(0, QR + 1)
    swap(1, QR + 2)
    drain(rb.at[0, c], QR)
    shard_copy(2).wait_recv()
    for i in (1, 2, 3):
        quarter_copy(i).start()

    def spread_values(half):
        vals = rb[2, half]
        turned = halves(vals)
        vd[half, 0:512, :] = jnp.where(low, vals, turned)
        vd[half, 512:1024, :] = jnp.where(low, turned, vals)

    head = (y + 1 - 2 * lax.rem(y, 2)) * 4 + x
    owner_y, owner_c = lax.rem(z, 4), lax.div(z, 4)
    scale = 0.125 * math.log2(math.e)

    def scores(m, half):
        q = rb[0, c, 128 * m : 128 * m + 128, :]
        turned = halves(q)
        none = jnp.zeros_like(q)
        q_low = jnp.concatenate([jnp.where(low, q, none), jnp.where(low, turned, none)], axis=0)
        q_high = jnp.concatenate([jnp.where(low, none, turned), jnp.where(low, none, q)], axis=0)
        keys = jnp.concatenate([rb[1, half], key_mark[half]], axis=1)
        both = [
            lax.dot_general(
                jnp.concatenate([part, query_mark[n, m]], axis=1), keys, NT,
                preferred_element_type=F32,
            )
            for n, part in enumerate((q_low, q_high))
        ]
        top = jnp.maximum(
            jnp.max(both[0], axis=1, keepdims=True), jnp.max(both[1], axis=1, keepdims=True)
        )
        return both[0], both[1], top

    def weigh(s_low, s_high, top, half):
        p_low = jnp.exp2((s_low - top) * scale)
        p_high = jnp.exp2((s_high - top) * scale)
        total = jnp.sum(p_low, axis=1, keepdims=True) + jnp.sum(p_high, axis=1, keepdims=True)
        mixed = jnp.dot(p_low.astype(BF), vd[half, 0:512, :], preferred_element_type=F32)
        mixed += jnp.dot(p_high.astype(BF), vd[half, 512:1024, :], preferred_element_type=F32)
        return total, mixed

    def first_part(m):
        s_low, s_high, top = scores(m, c)
        total, mixed = weigh(s_low, s_high, top, c)
        top_v[m] = top
        sum_v[m] = total
        acc[m] = mixed

    def second_part(m):
        s_low, s_high, top = scores(m, 1 - c)
        before = top_v[m]
        top = jnp.maximum(before, top)
        total, mixed = weigh(s_low, s_high, top, 1 - c)
        factor = jnp.exp2((before - top) * scale)
        context = (acc[m] * factor + mixed) / (sum_v[m] * factor + total)
        co[128 * m : 128 * m + 128, :] = jnp.where(low, context[:128], context[128:]).astype(BF)
        for k in (2, 1, 3, 0):
            push(
                co.at[pl.ds(128 * m + HALF * turn_x(k), HALF)],
                cb.at[lax.div(x, 2), lax.div(head, 4), lax.rem(x, 2)],
                CS, CR, turn_x(k), owner_y, 2 * m + c, owner_c, None if k else spare.at[1],
            )

    spread_values(c)
    for m in range(3):
        first_part(m)
    drain(theirs[0], PR)
    drain(theirs[1], PR + 1)
    spread_values(1 - c)
    for m in range(3):
        second_part(m)
    first_part(3)
    second_part(3)

    for i in (1, 3, 2):
        if i == 2:
            for k in (1, 2, 3):
                quarter_copy(k).wait_recv()
        else:
            shard_copy(i).wait_recv()
        to_sibling(i).start()

    for n in range(6):
        row_copy(n).wait_send()
    for i in (1, 2, 3):
        shard_copy(i).wait_send()
        quarter_copy(i).wait_send()
    remote(w_qkv, w.at[c], WS, WR, sibling).wait_send()
    drain(sb, SBS)
    for n in range(3):
        remote(mine[n], mine[n], PS + n, PR + n, sibling).wait_send()
    drain(gb.at[c], GS)

    drain(cb, CR)
    pieces = []
    for tc in range(2):
        for ty in range(4):
            even, odd = cb[tc, ty, 0], cb[tc, ty, 1]
            pieces.append(
                jnp.concatenate(
                    [jnp.where(low, even, halves(odd)), jnp.where(low, halves(even), odd)], axis=0
                )
            )
    context = jnp.concatenate(pieces, axis=1)
    for i in range(4):
        ty = lax.rem(y + i, 4)
        remote(wo.at[c, ty], wo.at[1 - c, ty], FS + i, FT + i, sibling).wait_recv()
    leaving = []
    for n in range(5):
        cols = slice(256 * n, 256 * n + 256)
        weights = wo[:, :, :, cols].reshape(1024, 256)
        result[:, cols] = jnp.dot(context, weights, preferred_element_type=F32).astype(BF)
        piece = local(result.at[:, cols], out.at[0, :, cols], RS + n)
        piece.start()
        leaving.append(piece)

    for i in range(4):
        to_sibling(i).wait_send()
    drain(co, CS)
    for piece in leaving:
        piece.wait()


SCRATCH = [
    pltpu.VMEM((ROWS, D), BF),
    pltpu.VMEM((1, ROWS), jnp.int32),
    pltpu.VMEM((1, 32), jnp.int32),
    pltpu.VMEM((D,), F32),
    pltpu.VMEM((4, ROWS, D), BF),
    pltpu.VMEM((2, D, 384), BF),
    pltpu.VMEM((2, 4, 128, D), BF),
    pltpu.VMEM((4, 12, HALF, 128), BF),
    pltpu.VMEM((1, 128), F32),
    pltpu.VMEM((3, 2, 512, 128), BF),
    pltpu.VMEM((2, 16, 1, 128), F32),
    pltpu.VMEM((2, 512, 128), BF),
    pltpu.VMEM((2, 4, 256, 128), BF),
    pltpu.VMEM((2, 1024, 128), BF),
    pltpu.VMEM((512, 128), BF),
    pltpu.VMEM((2, 4, 2, HALF, 128), BF),
    pltpu.VMEM((4, 256, 128), F32),
    pltpu.VMEM((4, 256, 1), F32),
    pltpu.VMEM((4, 256, 1), F32),
    pltpu.VMEM((2, HALF, 128), BF),
    pltpu.VMEM((1, 128), F32),
    pltpu.VMEM((ROWS, D), BF),
    pltpu.SemaphoreType.DMA((NSEM,)),
    pltpu.SemaphoreType.REGULAR,
    pltpu.SemaphoreType.REGULAR,
    pltpu.SemaphoreType.REGULAR,
]


def shards(frames, destination, plan, norm_gain, w_qkv, w_out):
    any_space = pl.BlockSpec(memory_space=pl.ANY)
    return pl.pallas_call(
        kernel,
        out_shape=jax.ShapeDtypeStruct((1, ROWS, D), BF),
        in_specs=[any_space] * 6,
        out_specs=any_space,
        scratch_shapes=SCRATCH,
        compiler_params=pltpu.CompilerParams(
            collective_id=0, has_side_effects=True, vmem_limit_bytes=60 * 2**20
        ),
        name="attend",
    )(frames, destination.reshape(1, ROWS), plan, norm_gain, w_qkv, w_out)


def solution(mesh):
    in_specs = (
        P("rep", "grp", None),
        P("rep", "grp", None),
        P("rep", None),
        P(),
        P(None, "rep"),
        P("rep", None),
    )
    out_specs = P("rep", "grp", None)
    return jax.shard_map(shards, mesh=mesh, in_specs=in_specs, out_specs=out_specs, check_vma=False)
```

```python
import math

import jax
import jax.numpy as jnp
from jax import lax
from jax.experimental import pallas as pl
from jax.experimental.pallas import tpu as pltpu
from jax.sharding import PartitionSpec as P

MESH = pl.DeviceIdType.MESH
NT = (((1,), (1,)), ((), ()))
BF = jnp.bfloat16
F32 = jnp.float32
D = 1280
ROWS = 64
HALF = 32
FR, DE, PL, GA, WL, WOL = 0, 1, 2, 3, 4, 5
XS, XR = 6, 12
WS, WR = 18, 19
OS, OR = 20, 24
QS, QV = 28, 32
FS, FT = 36, 40
SBS = 44
QR = 45
GS, GR = 48, 49
PS, PR = 50, 53
CS, CR = 56, 57
RS = 59
NSEM = 64


def halves(block):
    return jnp.concatenate([block[:, 64:], block[:, :64]], axis=1)


def kernel(
    frames, dest, plan, gain, w_qkv, w_out, out,
    raw, dest_v, plan_v, gain_v, xb, w, wo, sb, own_g, rb, gb, key_mark, query_mark, vd, co, cb, acc, top_v,
    sum_v, spare, spare_g, near, result, sem, line_x, line_y, line_z,
):
    g = lax.axis_index("grp")
    r = lax.axis_index("rep")
    x, z = lax.div(g, 8), lax.rem(g, 8)
    y, c = lax.div(r, 2), lax.rem(r, 2)
    cls = lax.rem(z, 2)
    slot = lax.div(z, 2) * 4 + x

    def at(tx, ty, tz, tc):
        return (tx * 8 + tz, ty * 2 + tc)

    def turn_x(i):
        return lax.rem(x + i, 4)

    def along_x(i):
        return at(turn_x(i), y, z, c)

    def along_y(i):
        return at(x, lax.rem(y + i, 4), z, c)

    def along_z(i):
        return at(x, y, lax.rem(z + i, 8), c)

    sibling = at(x, y, z, 1 - c)

    def remote(src, dst, ssem, rsem, target):
        return pltpu.make_async_remote_copy(
            src_ref=src, dst_ref=dst, send_sem=sem.at[ssem], recv_sem=sem.at[rsem],
            device_id=target, device_id_type=MESH,
        )

    def local(src, dst, s):
        return pltpu.make_async_copy(src, dst, sem.at[s])

    def push(src, dst, ssem, rsem, tx, ty, tz, tc, dummy):
        if dummy is None:
            remote(src, dst, ssem, rsem, at(tx, ty, tz, tc)).start()
            return
        same = (ty == y) & (tz == z) & (tc == c)

        @pl.when(jnp.logical_not(same))
        def _():
            remote(src, dst, ssem, rsem, at(tx, ty, tz, tc)).start()

        @pl.when(same)
        def _():
            local(src, dst, rsem).start()
            local(src, dummy, ssem).start()

    def drain(ref, s):
        local(ref, ref, s).wait()

    loads = [
        local(frames.at[0], raw, FR),
        local(dest, dest_v, DE),
        local(plan, plan_v, PL),
        local(gain, gain_v, GA),
        local(w_qkv, w.at[c], WL),
        local(w_out, wo.at[c, y], WOL),
    ]
    for load in loads:
        load.start()

    barrier = pltpu.get_barrier_semaphore()
    plane = [at(turn_x(i), y, z, c) for i in (1, 2, 3)]
    plane += [at(turn_x(i), y, z, 1 - c) for i in range(4)]
    partners = [along_y(i) for i in (1, 2, 3)] + plane
    partners += [along_z(i) for i in (1, 2, 6, 7)]
    for partner in partners:
        pl.semaphore_signal(barrier, inc=1, device_id=partner, device_id_type=MESH)

    low = lax.broadcasted_iota(jnp.int32, (1, 128), 1) < 64
    loads[0].wait()
    loads[3].wait()
    values = raw[...].astype(F32)
    mean = jnp.mean(values, axis=1, keepdims=True)
    centered = values - mean
    variance = jnp.mean(centered * centered, axis=1, keepdims=True)
    xb[0] = (centered * lax.rsqrt(variance + 1e-05) * gain_v[...][None, :]).astype(BF)

    pl.semaphore_wait(barrier, len(partners))

    upper, lower = pl.ds(0, HALF), pl.ds(HALF, HALF)

    def row_copy(n):
        block, to, part, source = (
            (1, 3, upper, 0), (3, 1, lower, 0), (1, 3, lower, 0), (3, 1, upper, 0),
            (2, 3, upper, 1), (2, 1, lower, 3),
        )[n]
        return remote(xb.at[source, part], xb.at[block, part], XS + n, XR + n, along_y(to))

    for i in (2, 6):
        pl.semaphore_signal(line_z, inc=1, device_id=along_z(i), device_id_type=MESH)
    for n in range(4):
        row_copy(n).start()
    remote(w_qkv, w.at[c], WS, WR, sibling).start()

    loads[1].wait()
    loads[2].wait()
    row32 = lax.broadcasted_iota(jnp.int32, (32, 32), 0)
    col32 = lax.broadcasted_iota(jnp.int32, (32, 32), 1)
    plan_rows = jnp.sum(
        jnp.where(row32 == col32, plan_v[...].astype(F32), 0.0), axis=1, keepdims=True
    )
    hot = dest_v[...] == lax.broadcasted_iota(jnp.int32, (32, ROWS), 0)
    group = jnp.sum(jnp.where(hot, plan_rows, 0.0), axis=0, keepdims=True)
    own_g[...] = jnp.concatenate([group, group], axis=1)

    def project(i, s):
        part = jnp.dot(xb[i], w[s], preferred_element_type=F32)
        for p in range(3):
            two = part[:, 128 * p : 128 * p + 128]
            first, last = two[:HALF], two[HALF:]
            sb[i, 6 * s + 2 * p] = jnp.where(low, first, halves(last)).astype(BF)
            sb[i, 6 * s + 2 * p + 1] = jnp.where(low, halves(first), last).astype(BF)

    def scatter(i, blocks):
        tz = lax.rem(y + i, 4) + 4 * (1 - c)
        for s in blocks:
            sub = 3 * y + s
            kind, block = lax.div(sub, 4), lax.rem(sub, 4)
            ty = block + 1 - 2 * lax.rem(block, 2)
            for k in (2, 1, 3, 0):
                push(
                    sb.at[i, 4 * s + turn_x(k)], rb.at[kind, cls, pl.ds(slot * HALF, HALF)],
                    SBS, QR + kind, turn_x(k), ty, tz, cls, None if k else spare.at[0],
                )

    loads[4].wait()
    project(0, c)
    pl.semaphore_wait(line_z, 2)
    for partner in plane:
        pl.semaphore_signal(line_x, inc=1, device_id=partner, device_id_type=MESH)
    pl.semaphore_wait(line_x, len(plane))
    for i in (1, 2, 3):
        pl.semaphore_signal(line_y, inc=1, device_id=along_y(i), device_id_type=MESH)
    for n in (0, 1):
        row_copy(n).wait_recv()
        row_copy(4 + n).start()
    remote(w_qkv, w.at[1 - c], WS, WR, sibling).wait_recv()
    project(0, 1 - c)
    scatter(0, (1,))
    pl.semaphore_wait(line_y, 3)
    scatter(0, (0, 2))
    for k in (2, 1, 3, 0):
        for i in (2, 1, 3, 0):
            push(
                own_g, gb.at[cls, slot], GS, GR, turn_x(k), lax.rem(y + i, 4), y + 4 * (1 - c), cls,
                None if k or i else spare_g,
            )
    for i, arrivals in ((1, (2,)), (3, (3,)), (2, (4, 5))):
        for n in arrivals:
            row_copy(n).wait_recv()
        project(i, 0)
        project(i, 1)
        scatter(i, (0, 2, 1))
    loads[5].wait()
    opposite = lax.rem(y + 2, 4)

    def quarter(ty, tx):
        return wo.at[c, ty, pl.ds(pl.multiple_of(tx * HALF, HALF), HALF)]

    def shard_copy(i):
        ref = quarter(y, x) if i == 2 else wo.at[c, y]
        return remote(ref, ref, OS + i, OR + i, along_y(4 - i))

    def quarter_copy(i):
        ref = quarter(opposite, x)
        return remote(ref, ref, QS + i, QV + i, along_x(i))

    for i in (2, 1, 3):
        shard_copy(i).start()

    def to_sibling(i):
        ty = lax.rem(y + i, 4)
        return remote(wo.at[c, ty], wo.at[c, ty], FS + i, FT + i, sibling)

    to_sibling(0).start()

    mine = [rb.at[1, c], rb.at[2, c], gb.at[c]]
    theirs = [rb.at[1, 1 - c], rb.at[2, 1 - c], gb.at[1 - c]]

    def swap(n, s):
        drain(mine[n], s)
        remote(mine[n], mine[n], PS + n, PR + n, sibling).start()

    lane = lax.broadcasted_iota(jnp.int32, (1, 128), 1)
    lane_group = jnp.where(lane < 64, lax.rem(lax.div(lane, 4), 8), -1).astype(F32)
    row = lax.rem(lax.broadcasted_iota(jnp.int32, (128, 128), 0), HALF)
    col = lax.broadcasted_iota(jnp.int32, (128, 128), 1)

    def group_columns(half, m):
        table = jnp.concatenate(
            [jnp.broadcast_to(gb[half, 4 * m + n], (HALF, 128)) for n in range(4)], axis=0
        )
        return [
            jnp.sum(jnp.where(col == row + base, table, 0.0), axis=1, keepdims=True)
            for base in (0, HALF)
        ]

    def mark_keys(half, m):
        for_low, for_high = group_columns(half, m)
        hit = jnp.where(lane < 32, for_low, for_high) == lane_group
        key_mark[half, 128 * m : 128 * m + 128, :] = jnp.where(hit, 1.0, 0.0).astype(BF)
        if half is not c:
            return
        group = jnp.concatenate([for_low, for_high], axis=0)
        miss = jnp.where(group == lane_group, 0.0, -(2.0**127))
        query_mark[0, m] = jnp.where(lane < 32, miss, 0.0).astype(BF)
        query_mark[1, m] = jnp.where((lane >= 32) & (lane < 64), miss, 0.0).astype(BF)

    swap(2, GR)
    for m in range(4):
        mark_keys(c, m)
    drain(theirs[2], PR + 2)
    for m in range(4):
        mark_keys(1 - c, m)
    swap(0, QR + 1)
    swap(1, QR + 2)
    drain(rb.at[0, c], QR)
    shard_copy(2).wait_recv()
    for i in (1, 2, 3):
        quarter_copy(i).start()

    def spread_values(half):
        vals = rb[2, half]
        turned = halves(vals)
        vd[half, 0:512, :] = jnp.where(low, vals, turned)
        vd[half, 512:1024, :] = jnp.where(low, turned, vals)

    owner_y, owner_c = lax.rem(z, 4), 1 - lax.div(z, 4)
    away = lax.rem(y + 4 - owner_y, 4)
    place = away + lax.div(away, 2) * (5 - 2 * away)
    scale = 0.125 * math.log2(math.e)

    def scores(m, half):
        q = rb[0, c, 128 * m : 128 * m + 128, :]
        turned = halves(q)
        none = jnp.zeros_like(q)
        q_low = jnp.concatenate([jnp.where(low, q, none), jnp.where(low, turned, none)], axis=0)
        q_high = jnp.concatenate([jnp.where(low, none, turned), jnp.where(low, none, q)], axis=0)
        keys = jnp.concatenate([rb[1, half], key_mark[half]], axis=1)
        both = [
            lax.dot_general(
                jnp.concatenate([part, query_mark[n, m]], axis=1), keys, NT,
                preferred_element_type=F32,
            )
            for n, part in enumerate((q_low, q_high))
        ]
        top = jnp.maximum(
            jnp.max(both[0], axis=1, keepdims=True), jnp.max(both[1], axis=1, keepdims=True)
        )
        return both[0], both[1], top

    def weigh(s_low, s_high, top, half):
        p_low = jnp.exp2((s_low - top) * scale)
        p_high = jnp.exp2((s_high - top) * scale)
        total = jnp.sum(p_low, axis=1, keepdims=True) + jnp.sum(p_high, axis=1, keepdims=True)
        mixed = jnp.dot(p_low.astype(BF), vd[half, 0:512, :], preferred_element_type=F32)
        mixed += jnp.dot(p_high.astype(BF), vd[half, 512:1024, :], preferred_element_type=F32)
        return total, mixed

    def first_part(m):
        s_low, s_high, top = scores(m, c)
        total, mixed = weigh(s_low, s_high, top, c)
        top_v[m] = top
        sum_v[m] = total
        acc[m] = mixed

    def second_part(m):
        s_low, s_high, top = scores(m, 1 - c)
        before = top_v[m]
        top = jnp.maximum(before, top)
        total, mixed = weigh(s_low, s_high, top, 1 - c)
        factor = jnp.exp2((before - top) * scale)
        context = (acc[m] * factor + mixed) / (sum_v[m] * factor + total)
        co[128 * m : 128 * m + 128, :] = jnp.where(low, context[:128], context[128:]).astype(BF)
        for k in (2, 1, 3, 0):
            push(
                co.at[pl.ds(128 * m + HALF * turn_x(k), HALF)],
                cb.at[place, lax.div(x, 2), lax.rem(x, 2)],
                CS, CR + lax.div(place, 3), turn_x(k), owner_y, 2 * m + c, owner_c, None if k else spare.at[1],
            )

    spread_values(c)
    for m in range(3):
        first_part(m)
    drain(theirs[0], PR)
    drain(theirs[1], PR + 1)
    spread_values(1 - c)
    for m in range(3):
        second_part(m)
    first_part(3)
    second_part(3)

    for i in (1, 3, 2):
        if i == 2:
            for k in (1, 2, 3):
                quarter_copy(k).wait_recv()
        else:
            shard_copy(i).wait_recv()
        to_sibling(i).start()

    for n in range(6):
        row_copy(n).wait_send()
    for i in (1, 2, 3):
        shard_copy(i).wait_send()
        quarter_copy(i).wait_send()
    remote(w_qkv, w.at[c], WS, WR, sibling).wait_send()
    drain(sb, SBS)
    for n in range(3):
        remote(mine[n], mine[n], PS + n, PR + n, sibling).wait_send()
    drain(gb.at[c], GS)

    def gathered(p):
        both = []
        for tc in range(2):
            even, odd = cb[p, tc, 0], cb[p, tc, 1]
            both.append(
                jnp.concatenate(
                    [jnp.where(low, even, halves(odd)), jnp.where(low, halves(even), odd)], axis=0
                )
            )
        return jnp.concatenate(both, axis=1)

    def product(p, context, cols):
        ty = lax.rem(y + (0, 1, 3, 2)[p], 4)
        ty = ty + 1 - 2 * lax.rem(ty, 2)
        weights = wo[:, ty, :, cols].reshape(256, 256)
        return jnp.dot(context, weights, preferred_element_type=F32)

    drain(cb.at[pl.ds(0, 3)], CR)
    for i in range(4):
        ty = lax.rem(y + i, 4)
        remote(wo.at[c, ty], wo.at[1 - c, ty], FS + i, FT + i, sibling).wait_recv()
    contexts = [gathered(p) for p in range(3)]
    spans = [slice(256 * n, 256 * n + 256) for n in range(5)]
    for cols in spans:
        near[:, cols] = sum(product(p, contexts[p], cols) for p in range(3))
    drain(cb.at[3], CR + 1)
    context = gathered(3)
    leaving = []
    for n, cols in enumerate(spans):
        result[:, cols] = (near[:, cols] + product(3, context, cols)).astype(BF)
        piece = local(result.at[:, cols], out.at[0, :, cols], RS + n)
        piece.start()
        leaving.append(piece)

    for i in range(4):
        to_sibling(i).wait_send()
    drain(co, CS)
    for piece in leaving:
        piece.wait()


SCRATCH = [
    pltpu.VMEM((ROWS, D), BF),
    pltpu.VMEM((1, ROWS), jnp.int32),
    pltpu.VMEM((1, 32), jnp.int32),
    pltpu.VMEM((D,), F32),
    pltpu.VMEM((4, ROWS, D), BF),
    pltpu.VMEM((2, D, 384), BF),
    pltpu.VMEM((2, 4, 128, D), BF),
    pltpu.VMEM((4, 12, HALF, 128), BF),
    pltpu.VMEM((1, 128), F32),
    pltpu.VMEM((3, 2, 512, 128), BF),
    pltpu.VMEM((2, 16, 1, 128), F32),
    pltpu.VMEM((2, 512, 128), BF),
    pltpu.VMEM((2, 4, 256, 128), BF),
    pltpu.VMEM((2, 1024, 128), BF),
    pltpu.VMEM((512, 128), BF),
    pltpu.VMEM((4, 2, 2, HALF, 128), BF),
    pltpu.VMEM((4, 256, 128), F32),
    pltpu.VMEM((4, 256, 1), F32),
    pltpu.VMEM((4, 256, 1), F32),
    pltpu.VMEM((2, HALF, 128), BF),
    pltpu.VMEM((1, 128), F32),
    pltpu.VMEM((ROWS, D), F32),
    pltpu.VMEM((ROWS, D), BF),
    pltpu.SemaphoreType.DMA((NSEM,)),
    pltpu.SemaphoreType.REGULAR,
    pltpu.SemaphoreType.REGULAR,
    pltpu.SemaphoreType.REGULAR,
]


def shards(frames, destination, plan, norm_gain, w_qkv, w_out):
    any_space = pl.BlockSpec(memory_space=pl.ANY)
    return pl.pallas_call(
        kernel,
        out_shape=jax.ShapeDtypeStruct((1, ROWS, D), BF),
        in_specs=[any_space] * 6,
        out_specs=any_space,
        scratch_shapes=SCRATCH,
        compiler_params=pltpu.CompilerParams(
            collective_id=0, has_side_effects=True, vmem_limit_bytes=60 * 2**20
        ),
        name="attend",
    )(frames, destination.reshape(1, ROWS), plan, norm_gain, w_qkv, w_out)


def solution(mesh):
    in_specs = (
        P("rep", "grp", None),
        P("rep", "grp", None),
        P("rep", None),
        P(),
        P(None, "rep"),
        P("rep", None),
    )
    out_specs = P("rep", "grp", None)
    return jax.shard_map(shards, mesh=mesh, in_specs=in_specs, out_specs=out_specs, check_vma=False)
```

```python
import math

import jax
import jax.numpy as jnp
from jax import lax
from jax.experimental import pallas as pl
from jax.experimental.pallas import tpu as pltpu
from jax.sharding import PartitionSpec as P

MESH = pl.DeviceIdType.MESH
NT = (((1,), (1,)), ((), ()))
BF = jnp.bfloat16
F32 = jnp.float32
D = 1280
ROWS = 64
HALF = 32
FR, DE, PL, GA, WL, WOL = 0, 1, 2, 3, 4, 5
XS, XR = 6, 12
WS, WR = 18, 19
OS, OR = 20, 24
QS, QV = 28, 32
FS, FT = 36, 40
SBS = 44
QR = 45
GS, GR = 48, 49
PS, PR = 50, 53
CS, CR = 56, 57
RS = 59
GF = 64
NSEM = 68


def halves(block):
    return jnp.concatenate([block[:, 64:], block[:, :64]], axis=1)


def kernel(
    frames, dest, plan, gain, w_qkv, w_out, out,
    raw, dest_v, plan_v, gain_v, xb, w, wo, sb, own_g, rb, gb, key_mark, query_mark, vd, co, cb, acc, top_v,
    sum_v, spare, spare_g, near, result, sem, line_x, line_y, line_z,
):
    g = lax.axis_index("grp")
    r = lax.axis_index("rep")
    x, z = lax.div(g, 8), lax.rem(g, 8)
    y, c = lax.div(r, 2), lax.rem(r, 2)
    cls = lax.rem(z, 2)
    slot = lax.div(z, 2) * 4 + x

    def at(tx, ty, tz, tc):
        return (tx * 8 + tz, ty * 2 + tc)

    def turn_x(i):
        return lax.rem(x + i, 4)

    def along_x(i):
        return at(turn_x(i), y, z, c)

    def along_y(i):
        return at(x, lax.rem(y + i, 4), z, c)

    def along_z(i):
        return at(x, y, lax.rem(z + i, 8), c)

    sibling = at(x, y, z, 1 - c)

    def remote(src, dst, ssem, rsem, target):
        return pltpu.make_async_remote_copy(
            src_ref=src, dst_ref=dst, send_sem=sem.at[ssem], recv_sem=sem.at[rsem],
            device_id=target, device_id_type=MESH,
        )

    def local(src, dst, s):
        return pltpu.make_async_copy(src, dst, sem.at[s])

    def push(src, dst, ssem, rsem, tx, ty, tz, tc, dummy):
        if dummy is None:
            remote(src, dst, ssem, rsem, at(tx, ty, tz, tc)).start()
            return
        same = (ty == y) & (tz == z) & (tc == c)

        @pl.when(jnp.logical_not(same))
        def _():
            remote(src, dst, ssem, rsem, at(tx, ty, tz, tc)).start()

        @pl.when(same)
        def _():
            local(src, dst, rsem).start()
            local(src, dummy, ssem).start()

    def drain(ref, s):
        local(ref, ref, s).wait()

    loads = [
        local(frames.at[0], raw, FR),
        local(dest, dest_v, DE),
        local(plan, plan_v, PL),
        local(gain, gain_v, GA),
        local(w_qkv, w.at[c], WL),
        local(w_out, wo.at[c, y], WOL),
    ]
    for load in loads:
        load.start()

    barrier = pltpu.get_barrier_semaphore()
    plane = [at(turn_x(i), y, z, c) for i in (1, 2, 3)]
    plane += [at(turn_x(i), y, z, 1 - c) for i in range(4)]
    partners = [along_y(i) for i in (1, 2, 3)] + plane
    partners += [along_z(i) for i in (1, 2, 6, 7)]
    for partner in partners:
        pl.semaphore_signal(barrier, inc=1, device_id=partner, device_id_type=MESH)

    low = lax.broadcasted_iota(jnp.int32, (1, 128), 1) < 64
    loads[0].wait()
    loads[3].wait()
    values = raw[...].astype(F32)
    mean = jnp.mean(values, axis=1, keepdims=True)
    centered = values - mean
    variance = jnp.mean(centered * centered, axis=1, keepdims=True)
    xb[0] = (centered * lax.rsqrt(variance + 1e-05) * gain_v[...][None, :]).astype(BF)

    pl.semaphore_wait(barrier, len(partners))

    upper, lower = pl.ds(0, HALF), pl.ds(HALF, HALF)

    def row_copy(n):
        block, to, part, source = (
            (1, 3, upper, 0), (2, 1, lower, 0), (1, 3, lower, 0), (2, 1, upper, 0),
            (3, 3, upper, 1), (3, 1, lower, 2),
        )[n]
        return remote(xb.at[source, part], xb.at[block, part], XS + n, XR + n, along_y(to))

    for i in (2, 6):
        pl.semaphore_signal(line_z, inc=1, device_id=along_z(i), device_id_type=MESH)
    for n in range(4):
        row_copy(n).start()
    remote(w_qkv, w.at[c], WS, WR, sibling).start()

    loads[1].wait()
    loads[2].wait()
    row32 = lax.broadcasted_iota(jnp.int32, (32, 32), 0)
    col32 = lax.broadcasted_iota(jnp.int32, (32, 32), 1)
    plan_rows = jnp.sum(
        jnp.where(row32 == col32, plan_v[...].astype(F32), 0.0), axis=1, keepdims=True
    )
    hot = dest_v[...] == lax.broadcasted_iota(jnp.int32, (32, ROWS), 0)
    group = jnp.sum(jnp.where(hot, plan_rows, 0.0), axis=0, keepdims=True)
    own_g[...] = jnp.concatenate([group, group], axis=1)

    along = (0, 1, 3, 2)

    def project(start, count, s):
        rows = xb[start : start + count].reshape(count * ROWS, D)
        part = jnp.dot(rows, w[s], preferred_element_type=F32)
        for n in range(count):
            for p in range(3):
                two = part[n * ROWS : (n + 1) * ROWS, 128 * p : 128 * p + 128]
                first, last = two[:HALF], two[HALF:]
                spot = 6 * s + 2 * p
                sb[start + n, spot] = jnp.where(low, first, halves(last)).astype(BF)
                sb[start + n, spot + 1] = jnp.where(low, halves(first), last).astype(BF)

    def scatter(i, blocks):
        tz = lax.rem(y + along[i], 4) + 4 * (1 - c)
        for s in blocks:
            sub = 3 * y + s
            kind, block = lax.div(sub, 4), lax.rem(sub, 4)
            ty = block + 1 - 2 * lax.rem(block, 2)
            for k in (2, 1, 3, 0):
                push(
                    sb.at[i, 4 * s + turn_x(k)], rb.at[kind, cls, pl.ds(slot * HALF, HALF)],
                    SBS, QR + kind, turn_x(k), ty, tz, cls, None if k else spare.at[0],
                )

    loads[4].wait()
    project(0, 1, c)
    pl.semaphore_wait(line_z, 2)
    for partner in plane:
        pl.semaphore_signal(line_x, inc=1, device_id=partner, device_id_type=MESH)
    pl.semaphore_wait(line_x, len(plane))
    for i in (1, 2, 3):
        pl.semaphore_signal(line_y, inc=1, device_id=along_y(i), device_id_type=MESH)
    for n in (0, 1):
        row_copy(n).wait_recv()
        row_copy(4 + n).start()
    remote(w_qkv, w.at[1 - c], WS, WR, sibling).wait_recv()
    project(0, 1, 1 - c)
    scatter(0, (1,))
    pl.semaphore_wait(line_y, 3)
    scatter(0, (0, 2))
    for k in (2, 1, 3, 0):
        push(
            own_g, gb.at[cls, slot], GS, GR, turn_x(k), y, y + 4 * (1 - c), cls,
            None if k else spare_g,
        )
    for n in (2, 3):
        row_copy(n).wait_recv()
    for s in range(2):
        project(1, 2, s)
    scatter(1, (0, 2, 1))
    scatter(2, (0, 2, 1))
    for n in (4, 5):
        row_copy(n).wait_recv()
    for s in range(2):
        project(3, 1, s)
    scatter(3, (0, 2, 1))
    loads[5].wait()
    opposite = lax.rem(y + 2, 4)

    def quarter(ty, tx):
        return wo.at[c, ty, pl.ds(pl.multiple_of(tx * HALF, HALF), HALF)]

    def shard_copy(i):
        ref = quarter(y, x) if i == 2 else wo.at[c, y]
        return remote(ref, ref, OS + i, OR + i, along_y(4 - i))

    def quarter_copy(i):
        ref = quarter(opposite, x)
        return remote(ref, ref, QS + i, QV + i, along_x(i))

    for i in (2, 1, 3):
        shard_copy(i).start()

    def to_sibling(i):
        ty = lax.rem(y + i, 4)
        return remote(wo.at[c, ty], wo.at[c, ty], FS + i, FT + i, sibling)

    to_sibling(0).start()

    mine = [rb.at[1, c], rb.at[2, c], gb.at[c]]
    theirs = [rb.at[1, 1 - c], rb.at[2, 1 - c], gb.at[1 - c]]

    def swap(n, s):
        drain(mine[n], s)
        remote(mine[n], mine[n], PS + n, PR + n, sibling).start()

    lane = lax.broadcasted_iota(jnp.int32, (1, 128), 1)
    lane_group = jnp.where(lane < 64, lax.rem(lax.div(lane, 4), 8), -1).astype(F32)
    row = lax.rem(lax.broadcasted_iota(jnp.int32, (128, 128), 0), HALF)
    col = lax.broadcasted_iota(jnp.int32, (128, 128), 1)

    def group_columns(half, m):
        table = jnp.concatenate(
            [jnp.broadcast_to(gb[half, 4 * m + n], (HALF, 128)) for n in range(4)], axis=0
        )
        return [
            jnp.sum(jnp.where(col == row + base, table, 0.0), axis=1, keepdims=True)
            for base in (0, HALF)
        ]

    def mark_keys(half, m):
        for_low, for_high = group_columns(half, m)
        hit = jnp.where(lane < 32, for_low, for_high) == lane_group
        key_mark[half, 128 * m : 128 * m + 128, :] = jnp.where(hit, 1.0, 0.0).astype(BF)
        if half is not c:
            return
        group = jnp.concatenate([for_low, for_high], axis=0)
        miss = jnp.where(group == lane_group, 0.0, -(2.0**127))
        query_mark[0, m] = jnp.where(lane < 32, miss, 0.0).astype(BF)
        query_mark[1, m] = jnp.where((lane >= 32) & (lane < 64), miss, 0.0).astype(BF)

    owner_y, owner_c = lax.rem(z, 4), 1 - lax.div(z, 4)
    drain(gb.at[c], GR)

    def pass_groups(i):
        return remote(gb.at[c], gb.at[c], GF + i, GR, along_y(i))

    @pl.when(y == owner_y)
    def _():
        for i in (2, 1, 3):
            pass_groups(i).start()

    remote(gb.at[c], gb.at[c], PS + 2, PR + 2, sibling).start()
    for m in range(4):
        mark_keys(c, m)
    drain(theirs[2], PR + 2)
    for m in range(4):
        mark_keys(1 - c, m)
    swap(0, QR + 1)
    swap(1, QR + 2)
    drain(rb.at[0, c], QR)
    shard_copy(2).wait_recv()
    for i in (1, 2, 3):
        quarter_copy(i).start()

    def spread_values(half):
        vals = rb[2, half]
        turned = halves(vals)
        vd[half, 0:512, :] = jnp.where(low, vals, turned)
        vd[half, 512:1024, :] = jnp.where(low, turned, vals)

    away = lax.rem(y + 4 - owner_y, 4)
    place = away + lax.div(away, 2) * (5 - 2 * away)
    scale = 0.125 * math.log2(math.e)

    def scores(m, half):
        q = rb[0, c, 128 * m : 128 * m + 128, :]
        turned = halves(q)
        none = jnp.zeros_like(q)
        q_low = jnp.concatenate([jnp.where(low, q, none), jnp.where(low, turned, none)], axis=0)
        q_high = jnp.concatenate([jnp.where(low, none, turned), jnp.where(low, none, q)], axis=0)
        keys = jnp.concatenate([rb[1, half], key_mark[half]], axis=1)
        both = [
            lax.dot_general(
                jnp.concatenate([part, query_mark[n, m]], axis=1), keys, NT,
                preferred_element_type=F32,
            )
            for n, part in enumerate((q_low, q_high))
        ]
        top = jnp.maximum(
            jnp.max(both[0], axis=1, keepdims=True), jnp.max(both[1], axis=1, keepdims=True)
        )
        return both[0], both[1], top

    def weigh(s_low, s_high, top, half):
        p_low = jnp.exp2((s_low - top) * scale)
        p_high = jnp.exp2((s_high - top) * scale)
        total = jnp.sum(p_low, axis=1, keepdims=True) + jnp.sum(p_high, axis=1, keepdims=True)
        mixed = jnp.dot(p_low.astype(BF), vd[half, 0:512, :], preferred_element_type=F32)
        mixed += jnp.dot(p_high.astype(BF), vd[half, 512:1024, :], preferred_element_type=F32)
        return total, mixed

    def first_part(m):
        s_low, s_high, top = scores(m, c)
        total, mixed = weigh(s_low, s_high, top, c)
        top_v[m] = top
        sum_v[m] = total
        acc[m] = mixed

    def second_part(m):
        s_low, s_high, top = scores(m, 1 - c)
        before = top_v[m]
        top = jnp.maximum(before, top)
        total, mixed = weigh(s_low, s_high, top, 1 - c)
        factor = jnp.exp2((before - top) * scale)
        context = (acc[m] * factor + mixed) / (sum_v[m] * factor + total)
        co[128 * m : 128 * m + 128, :] = jnp.where(low, context[:128], context[128:]).astype(BF)
        for k in (2, 1, 3, 0):
            push(
                co.at[pl.ds(128 * m + HALF * turn_x(k), HALF)],
                cb.at[place, lax.div(x, 2), lax.rem(x, 2)],
                CS, CR + lax.div(place, 3), turn_x(k), owner_y, 2 * m + c, owner_c, None if k else spare.at[1],
            )

    spread_values(c)
    for m in range(3):
        first_part(m)
    drain(theirs[0], PR)
    drain(theirs[1], PR + 1)
    spread_values(1 - c)
    for m in range(3):
        second_part(m)
    first_part(3)
    second_part(3)

    for i in (1, 3, 2):
        if i == 2:
            for k in (1, 2, 3):
                quarter_copy(k).wait_recv()
        else:
            shard_copy(i).wait_recv()
        to_sibling(i).start()

    for n in range(6):
        row_copy(n).wait_send()
    for i in (1, 2, 3):
        shard_copy(i).wait_send()
        quarter_copy(i).wait_send()
    remote(w_qkv, w.at[c], WS, WR, sibling).wait_send()
    drain(sb, SBS)
    for n in range(3):
        remote(mine[n], mine[n], PS + n, PR + n, sibling).wait_send()
    drain(gb.at[c, pl.ds(0, 4)], GS)

    @pl.when(y == owner_y)
    def _():
        for i in (1, 2, 3):
            pass_groups(i).wait_send()


    def gathered(p):
        both = []
        for tc in range(2):
            even, odd = cb[p, tc, 0], cb[p, tc, 1]
            both.append(
                jnp.concatenate(
                    [jnp.where(low, even, halves(odd)), jnp.where(low, halves(even), odd)], axis=0
                )
            )
        return jnp.concatenate(both, axis=1)

    def product(p, context, cols):
        ty = lax.rem(y + (0, 1, 3, 2)[p], 4)
        ty = ty + 1 - 2 * lax.rem(ty, 2)
        weights = wo[:, ty, :, cols].reshape(256, 256)
        return jnp.dot(context, weights, preferred_element_type=F32)

    drain(cb.at[pl.ds(0, 3)], CR)
    for i in range(4):
        ty = lax.rem(y + i, 4)
        remote(wo.at[c, ty], wo.at[1 - c, ty], FS + i, FT + i, sibling).wait_recv()
    contexts = [gathered(p) for p in range(3)]
    spans = [slice(256 * n, 256 * n + 256) for n in range(5)]
    for cols in spans:
        near[:, cols] = sum(product(p, contexts[p], cols) for p in range(3))
    drain(cb.at[3], CR + 1)
    context = gathered(3)
    leaving = []
    for n, cols in enumerate(spans):
        result[:, cols] = (near[:, cols] + product(3, context, cols)).astype(BF)
        piece = local(result.at[:, cols], out.at[0, :, cols], RS + n)
        piece.start()
        leaving.append(piece)

    for i in range(4):
        to_sibling(i).wait_send()
    drain(co, CS)
    for piece in leaving:
        piece.wait()


SCRATCH = [
    pltpu.VMEM((ROWS, D), BF),
    pltpu.VMEM((1, ROWS), jnp.int32),
    pltpu.VMEM((1, 32), jnp.int32),
    pltpu.VMEM((D,), F32),
    pltpu.VMEM((4, ROWS, D), BF),
    pltpu.VMEM((2, D, 384), BF),
    pltpu.VMEM((2, 4, 128, D), BF),
    pltpu.VMEM((4, 12, HALF, 128), BF),
    pltpu.VMEM((1, 128), F32),
    pltpu.VMEM((3, 2, 512, 128), BF),
    pltpu.VMEM((2, 16, 1, 128), F32),
    pltpu.VMEM((2, 512, 128), BF),
    pltpu.VMEM((2, 4, 256, 128), BF),
    pltpu.VMEM((2, 1024, 128), BF),
    pltpu.VMEM((512, 128), BF),
    pltpu.VMEM((4, 2, 2, HALF, 128), BF),
    pltpu.VMEM((4, 256, 128), F32),
    pltpu.VMEM((4, 256, 1), F32),
    pltpu.VMEM((4, 256, 1), F32),
    pltpu.VMEM((2, HALF, 128), BF),
    pltpu.VMEM((1, 128), F32),
    pltpu.VMEM((ROWS, D), F32),
    pltpu.VMEM((ROWS, D), BF),
    pltpu.SemaphoreType.DMA((NSEM,)),
    pltpu.SemaphoreType.REGULAR,
    pltpu.SemaphoreType.REGULAR,
    pltpu.SemaphoreType.REGULAR,
]


def shards(frames, destination, plan, norm_gain, w_qkv, w_out):
    any_space = pl.BlockSpec(memory_space=pl.ANY)
    return pl.pallas_call(
        kernel,
        out_shape=jax.ShapeDtypeStruct((1, ROWS, D), BF),
        in_specs=[any_space] * 6,
        out_specs=any_space,
        scratch_shapes=SCRATCH,
        compiler_params=pltpu.CompilerParams(
            collective_id=0, has_side_effects=True, vmem_limit_bytes=60 * 2**20
        ),
        name="attend",
    )(frames, destination.reshape(1, ROWS), plan, norm_gain, w_qkv, w_out)


def solution(mesh):
    in_specs = (
        P("rep", "grp", None),
        P("rep", "grp", None),
        P("rep", None),
        P(),
        P(None, "rep"),
        P("rep", None),
    )
    out_specs = P("rep", "grp", None)
    return jax.shard_map(shards, mesh=mesh, in_specs=in_specs, out_specs=out_specs, check_vma=False)
```

```python
import math

import jax
import jax.numpy as jnp
from jax import lax
from jax.experimental import pallas as pl
from jax.experimental.pallas import tpu as pltpu
from jax.sharding import PartitionSpec as P

MESH = pl.DeviceIdType.MESH
NT = (((1,), (1,)), ((), ()))
BF = jnp.bfloat16
F32 = jnp.float32
D = 1280
ROWS = 64
HALF = 32
FR, DE, PL, GA, WL, WOL = 0, 1, 2, 3, 4, 5
XS, XR = 6, 12
WS, WR = 18, 19
OS, OR = 20, 24
QS, QV = 28, 32
FS, FT = 36, 40
SBS = 44
QR = 45
GS, GR = 48, 49
PS, PR = 50, 53
CS, CR = 56, 57
RS = 59
NSEM = 64


def halves(block):
    return jnp.concatenate([block[:, 64:], block[:, :64]], axis=1)


def kernel(
    frames, dest, plan, gain, w_qkv, w_out, out,
    raw, dest_v, plan_v, gain_v, xb, w, wo, sb, own_g, rb, gb, key_mark, query_mark, vd, co, cb, acc, top_v,
    sum_v, spare, spare_g, near, result, sem, line_x, line_y, line_z,
):
    g = lax.axis_index("grp")
    r = lax.axis_index("rep")
    x, z = lax.div(g, 8), lax.rem(g, 8)
    y, c = lax.div(r, 2), lax.rem(r, 2)
    cls = lax.rem(z, 2)
    slot = lax.div(z, 2) * 4 + x

    def at(tx, ty, tz, tc):
        return (tx * 8 + tz, ty * 2 + tc)

    def turn_x(i):
        return lax.rem(x + i, 4)

    def along_x(i):
        return at(turn_x(i), y, z, c)

    def along_y(i):
        return at(x, lax.rem(y + i, 4), z, c)

    def along_z(i):
        return at(x, y, lax.rem(z + i, 8), c)

    sibling = at(x, y, z, 1 - c)

    def remote(src, dst, ssem, rsem, target):
        return pltpu.make_async_remote_copy(
            src_ref=src, dst_ref=dst, send_sem=sem.at[ssem], recv_sem=sem.at[rsem],
            device_id=target, device_id_type=MESH,
        )

    def local(src, dst, s):
        return pltpu.make_async_copy(src, dst, sem.at[s])

    def push(src, dst, ssem, rsem, tx, ty, tz, tc, dummy):
        if dummy is None:
            remote(src, dst, ssem, rsem, at(tx, ty, tz, tc)).start()
            return
        same = (ty == y) & (tz == z) & (tc == c)

        @pl.when(jnp.logical_not(same))
        def _():
            remote(src, dst, ssem, rsem, at(tx, ty, tz, tc)).start()

        @pl.when(same)
        def _():
            local(src, dst, rsem).start()
            local(src, dummy, ssem).start()

    def drain(ref, s):
        local(ref, ref, s).wait()

    loads = [
        local(frames.at[0], raw, FR),
        local(dest, dest_v, DE),
        local(plan, plan_v, PL),
        local(gain, gain_v, GA),
        local(w_qkv, w.at[c], WL),
        local(w_out, wo.at[c, y], WOL),
    ]
    for load in loads:
        load.start()

    barrier = pltpu.get_barrier_semaphore()
    plane = [at(turn_x(i), y, z, c) for i in (1, 2, 3)]
    plane += [at(turn_x(i), y, z, 1 - c) for i in range(4)]
    partners = [along_y(i) for i in (1, 2, 3)] + plane
    partners += [along_z(i) for i in (1, 2, 6, 7)]
    for partner in partners:
        pl.semaphore_signal(barrier, inc=1, device_id=partner, device_id_type=MESH)

    low = lax.broadcasted_iota(jnp.int32, (1, 128), 1) < 64
    loads[0].wait()
    loads[3].wait()
    values = raw[...].astype(F32)
    mean = jnp.mean(values, axis=1, keepdims=True)
    centered = values - mean
    variance = jnp.mean(centered * centered, axis=1, keepdims=True)
    xb[0] = (centered * lax.rsqrt(variance + 1e-05) * gain_v[...][None, :]).astype(BF)

    pl.semaphore_wait(barrier, len(partners))

    upper, lower = pl.ds(0, HALF), pl.ds(HALF, HALF)

    def row_copy(n):
        block, to, part, source = (
            (1, 3, upper, 0), (2, 1, lower, 0), (1, 3, lower, 0), (2, 1, upper, 0),
            (3, 3, upper, 1), (3, 1, lower, 2),
        )[n]
        return remote(xb.at[source, part], xb.at[block, part], XS + n, XR + n, along_y(to))

    for i in (2, 6):
        pl.semaphore_signal(line_z, inc=1, device_id=along_z(i), device_id_type=MESH)
    for n in range(4):
        row_copy(n).start()
    remote(w_qkv, w.at[c], WS, WR, sibling).start()

    loads[1].wait()
    loads[2].wait()
    row32 = lax.broadcasted_iota(jnp.int32, (32, 32), 0)
    col32 = lax.broadcasted_iota(jnp.int32, (32, 32), 1)
    plan_rows = jnp.sum(
        jnp.where(row32 == col32, plan_v[...].astype(F32), 0.0), axis=1, keepdims=True
    )
    hot = dest_v[...] == lax.broadcasted_iota(jnp.int32, (32, ROWS), 0)
    group = jnp.sum(jnp.where(hot, plan_rows, 0.0), axis=0, keepdims=True)
    own_g[...] = jnp.concatenate([group, group], axis=1)

    along = (0, 1, 3, 2)

    def project(start, count, s):
        rows = xb[start : start + count].reshape(count * ROWS, D)
        part = jnp.dot(rows, w[s], preferred_element_type=F32)
        for n in range(count):
            for p in range(3):
                two = part[n * ROWS : (n + 1) * ROWS, 128 * p : 128 * p + 128]
                first, last = two[:HALF], two[HALF:]
                spot = 6 * s + 2 * p
                sb[start + n, spot] = jnp.where(low, first, halves(last)).astype(BF)
                sb[start + n, spot + 1] = jnp.where(low, halves(first), last).astype(BF)

    def scatter(i, blocks):
        tz = lax.rem(y + along[i], 4) + 4 * (1 - c)
        for s in blocks:
            sub = 3 * y + s
            kind, block = lax.div(sub, 4), lax.rem(sub, 4)
            ty = block + 1 - 2 * lax.rem(block, 2)
            for k in (2, 1, 3, 0):
                push(
                    sb.at[i, 4 * s + turn_x(k)], rb.at[kind, cls, pl.ds(slot * HALF, HALF)],
                    SBS, QR + kind, turn_x(k), ty, tz, cls, None if k else spare.at[0],
                )

    loads[4].wait()
    project(0, 1, c)
    pl.semaphore_wait(line_z, 2)
    for partner in plane:
        pl.semaphore_signal(line_x, inc=1, device_id=partner, device_id_type=MESH)
    pl.semaphore_wait(line_x, len(plane))
    for i in (1, 2, 3):
        pl.semaphore_signal(line_y, inc=1, device_id=along_y(i), device_id_type=MESH)
    for n in (0, 1):
        row_copy(n).wait_recv()
        row_copy(4 + n).start()
    remote(w_qkv, w.at[1 - c], WS, WR, sibling).wait_recv()
    project(0, 1, 1 - c)
    scatter(0, (1,))
    pl.semaphore_wait(line_y, 3)
    scatter(0, (0, 2))
    for n in (2, 3):
        row_copy(n).wait_recv()
    for s in range(2):
        project(1, 2, s)
    scatter(1, (0, 2, 1))
    scatter(2, (0, 2, 1))
    for n in (4, 5):
        row_copy(n).wait_recv()
    for s in range(2):
        project(3, 1, s)
    scatter(3, (0, 2, 1))
    for k in (2, 1, 3, 0):
        for i in (2, 1, 3, 0):
            push(
                own_g, gb.at[cls, slot], GS, GR, turn_x(k), lax.rem(y + i, 4), y + 4 * (1 - c),
                cls, None if k or i else spare_g,
            )
    loads[5].wait()
    opposite = lax.rem(y + 2, 4)

    def quarter(ty, tx):
        return wo.at[c, ty, pl.ds(pl.multiple_of(tx * HALF, HALF), HALF)]

    def shard_copy(i):
        ref = quarter(y, x) if i == 2 else wo.at[c, y]
        return remote(ref, ref, OS + i, OR + i, along_y(4 - i))

    def quarter_copy(i):
        ref = quarter(opposite, x)
        return remote(ref, ref, QS + i, QV + i, along_x(i))

    for i in (2, 1, 3):
        shard_copy(i).start()

    def to_sibling(i):
        ty = lax.rem(y + i, 4)
        return remote(wo.at[c, ty], wo.at[c, ty], FS + i, FT + i, sibling)

    to_sibling(0).start()

    mine = [rb.at[1, c], rb.at[2, c], gb.at[c]]
    theirs = [rb.at[1, 1 - c], rb.at[2, 1 - c], gb.at[1 - c]]

    def swap(n, s):
        drain(mine[n], s)
        remote(mine[n], mine[n], PS + n, PR + n, sibling).start()

    lane = lax.broadcasted_iota(jnp.int32, (1, 128), 1)
    lane_group = jnp.where(lane < 64, lax.rem(lax.div(lane, 4), 8), -1).astype(F32)
    row = lax.rem(lax.broadcasted_iota(jnp.int32, (128, 128), 0), HALF)
    col = lax.broadcasted_iota(jnp.int32, (128, 128), 1)

    def group_columns(half, m):
        table = jnp.concatenate(
            [jnp.broadcast_to(gb[half, 4 * m + n], (HALF, 128)) for n in range(4)], axis=0
        )
        return [
            jnp.sum(jnp.where(col == row + base, table, 0.0), axis=1, keepdims=True)
            for base in (0, HALF)
        ]

    def mark_keys(half, m):
        for_low, for_high = group_columns(half, m)
        hit = jnp.where(lane < 32, for_low, for_high) == lane_group
        key_mark[half, 128 * m : 128 * m + 128, :] = jnp.where(hit, 1.0, 0.0).astype(BF)
        if half is not c:
            return
        group = jnp.concatenate([for_low, for_high], axis=0)
        miss = jnp.where(group == lane_group, 0.0, -(2.0**127))
        query_mark[0, m] = jnp.where(lane < 32, miss, 0.0).astype(BF)
        query_mark[1, m] = jnp.where((lane >= 32) & (lane < 64), miss, 0.0).astype(BF)

    swap(2, GR)
    for m in range(4):
        mark_keys(c, m)
    drain(theirs[2], PR + 2)
    for m in range(4):
        mark_keys(1 - c, m)
    swap(0, QR + 1)
    swap(1, QR + 2)
    drain(rb.at[0, c], QR)
    shard_copy(2).wait_recv()
    for i in (1, 2, 3):
        quarter_copy(i).start()

    def spread_values(half):
        vals = rb[2, half]
        turned = halves(vals)
        vd[half, 0:512, :] = jnp.where(low, vals, turned)
        vd[half, 512:1024, :] = jnp.where(low, turned, vals)

    owner_y, owner_c = lax.rem(z, 4), 1 - lax.div(z, 4)
    away = lax.rem(y + 4 - owner_y, 4)
    place = away + lax.div(away, 2) * (5 - 2 * away)
    scale = 0.125 * math.log2(math.e)

    def scores(m, half):
        q = rb[0, c, 128 * m : 128 * m + 128, :]
        turned = halves(q)
        none = jnp.zeros_like(q)
        q_low = jnp.concatenate([jnp.where(low, q, none), jnp.where(low, turned, none)], axis=0)
        q_high = jnp.concatenate([jnp.where(low, none, turned), jnp.where(low, none, q)], axis=0)
        keys = jnp.concatenate([rb[1, half], key_mark[half]], axis=1)
        both = [
            lax.dot_general(
                jnp.concatenate([part, query_mark[n, m]], axis=1), keys, NT,
                preferred_element_type=F32,
            )
            for n, part in enumerate((q_low, q_high))
        ]
        top = jnp.maximum(
            jnp.max(both[0], axis=1, keepdims=True), jnp.max(both[1], axis=1, keepdims=True)
        )
        return both[0], both[1], top

    def weigh(s_low, s_high, top, half):
        p_low = jnp.exp2((s_low - top) * scale)
        p_high = jnp.exp2((s_high - top) * scale)
        total = jnp.sum(p_low, axis=1, keepdims=True) + jnp.sum(p_high, axis=1, keepdims=True)
        mixed = jnp.dot(p_low.astype(BF), vd[half, 0:512, :], preferred_element_type=F32)
        mixed += jnp.dot(p_high.astype(BF), vd[half, 512:1024, :], preferred_element_type=F32)
        return total, mixed

    def first_part(m):
        s_low, s_high, top = scores(m, c)
        total, mixed = weigh(s_low, s_high, top, c)
        top_v[m] = top
        sum_v[m] = total
        acc[m] = mixed

    def second_part(m):
        s_low, s_high, top = scores(m, 1 - c)
        before = top_v[m]
        top = jnp.maximum(before, top)
        total, mixed = weigh(s_low, s_high, top, 1 - c)
        factor = jnp.exp2((before - top) * scale)
        context = (acc[m] * factor + mixed) / (sum_v[m] * factor + total)
        co[128 * m : 128 * m + 128, :] = jnp.where(low, context[:128], context[128:]).astype(BF)
        for k in (2, 1, 3, 0):
            push(
                co.at[pl.ds(128 * m + HALF * turn_x(k), HALF)],
                cb.at[place, lax.div(x, 2), lax.rem(x, 2)],
                CS, CR + lax.div(place, 3), turn_x(k), owner_y, 2 * m + c, owner_c, None if k else spare.at[1],
            )

    spread_values(c)
    for m in range(3):
        first_part(m)
    drain(theirs[0], PR)
    drain(theirs[1], PR + 1)
    spread_values(1 - c)
    for m in range(3):
        second_part(m)
    first_part(3)
    second_part(3)

    for i in (1, 3, 2):
        if i == 2:
            for k in (1, 2, 3):
                quarter_copy(k).wait_recv()
        else:
            shard_copy(i).wait_recv()
        to_sibling(i).start()

    for n in range(6):
        row_copy(n).wait_send()
    for i in (1, 2, 3):
        shard_copy(i).wait_send()
        quarter_copy(i).wait_send()
    remote(w_qkv, w.at[c], WS, WR, sibling).wait_send()
    drain(sb, SBS)
    for n in range(3):
        remote(mine[n], mine[n], PS + n, PR + n, sibling).wait_send()
    drain(gb.at[c], GS)

    def gathered(p):
        both = []
        for tc in range(2):
            even, odd = cb[p, tc, 0], cb[p, tc, 1]
            both.append(
                jnp.concatenate(
                    [jnp.where(low, even, halves(odd)), jnp.where(low, halves(even), odd)], axis=0
                )
            )
        return jnp.concatenate(both, axis=1)

    def product(p, context, cols):
        ty = lax.rem(y + (0, 1, 3, 2)[p], 4)
        ty = ty + 1 - 2 * lax.rem(ty, 2)
        weights = wo[:, ty, :, cols].reshape(256, 256)
        return jnp.dot(context, weights, preferred_element_type=F32)

    drain(cb.at[pl.ds(0, 3)], CR)
    for i in range(4):
        ty = lax.rem(y + i, 4)
        remote(wo.at[c, ty], wo.at[1 - c, ty], FS + i, FT + i, sibling).wait_recv()
    contexts = [gathered(p) for p in range(3)]
    spans = [slice(256 * n, 256 * n + 256) for n in range(5)]
    for cols in spans:
        near[:, cols] = sum(product(p, contexts[p], cols) for p in range(3))
    drain(cb.at[3], CR + 1)
    context = gathered(3)
    leaving = []
    for n, cols in enumerate(spans):
        result[:, cols] = (near[:, cols] + product(3, context, cols)).astype(BF)
        piece = local(result.at[:, cols], out.at[0, :, cols], RS + n)
        piece.start()
        leaving.append(piece)

    for i in range(4):
        to_sibling(i).wait_send()
    drain(co, CS)
    for piece in leaving:
        piece.wait()


SCRATCH = [
    pltpu.VMEM((ROWS, D), BF),
    pltpu.VMEM((1, ROWS), jnp.int32),
    pltpu.VMEM((1, 32), jnp.int32),
    pltpu.VMEM((D,), F32),
    pltpu.VMEM((4, ROWS, D), BF),
    pltpu.VMEM((2, D, 384), BF),
    pltpu.VMEM((2, 4, 128, D), BF),
    pltpu.VMEM((4, 12, HALF, 128), BF),
    pltpu.VMEM((1, 128), F32),
    pltpu.VMEM((3, 2, 512, 128), BF),
    pltpu.VMEM((2, 16, 1, 128), F32),
    pltpu.VMEM((2, 512, 128), BF),
    pltpu.VMEM((2, 4, 256, 128), BF),
    pltpu.VMEM((2, 1024, 128), BF),
    pltpu.VMEM((512, 128), BF),
    pltpu.VMEM((4, 2, 2, HALF, 128), BF),
    pltpu.VMEM((4, 256, 128), F32),
    pltpu.VMEM((4, 256, 1), F32),
    pltpu.VMEM((4, 256, 1), F32),
    pltpu.VMEM((2, HALF, 128), BF),
    pltpu.VMEM((1, 128), F32),
    pltpu.VMEM((ROWS, D), F32),
    pltpu.VMEM((ROWS, D), BF),
    pltpu.SemaphoreType.DMA((NSEM,)),
    pltpu.SemaphoreType.REGULAR,
    pltpu.SemaphoreType.REGULAR,
    pltpu.SemaphoreType.REGULAR,
]


def shards(frames, destination, plan, norm_gain, w_qkv, w_out):
    any_space = pl.BlockSpec(memory_space=pl.ANY)
    return pl.pallas_call(
        kernel,
        out_shape=jax.ShapeDtypeStruct((1, ROWS, D), BF),
        in_specs=[any_space] * 6,
        out_specs=any_space,
        scratch_shapes=SCRATCH,
        compiler_params=pltpu.CompilerParams(
            collective_id=0, has_side_effects=True, vmem_limit_bytes=60 * 2**20
        ),
        name="attend",
    )(frames, destination.reshape(1, ROWS), plan, norm_gain, w_qkv, w_out)


def solution(mesh):
    in_specs = (
        P("rep", "grp", None),
        P("rep", "grp", None),
        P("rep", None),
        P(),
        P(None, "rep"),
        P("rep", None),
    )
    out_specs = P("rep", "grp", None)
    return jax.shard_map(shards, mesh=mesh, in_specs=in_specs, out_specs=out_specs, check_vma=False)
```

```python
import math

import jax
import jax.numpy as jnp
from jax import lax
from jax.experimental import pallas as pl
from jax.experimental.pallas import tpu as pltpu
from jax.sharding import PartitionSpec as P

MESH = pl.DeviceIdType.MESH
NT = (((1,), (1,)), ((), ()))
BF = jnp.bfloat16
F32 = jnp.float32
D = 1280
ROWS = 64
HALF = 32
FR, DE, PL, GA, WL, WOL = 0, 1, 2, 3, 4, 5
XS, XR = 6, 12
WS, WR = 18, 19
OS, OR = 20, 24
QS, QV = 28, 32
FS, FT = 36, 40
SBS = 44
QR = 45
GS, GR = 48, 49
PS, PR = 50, 53
CS, CR = 56, 57
RS = 59
GX, GY = 64, 68
NSEM = 72


def halves(block):
    return jnp.concatenate([block[:, 64:], block[:, :64]], axis=1)


def kernel(
    frames, dest, plan, gain, w_qkv, w_out, out,
    raw, dest_v, plan_v, gain_v, xb, w, wo, sb, line_g, rb, gb, key_mark, query_mark, vd, co, cb, acc, top_v,
    sum_v, near, result, sem, line_x, line_y, line_z,
):
    g = lax.axis_index("grp")
    r = lax.axis_index("rep")
    x, z = lax.div(g, 8), lax.rem(g, 8)
    y, c = lax.div(r, 2), lax.rem(r, 2)
    cls = lax.div(z, 4)
    slot = lax.rem(z, 4) * 4 + x

    def at(tx, ty, tz, tc):
        return (tx * 8 + tz, ty * 2 + tc)

    def turn_x(i):
        return lax.rem(x + i, 4)

    def along_x(i):
        return at(turn_x(i), y, z, c)

    def along_y(i):
        return at(x, lax.rem(y + i, 4), z, c)

    def along_z(i):
        return at(x, y, lax.rem(z + i, 8), c)

    sibling = at(x, y, z, 1 - c)

    def remote(src, dst, ssem, rsem, target):
        return pltpu.make_async_remote_copy(
            src_ref=src, dst_ref=dst, send_sem=sem.at[ssem], recv_sem=sem.at[rsem],
            device_id=target, device_id_type=MESH,
        )

    def local(src, dst, s):
        return pltpu.make_async_copy(src, dst, sem.at[s])

    def push(src, dst, ssem, rsem, tx, ty, tz, tc):
        remote(src, dst, ssem, rsem, at(tx, ty, tz, tc)).start()

    def drain(ref, s):
        local(ref, ref, s).wait()

    loads = [
        local(frames.at[0], raw, FR),
        local(dest, dest_v, DE),
        local(plan, plan_v, PL),
        local(gain, gain_v, GA),
        local(w_qkv, w.at[c], WL),
        local(w_out, wo.at[c, y], WOL),
    ]
    for load in loads:
        load.start()

    barrier = pltpu.get_barrier_semaphore()
    plane = [at(turn_x(i), y, z, c) for i in (1, 2, 3)]
    plane += [at(turn_x(i), y, z, 1 - c) for i in range(4)]
    partners = [along_y(i) for i in (1, 2, 3)] + plane
    partners += [along_z(i) for i in (1, 2, 6, 7)]
    for partner in partners:
        pl.semaphore_signal(barrier, inc=1, device_id=partner, device_id_type=MESH)

    low = lax.broadcasted_iota(jnp.int32, (1, 128), 1) < 64
    loads[0].wait()
    loads[3].wait()
    values = raw[...].astype(F32)
    mean = jnp.mean(values, axis=1, keepdims=True)
    centered = values - mean
    variance = jnp.mean(centered * centered, axis=1, keepdims=True)
    xb[0] = (centered * lax.rsqrt(variance + 1e-05) * gain_v[...][None, :]).astype(BF)

    pl.semaphore_wait(barrier, len(partners))

    upper, lower = pl.ds(0, HALF), pl.ds(HALF, HALF)

    def row_copy(n):
        block, to, part, source = (
            (1, 3, upper, 0), (2, 1, lower, 0), (1, 3, lower, 0), (2, 1, upper, 0),
            (3, 3, upper, 1), (3, 1, lower, 2),
        )[n]
        return remote(xb.at[source, part], xb.at[block, part], XS + n, XR + n, along_y(to))

    for i in (2, 6):
        pl.semaphore_signal(line_z, inc=1, device_id=along_z(i), device_id_type=MESH)
    for n in range(4):
        row_copy(n).start()
    remote(w_qkv, w.at[c], WS, WR, sibling).start()

    loads[1].wait()
    loads[2].wait()
    row32 = lax.broadcasted_iota(jnp.int32, (32, 32), 0)
    col32 = lax.broadcasted_iota(jnp.int32, (32, 32), 1)
    plan_rows = jnp.sum(
        jnp.where(row32 == col32, plan_v[...].astype(F32), 0.0), axis=1, keepdims=True
    )
    hot = dest_v[...] == lax.broadcasted_iota(jnp.int32, (32, ROWS), 0)
    group = jnp.sum(jnp.where(hot, plan_rows, 0.0), axis=0, keepdims=True)
    line_g[0] = jnp.concatenate([group, group], axis=1)

    def group_copy(i):
        return remote(line_g.at[0], line_g.at[i], GX + i, GY + i, along_y(4 - i))

    for i in (2, 1, 3):
        group_copy(i).start()

    along = (0, 1, 3, 2)

    def project(start, count, s):
        rows = xb[start : start + count].reshape(count * ROWS, D)
        part = jnp.dot(rows, w[s], preferred_element_type=F32)
        for n in range(count):
            for p in range(3):
                two = part[n * ROWS : (n + 1) * ROWS, 128 * p : 128 * p + 128]
                first, last = two[:HALF], two[HALF:]
                spot = 6 * s + 2 * p
                sb[start + n, spot] = jnp.where(low, first, halves(last)).astype(BF)
                sb[start + n, spot + 1] = jnp.where(low, halves(first), last).astype(BF)

    def scatter(i, blocks):
        tz = lax.rem(y + along[i], 4) + 4 * (1 - c)
        for s in blocks:
            sub = 3 * y + s
            kind, block = lax.div(sub, 4), lax.rem(sub, 4)
            ty = block + 1 - 2 * lax.rem(block, 2)
            for k in (2, 1, 3, 0):
                push(
                    sb.at[i, 4 * s + turn_x(k)], rb.at[kind, cls, pl.ds(slot * HALF, HALF)],
                    SBS, QR + kind, turn_x(k), ty, tz, cls,
                )

    loads[4].wait()
    project(0, 1, c)
    pl.semaphore_wait(line_z, 2)
    for partner in plane:
        pl.semaphore_signal(line_x, inc=1, device_id=partner, device_id_type=MESH)
    pl.semaphore_wait(line_x, len(plane))
    for i in (1, 2, 3):
        pl.semaphore_signal(line_y, inc=1, device_id=along_y(i), device_id_type=MESH)
    for n in (0, 1):
        row_copy(n).wait_recv()
        row_copy(4 + n).start()
    for i in (0, 1, 3, 2):
        if i:
            group_copy(i).wait_recv()
        tz = lax.rem(y + i, 4) + 4 * (1 - c)
        for k in (2, 1, 3, 0):
            push(line_g.at[i], gb.at[cls, slot], GS, GR, turn_x(k), y, tz, cls)
    remote(w_qkv, w.at[1 - c], WS, WR, sibling).wait_recv()
    project(0, 1, 1 - c)
    scatter(0, (1,))
    pl.semaphore_wait(line_y, 3)
    scatter(0, (0, 2))
    for n in (2, 3):
        row_copy(n).wait_recv()
    for s in range(2):
        project(1, 2, s)
    scatter(1, (0, 2, 1))
    scatter(2, (0, 2, 1))
    for n in (4, 5):
        row_copy(n).wait_recv()
    for s in range(2):
        project(3, 1, s)
    scatter(3, (0, 2, 1))
    loads[5].wait()
    opposite = lax.rem(y + 2, 4)

    def quarter(ty, tx):
        return wo.at[c, ty, pl.ds(pl.multiple_of(tx * HALF, HALF), HALF)]

    def shard_copy(i):
        ref = quarter(y, x) if i == 2 else wo.at[c, y]
        return remote(ref, ref, OS + i, OR + i, along_y(4 - i))

    def quarter_copy(i):
        ref = quarter(opposite, x)
        return remote(ref, ref, QS + i, QV + i, along_x(i))

    for i in (2, 1, 3):
        shard_copy(i).start()

    def to_sibling(i):
        ty = lax.rem(y + i, 4)
        return remote(wo.at[c, ty], wo.at[c, ty], FS + i, FT + i, sibling)

    to_sibling(0).start()

    mine = [rb.at[1, c], rb.at[2, c], gb.at[c]]
    theirs = [rb.at[1, 1 - c], rb.at[2, 1 - c], gb.at[1 - c]]

    def swap(n, s):
        drain(mine[n], s)
        remote(mine[n], mine[n], PS + n, PR + n, sibling).start()

    lane = lax.broadcasted_iota(jnp.int32, (1, 128), 1)
    lane_group = jnp.where(lane < 64, lax.rem(lax.div(lane, 4), 8), -1).astype(F32)
    row = lax.rem(lax.broadcasted_iota(jnp.int32, (128, 128), 0), HALF)
    col = lax.broadcasted_iota(jnp.int32, (128, 128), 1)

    def group_columns(half, m):
        table = jnp.concatenate(
            [jnp.broadcast_to(gb[half, 4 * m + n], (HALF, 128)) for n in range(4)], axis=0
        )
        return [
            jnp.sum(jnp.where(col == row + base, table, 0.0), axis=1, keepdims=True)
            for base in (0, HALF)
        ]

    def mark_keys(half, m):
        for_low, for_high = group_columns(half, m)
        hit = jnp.where(lane < 32, for_low, for_high) == lane_group
        key_mark[half, 128 * m : 128 * m + 128, :] = jnp.where(hit, 1.0, 0.0).astype(BF)
        if half is not c:
            return
        group = jnp.concatenate([for_low, for_high], axis=0)
        miss = jnp.where(group == lane_group, 0.0, -(2.0**127))
        query_mark[0, m] = jnp.where(lane < 32, miss, 0.0).astype(BF)
        query_mark[1, m] = jnp.where((lane >= 32) & (lane < 64), miss, 0.0).astype(BF)

    swap(2, GR)
    for m in range(4):
        mark_keys(c, m)
    drain(theirs[2], PR + 2)
    for m in range(4):
        mark_keys(1 - c, m)
    swap(0, QR + 1)
    swap(1, QR + 2)
    drain(rb.at[0, c], QR)
    shard_copy(2).wait_recv()
    for i in (1, 2, 3):
        quarter_copy(i).start()

    def spread_values(half):
        vals = rb[2, half]
        turned = halves(vals)
        vd[half, 0:512, :] = jnp.where(low, vals, turned)
        vd[half, 512:1024, :] = jnp.where(low, turned, vals)

    owner_y, owner_c = lax.rem(z, 4), 1 - lax.div(z, 4)
    away = lax.rem(y + 4 - owner_y, 4)
    place = away + lax.div(away, 2) * (5 - 2 * away)
    scale = 0.125 * math.log2(math.e)

    def scores(m, half):
        q = rb[0, c, 128 * m : 128 * m + 128, :]
        turned = halves(q)
        none = jnp.zeros_like(q)
        q_low = jnp.concatenate([jnp.where(low, q, none), jnp.where(low, turned, none)], axis=0)
        q_high = jnp.concatenate([jnp.where(low, none, turned), jnp.where(low, none, q)], axis=0)
        keys = jnp.concatenate([rb[1, half], key_mark[half]], axis=1)
        both = [
            lax.dot_general(
                jnp.concatenate([part, query_mark[n, m]], axis=1), keys, NT,
                preferred_element_type=F32,
            )
            for n, part in enumerate((q_low, q_high))
        ]
        top = jnp.maximum(
            jnp.max(both[0], axis=1, keepdims=True), jnp.max(both[1], axis=1, keepdims=True)
        )
        return both[0], both[1], top

    def weigh(s_low, s_high, top, half):
        p_low = jnp.exp2((s_low - top) * scale)
        p_high = jnp.exp2((s_high - top) * scale)
        total = jnp.sum(p_low, axis=1, keepdims=True) + jnp.sum(p_high, axis=1, keepdims=True)
        mixed = jnp.dot(p_low.astype(BF), vd[half, 0:512, :], preferred_element_type=F32)
        mixed += jnp.dot(p_high.astype(BF), vd[half, 512:1024, :], preferred_element_type=F32)
        return total, mixed

    def first_part(m):
        s_low, s_high, top = scores(m, c)
        total, mixed = weigh(s_low, s_high, top, c)
        top_v[m] = top
        sum_v[m] = total
        acc[m] = mixed

    def second_part(m):
        s_low, s_high, top = scores(m, 1 - c)
        before = top_v[m]
        top = jnp.maximum(before, top)
        total, mixed = weigh(s_low, s_high, top, 1 - c)
        factor = jnp.exp2((before - top) * scale)
        context = (acc[m] * factor + mixed) / (sum_v[m] * factor + total)
        co[128 * m : 128 * m + 128, :] = jnp.where(low, context[:128], context[128:]).astype(BF)
        for k in (2, 1, 3, 0):
            push(
                co.at[pl.ds(128 * m + HALF * turn_x(k), HALF)],
                cb.at[place, lax.div(x, 2), lax.rem(x, 2)],
                CS, CR + lax.div(place, 3), turn_x(k), owner_y, 4 * c + m, owner_c,
            )

    spread_values(c)
    for m in range(3):
        first_part(m)
    drain(theirs[0], PR)
    drain(theirs[1], PR + 1)
    spread_values(1 - c)
    for m in range(3):
        second_part(m)
    first_part(3)
    second_part(3)

    for i in (1, 3, 2):
        if i == 2:
            for k in (1, 2, 3):
                quarter_copy(k).wait_recv()
        else:
            shard_copy(i).wait_recv()
        to_sibling(i).start()

    for n in range(6):
        row_copy(n).wait_send()
    for i in (1, 2, 3):
        shard_copy(i).wait_send()
        quarter_copy(i).wait_send()
    remote(w_qkv, w.at[c], WS, WR, sibling).wait_send()
    drain(sb, SBS)
    for n in range(3):
        remote(mine[n], mine[n], PS + n, PR + n, sibling).wait_send()
    drain(gb.at[c], GS)
    for i in (1, 2, 3):
        group_copy(i).wait_send()

    def gathered(p):
        both = []
        for tc in range(2):
            even, odd = cb[p, tc, 0], cb[p, tc, 1]
            both.append(
                jnp.concatenate(
                    [jnp.where(low, even, halves(odd)), jnp.where(low, halves(even), odd)], axis=0
                )
            )
        return jnp.concatenate(both, axis=1)

    def product(p, context, cols):
        ty = lax.rem(y + (0, 1, 3, 2)[p], 4)
        ty = ty + 1 - 2 * lax.rem(ty, 2)
        weights = wo[:, ty, :, cols].reshape(256, 256)
        return jnp.dot(context, weights, preferred_element_type=F32)

    drain(cb.at[pl.ds(0, 3)], CR)
    for i in range(4):
        ty = lax.rem(y + i, 4)
        remote(wo.at[c, ty], wo.at[1 - c, ty], FS + i, FT + i, sibling).wait_recv()
    contexts = [gathered(p) for p in range(3)]
    spans = [slice(256 * n, 256 * n + 256) for n in range(5)]
    for cols in spans:
        near[:, cols] = sum(product(p, contexts[p], cols) for p in range(3))
    drain(cb.at[3], CR + 1)
    context = gathered(3)
    leaving = []
    for n, cols in enumerate(spans):
        result[:, cols] = (near[:, cols] + product(3, context, cols)).astype(BF)
        piece = local(result.at[:, cols], out.at[0, :, cols], RS + n)
        piece.start()
        leaving.append(piece)

    for i in range(4):
        to_sibling(i).wait_send()
    drain(co, CS)
    for piece in leaving:
        piece.wait()


SCRATCH = [
    pltpu.VMEM((ROWS, D), BF),
    pltpu.VMEM((1, ROWS), jnp.int32),
    pltpu.VMEM((1, 32), jnp.int32),
    pltpu.VMEM((D,), F32),
    pltpu.VMEM((4, ROWS, D), BF),
    pltpu.VMEM((2, D, 384), BF),
    pltpu.VMEM((2, 4, 128, D), BF),
    pltpu.VMEM((4, 12, HALF, 128), BF),
    pltpu.VMEM((4, 1, 128), F32),
    pltpu.VMEM((3, 2, 512, 128), BF),
    pltpu.VMEM((2, 16, 1, 128), F32),
    pltpu.VMEM((2, 512, 128), BF),
    pltpu.VMEM((2, 4, 256, 128), BF),
    pltpu.VMEM((2, 1024, 128), BF),
    pltpu.VMEM((512, 128), BF),
    pltpu.VMEM((4, 2, 2, HALF, 128), BF),
    pltpu.VMEM((4, 256, 128), F32),
    pltpu.VMEM((4, 256, 1), F32),
    pltpu.VMEM((4, 256, 1), F32),
    pltpu.VMEM((ROWS, D), F32),
    pltpu.VMEM((ROWS, D), BF),
    pltpu.SemaphoreType.DMA((NSEM,)),
    pltpu.SemaphoreType.REGULAR,
    pltpu.SemaphoreType.REGULAR,
    pltpu.SemaphoreType.REGULAR,
]


def shards(frames, destination, plan, norm_gain, w_qkv, w_out):
    any_space = pl.BlockSpec(memory_space=pl.ANY)
    return pl.pallas_call(
        kernel,
        out_shape=jax.ShapeDtypeStruct((1, ROWS, D), BF),
        in_specs=[any_space] * 6,
        out_specs=any_space,
        scratch_shapes=SCRATCH,
        compiler_params=pltpu.CompilerParams(
            collective_id=0, has_side_effects=True, vmem_limit_bytes=60 * 2**20
        ),
        name="attend",
    )(frames, destination.reshape(1, ROWS), plan, norm_gain, w_qkv, w_out)


def solution(mesh):
    in_specs = (
        P("rep", "grp", None),
        P("rep", "grp", None),
        P("rep", None),
        P(),
        P(None, "rep"),
        P("rep", None),
    )
    out_specs = P("rep", "grp", None)
    return jax.shard_map(shards, mesh=mesh, in_specs=in_specs, out_specs=out_specs, check_vma=False)
```

```python
import math

import jax
import jax.numpy as jnp
from jax import lax
from jax.experimental import pallas as pl
from jax.experimental.pallas import tpu as pltpu
from jax.sharding import PartitionSpec as P

MESH = pl.DeviceIdType.MESH
NT = (((1,), (1,)), ((), ()))
BF = jnp.bfloat16
F32 = jnp.float32
D = 1280
ROWS = 64
HALF = 32
FR, DE, PL, GA, WL, WOL = 0, 1, 2, 3, 4, 5
XS, XR = 6, 12
WS, WR = 18, 19
OS, OR = 20, 24
QS, QV = 28, 32
FS, FT = 36, 40
SBS = 44
QR = 45
GS, GR = 48, 49
PS, PR = 50, 53
CS, CR = 56, 57
RS = 59
GX, GY = 64, 68
NSEM = 72


def halves(block):
    return jnp.concatenate([block[:, 64:], block[:, :64]], axis=1)


def kernel(
    frames, dest, plan, gain, w_qkv, w_out, out,
    raw, dest_v, plan_v, gain_v, xb, w, wo, sb, line_g, rb, gb, key_mark, query_mark, vd, co, cb, acc, top_v,
    sum_v, near, result, sem, line_x, line_y, line_z,
):
    g = lax.axis_index("grp")
    r = lax.axis_index("rep")
    x, z = lax.div(g, 8), lax.rem(g, 8)
    y, c = lax.div(r, 2), lax.rem(r, 2)
    cls = lax.rem(z, 2)
    slot = lax.div(z, 2) * 4 + x

    def at(tx, ty, tz, tc):
        return (tx * 8 + tz, ty * 2 + tc)

    def turn_x(i):
        return lax.rem(x + i, 4)

    def along_x(i):
        return at(turn_x(i), y, z, c)

    def along_y(i):
        return at(x, lax.rem(y + i, 4), z, c)

    def along_z(i):
        return at(x, y, lax.rem(z + i, 8), c)

    sibling = at(x, y, z, 1 - c)

    def remote(src, dst, ssem, rsem, target):
        return pltpu.make_async_remote_copy(
            src_ref=src, dst_ref=dst, send_sem=sem.at[ssem], recv_sem=sem.at[rsem],
            device_id=target, device_id_type=MESH,
        )

    def local(src, dst, s):
        return pltpu.make_async_copy(src, dst, sem.at[s])

    def push(src, dst, ssem, rsem, tx, ty, tz, tc):
        remote(src, dst, ssem, rsem, at(tx, ty, tz, tc)).start()

    def plane_of(i):
        return lax.rem(2 * lax.rem(y + i, 4) + 5 * (1 - c), 8)

    def drain(ref, s):
        local(ref, ref, s).wait()

    loads = [
        local(frames.at[0], raw, FR),
        local(dest, dest_v, DE),
        local(plan, plan_v, PL),
        local(gain, gain_v, GA),
        local(w_qkv, w.at[c], WL),
        local(w_out, wo.at[c, y], WOL),
    ]
    for load in loads:
        load.start()

    barrier = pltpu.get_barrier_semaphore()
    plane = [at(turn_x(i), y, z, c) for i in (1, 2, 3)]
    plane += [at(turn_x(i), y, z, 1 - c) for i in range(4)]
    partners = [along_y(i) for i in (1, 2, 3)] + plane
    partners += [along_z(i) for i in (1, 2, 6, 7)]
    for partner in partners:
        pl.semaphore_signal(barrier, inc=1, device_id=partner, device_id_type=MESH)

    low = lax.broadcasted_iota(jnp.int32, (1, 128), 1) < 64
    loads[0].wait()
    loads[3].wait()
    values = raw[...].astype(F32)
    mean = jnp.mean(values, axis=1, keepdims=True)
    centered = values - mean
    variance = jnp.mean(centered * centered, axis=1, keepdims=True)
    xb[0] = (centered * lax.rsqrt(variance + 1e-05) * gain_v[...][None, :]).astype(BF)

    pl.semaphore_wait(barrier, len(partners))

    upper, lower = pl.ds(0, HALF), pl.ds(HALF, HALF)

    def row_copy(n):
        block, to, part, source = (
            (1, 3, upper, 0), (2, 1, lower, 0), (1, 3, lower, 0), (2, 1, upper, 0),
            (3, 3, upper, 1), (3, 1, lower, 2),
        )[n]
        return remote(xb.at[source, part], xb.at[block, part], XS + n, XR + n, along_y(to))

    for i in (2, 6):
        pl.semaphore_signal(line_z, inc=1, device_id=along_z(i), device_id_type=MESH)
    for n in range(4):
        row_copy(n).start()
    remote(w_qkv, w.at[c], WS, WR, sibling).start()

    loads[1].wait()
    loads[2].wait()
    row32 = lax.broadcasted_iota(jnp.int32, (32, 32), 0)
    col32 = lax.broadcasted_iota(jnp.int32, (32, 32), 1)
    plan_rows = jnp.sum(
        jnp.where(row32 == col32, plan_v[...].astype(F32), 0.0), axis=1, keepdims=True
    )
    hot = dest_v[...] == lax.broadcasted_iota(jnp.int32, (32, ROWS), 0)
    group = jnp.sum(jnp.where(hot, plan_rows, 0.0), axis=0, keepdims=True)
    line_g[0] = jnp.concatenate([group, group], axis=1)

    def group_copy(i):
        return remote(line_g.at[0], line_g.at[i], GX + i, GY + i, along_y(4 - i))

    for i in (2, 1, 3):
        group_copy(i).start()

    along = (0, 1, 3, 2)

    def project(start, count, s):
        rows = xb[start : start + count].reshape(count * ROWS, D)
        part = jnp.dot(rows, w[s], preferred_element_type=F32)
        for n in range(count):
            for p in range(3):
                two = part[n * ROWS : (n + 1) * ROWS, 128 * p : 128 * p + 128]
                first, last = two[:HALF], two[HALF:]
                spot = 6 * s + 2 * p
                sb[start + n, spot] = jnp.where(low, first, halves(last)).astype(BF)
                sb[start + n, spot + 1] = jnp.where(low, halves(first), last).astype(BF)

    def scatter(i, blocks):
        tz = plane_of(along[i])
        for s in blocks:
            sub = 3 * y + s
            kind, block = lax.div(sub, 4), lax.rem(sub, 4)
            ty = block + 1 - 2 * lax.rem(block, 2)
            for k in (2, 1, 3, 0):
                push(
                    sb.at[i, 4 * s + turn_x(k)], rb.at[kind, cls, pl.ds(slot * HALF, HALF)],
                    SBS, QR + kind, turn_x(k), ty, tz, cls,
                )

    loads[4].wait()
    project(0, 1, c)
    pl.semaphore_wait(line_z, 2)
    for partner in plane:
        pl.semaphore_signal(line_x, inc=1, device_id=partner, device_id_type=MESH)
    pl.semaphore_wait(line_x, len(plane))
    for i in (1, 2, 3):
        pl.semaphore_signal(line_y, inc=1, device_id=along_y(i), device_id_type=MESH)
    for n in (0, 1):
        row_copy(n).wait_recv()
        row_copy(4 + n).start()
    for i in (0, 1, 3, 2):
        if i:
            group_copy(i).wait_recv()
        tz = plane_of(i)
        for k in (2, 1, 3, 0):
            push(line_g.at[i], gb.at[cls, slot], GS, GR, turn_x(k), y, tz, cls)
    remote(w_qkv, w.at[1 - c], WS, WR, sibling).wait_recv()
    project(0, 1, 1 - c)
    scatter(0, (1,))
    pl.semaphore_wait(line_y, 3)
    scatter(0, (0, 2))
    for n in (2, 3):
        row_copy(n).wait_recv()
    for s in range(2):
        project(1, 2, s)
    scatter(1, (0, 2, 1))
    scatter(2, (0, 2, 1))
    for n in (4, 5):
        row_copy(n).wait_recv()
    for s in range(2):
        project(3, 1, s)
    scatter(3, (0, 2, 1))
    loads[5].wait()
    opposite = lax.rem(y + 2, 4)

    def quarter(ty, tx):
        return wo.at[c, ty, pl.ds(pl.multiple_of(tx * HALF, HALF), HALF)]

    def shard_copy(i):
        ref = quarter(y, x) if i == 2 else wo.at[c, y]
        return remote(ref, ref, OS + i, OR + i, along_y(4 - i))

    def quarter_copy(i):
        ref = quarter(opposite, x)
        return remote(ref, ref, QS + i, QV + i, along_x(i))

    for i in (2, 1, 3):
        shard_copy(i).start()

    def to_sibling(i):
        ty = lax.rem(y + i, 4)
        return remote(wo.at[c, ty], wo.at[c, ty], FS + i, FT + i, sibling)

    to_sibling(0).start()

    mine = [rb.at[1, c], rb.at[2, c], gb.at[c]]
    theirs = [rb.at[1, 1 - c], rb.at[2, 1 - c], gb.at[1 - c]]

    def swap(n, s):
        drain(mine[n], s)
        remote(mine[n], mine[n], PS + n, PR + n, sibling).start()

    lane = lax.broadcasted_iota(jnp.int32, (1, 128), 1)
    lane_group = jnp.where(lane < 64, lax.rem(lax.div(lane, 4), 8), -1).astype(F32)
    row = lax.rem(lax.broadcasted_iota(jnp.int32, (128, 128), 0), HALF)
    col = lax.broadcasted_iota(jnp.int32, (128, 128), 1)

    def group_columns(half, m):
        table = jnp.concatenate(
            [jnp.broadcast_to(gb[half, 4 * m + n], (HALF, 128)) for n in range(4)], axis=0
        )
        return [
            jnp.sum(jnp.where(col == row + base, table, 0.0), axis=1, keepdims=True)
            for base in (0, HALF)
        ]

    def mark_keys(half, m):
        for_low, for_high = group_columns(half, m)
        hit = jnp.where(lane < 32, for_low, for_high) == lane_group
        key_mark[half, 128 * m : 128 * m + 128, :] = jnp.where(hit, 1.0, 0.0).astype(BF)
        if half is not c:
            return
        group = jnp.concatenate([for_low, for_high], axis=0)
        miss = jnp.where(group == lane_group, 0.0, -(2.0**127))
        query_mark[0, m] = jnp.where(lane < 32, miss, 0.0).astype(BF)
        query_mark[1, m] = jnp.where((lane >= 32) & (lane < 64), miss, 0.0).astype(BF)

    swap(2, GR)
    for m in range(4):
        mark_keys(c, m)
    drain(theirs[2], PR + 2)
    for m in range(4):
        mark_keys(1 - c, m)
    swap(0, QR + 1)
    swap(1, QR + 2)
    drain(rb.at[0, c], QR)
    shard_copy(2).wait_recv()
    for i in (1, 2, 3):
        quarter_copy(i).start()

    def spread_values(half):
        vals = rb[2, half]
        turned = halves(vals)
        vd[half, 0:512, :] = jnp.where(low, vals, turned)
        vd[half, 512:1024, :] = jnp.where(low, turned, vals)

    owner_y, owner_c = lax.div(lax.rem(z + 3 * lax.rem(z, 2), 8), 2), 1 - lax.rem(z, 2)
    away = lax.rem(y + 4 - owner_y, 4)
    place = away + lax.div(away, 2) * (5 - 2 * away)
    scale = 0.125 * math.log2(math.e)

    def scores(m, half):
        q = rb[0, c, 128 * m : 128 * m + 128, :]
        turned = halves(q)
        none = jnp.zeros_like(q)
        q_low = jnp.concatenate([jnp.where(low, q, none), jnp.where(low, turned, none)], axis=0)
        q_high = jnp.concatenate([jnp.where(low, none, turned), jnp.where(low, none, q)], axis=0)
        keys = jnp.concatenate([rb[1, half], key_mark[half]], axis=1)
        both = [
            lax.dot_general(
                jnp.concatenate([part, query_mark[n, m]], axis=1), keys, NT,
                preferred_element_type=F32,
            )
            for n, part in enumerate((q_low, q_high))
        ]
        top = jnp.maximum(
            jnp.max(both[0], axis=1, keepdims=True), jnp.max(both[1], axis=1, keepdims=True)
        )
        return both[0], both[1], top

    def weigh(s_low, s_high, top, half):
        p_low = jnp.exp2((s_low - top) * scale)
        p_high = jnp.exp2((s_high - top) * scale)
        total = jnp.sum(p_low, axis=1, keepdims=True) + jnp.sum(p_high, axis=1, keepdims=True)
        mixed = jnp.dot(p_low.astype(BF), vd[half, 0:512, :], preferred_element_type=F32)
        mixed += jnp.dot(p_high.astype(BF), vd[half, 512:1024, :], preferred_element_type=F32)
        return total, mixed

    def first_part(m):
        s_low, s_high, top = scores(m, c)
        total, mixed = weigh(s_low, s_high, top, c)
        top_v[m] = top
        sum_v[m] = total
        acc[m] = mixed

    def second_part(m):
        s_low, s_high, top = scores(m, 1 - c)
        before = top_v[m]
        top = jnp.maximum(before, top)
        total, mixed = weigh(s_low, s_high, top, 1 - c)
        factor = jnp.exp2((before - top) * scale)
        context = (acc[m] * factor + mixed) / (sum_v[m] * factor + total)
        co[128 * m : 128 * m + 128, :] = jnp.where(low, context[:128], context[128:]).astype(BF)
        for k in (2, 1, 3, 0):
            push(
                co.at[pl.ds(128 * m + HALF * turn_x(k), HALF)],
                cb.at[place, lax.div(x, 2), lax.rem(x, 2)],
                CS, CR + lax.div(place, 3), turn_x(k), owner_y, 2 * m + c, owner_c,
            )

    spread_values(c)
    for m in range(3):
        first_part(m)
    drain(theirs[0], PR)
    drain(theirs[1], PR + 1)
    spread_values(1 - c)
    for m in range(3):
        second_part(m)
    first_part(3)
    second_part(3)

    for i in (1, 3, 2):
        if i == 2:
            for k in (1, 2, 3):
                quarter_copy(k).wait_recv()
        else:
            shard_copy(i).wait_recv()
        to_sibling(i).start()

    for n in range(6):
        row_copy(n).wait_send()
    for i in (1, 2, 3):
        shard_copy(i).wait_send()
        quarter_copy(i).wait_send()
    remote(w_qkv, w.at[c], WS, WR, sibling).wait_send()
    drain(sb, SBS)
    for n in range(3):
        remote(mine[n], mine[n], PS + n, PR + n, sibling).wait_send()
    drain(gb.at[c], GS)
    for i in (1, 2, 3):
        group_copy(i).wait_send()

    def gathered(p):
        both = []
        for tc in range(2):
            even, odd = cb[p, tc, 0], cb[p, tc, 1]
            both.append(
                jnp.concatenate(
                    [jnp.where(low, even, halves(odd)), jnp.where(low, halves(even), odd)], axis=0
                )
            )
        return jnp.concatenate(both, axis=1)

    def product(p, context, cols):
        ty = lax.rem(y + (0, 1, 3, 2)[p], 4)
        ty = ty + 1 - 2 * lax.rem(ty, 2)
        weights = wo[:, ty, :, cols].reshape(256, 256)
        return jnp.dot(context, weights, preferred_element_type=F32)

    drain(cb.at[pl.ds(0, 3)], CR)
    for i in range(4):
        ty = lax.rem(y + i, 4)
        remote(wo.at[c, ty], wo.at[1 - c, ty], FS + i, FT + i, sibling).wait_recv()
    contexts = [gathered(p) for p in range(3)]
    spans = [slice(256 * n, 256 * n + 256) for n in range(5)]
    for cols in spans:
        near[:, cols] = sum(product(p, contexts[p], cols) for p in range(3))
    drain(cb.at[3], CR + 1)
    context = gathered(3)
    leaving = []
    for n, cols in enumerate(spans):
        result[:, cols] = (near[:, cols] + product(3, context, cols)).astype(BF)
        piece = local(result.at[:, cols], out.at[0, :, cols], RS + n)
        piece.start()
        leaving.append(piece)

    for i in range(4):
        to_sibling(i).wait_send()
    drain(co, CS)
    for piece in leaving:
        piece.wait()


SCRATCH = [
    pltpu.VMEM((ROWS, D), BF),
    pltpu.VMEM((1, ROWS), jnp.int32),
    pltpu.VMEM((1, 32), jnp.int32),
    pltpu.VMEM((D,), F32),
    pltpu.VMEM((4, ROWS, D), BF),
    pltpu.VMEM((2, D, 384), BF),
    pltpu.VMEM((2, 4, 128, D), BF),
    pltpu.VMEM((4, 12, HALF, 128), BF),
    pltpu.VMEM((4, 1, 128), F32),
    pltpu.VMEM((3, 2, 512, 128), BF),
    pltpu.VMEM((2, 16, 1, 128), F32),
    pltpu.VMEM((2, 512, 128), BF),
    pltpu.VMEM((2, 4, 256, 128), BF),
    pltpu.VMEM((2, 1024, 128), BF),
    pltpu.VMEM((512, 128), BF),
    pltpu.VMEM((4, 2, 2, HALF, 128), BF),
    pltpu.VMEM((4, 256, 128), F32),
    pltpu.VMEM((4, 256, 1), F32),
    pltpu.VMEM((4, 256, 1), F32),
    pltpu.VMEM((ROWS, D), F32),
    pltpu.VMEM((ROWS, D), BF),
    pltpu.SemaphoreType.DMA((NSEM,)),
    pltpu.SemaphoreType.REGULAR,
    pltpu.SemaphoreType.REGULAR,
    pltpu.SemaphoreType.REGULAR,
]


def shards(frames, destination, plan, norm_gain, w_qkv, w_out):
    any_space = pl.BlockSpec(memory_space=pl.ANY)
    return pl.pallas_call(
        kernel,
        out_shape=jax.ShapeDtypeStruct((1, ROWS, D), BF),
        in_specs=[any_space] * 6,
        out_specs=any_space,
        scratch_shapes=SCRATCH,
        compiler_params=pltpu.CompilerParams(
            collective_id=0, has_side_effects=True, vmem_limit_bytes=60 * 2**20
        ),
        name="attend",
    )(frames, destination.reshape(1, ROWS), plan, norm_gain, w_qkv, w_out)


def solution(mesh):
    in_specs = (
        P("rep", "grp", None),
        P("rep", "grp", None),
        P("rep", None),
        P(),
        P(None, "rep"),
        P("rep", None),
    )
    out_specs = P("rep", "grp", None)
    return jax.shard_map(shards, mesh=mesh, in_specs=in_specs, out_specs=out_specs, check_vma=False)
```

```python
import math

import jax
import jax.numpy as jnp
from jax import lax
from jax.experimental import pallas as pl
from jax.experimental.pallas import tpu as pltpu
from jax.sharding import PartitionSpec as P

MESH = pl.DeviceIdType.MESH
NT = (((1,), (1,)), ((), ()))
BF = jnp.bfloat16
F32 = jnp.float32
D = 1280
ROWS = 64
HALF = 32
FR, DE, PL, GA, WL, WOL = 0, 1, 2, 3, 4, 5
XS, XR = 6, 12
WS, WR = 18, 19
OS, OR = 20, 24
QS, QV = 28, 32
FS, FT = 36, 40
SBS = 44
QR = 45
GS, GR = 48, 49
PS, PR = 50, 53
CS, CR = 56, 57
RS = 59
GX, GY = 64, 68
NSEM = 72


def halves(block):
    return jnp.concatenate([block[:, 64:], block[:, :64]], axis=1)


def kernel(
    frames, dest, plan, gain, w_qkv, w_out, out,
    raw, dest_v, plan_v, gain_v, xb, w, wo, sb, line_g, rb, gb, key_mark, query_mark, vd, co, cb, acc, top_v,
    sum_v, near, result, sem, line_x, line_y, line_z,
):
    g = lax.axis_index("grp")
    r = lax.axis_index("rep")
    x, z = lax.div(g, 8), lax.rem(g, 8)
    y, c = lax.div(r, 2), lax.rem(r, 2)
    cls = lax.rem(z, 2)
    slot = lax.div(z, 2) * 4 + x

    def at(tx, ty, tz, tc):
        return (tx * 8 + tz, ty * 2 + tc)

    def turn_x(i):
        return lax.rem(x + i, 4)

    def along_x(i):
        return at(turn_x(i), y, z, c)

    def along_y(i):
        return at(x, lax.rem(y + i, 4), z, c)

    def along_z(i):
        return at(x, y, lax.rem(z + i, 8), c)

    sibling = at(x, y, z, 1 - c)

    def remote(src, dst, ssem, rsem, target):
        return pltpu.make_async_remote_copy(
            src_ref=src, dst_ref=dst, send_sem=sem.at[ssem], recv_sem=sem.at[rsem],
            device_id=target, device_id_type=MESH,
        )

    def local(src, dst, s):
        return pltpu.make_async_copy(src, dst, sem.at[s])

    def push(src, dst, ssem, rsem, tx, ty, tz, tc):
        remote(src, dst, ssem, rsem, at(tx, ty, tz, tc)).start()

    def plane_of(i):
        return lax.rem(2 * lax.rem(y + i, 4) + 1 + 5 * c, 8)

    def drain(ref, s):
        local(ref, ref, s).wait()

    loads = [
        local(frames.at[0], raw, FR),
        local(dest, dest_v, DE),
        local(plan, plan_v, PL),
        local(gain, gain_v, GA),
        local(w_qkv, w.at[c], WL),
        local(w_out, wo.at[c, y], WOL),
    ]
    for load in loads:
        load.start()

    barrier = pltpu.get_barrier_semaphore()
    plane = [at(turn_x(i), y, z, c) for i in (1, 2, 3)]
    plane += [at(turn_x(i), y, z, 1 - c) for i in range(4)]
    partners = [along_y(i) for i in (1, 2, 3)] + plane
    partners += [along_z(i) for i in (1, 2, 6, 7)]
    for partner in partners:
        pl.semaphore_signal(barrier, inc=1, device_id=partner, device_id_type=MESH)

    low = lax.broadcasted_iota(jnp.int32, (1, 128), 1) < 64
    loads[0].wait()
    loads[3].wait()
    values = raw[...].astype(F32)
    mean = jnp.mean(values, axis=1, keepdims=True)
    centered = values - mean
    variance = jnp.mean(centered * centered, axis=1, keepdims=True)
    xb[0] = (centered * lax.rsqrt(variance + 1e-05) * gain_v[...][None, :]).astype(BF)

    pl.semaphore_wait(barrier, len(partners))

    upper, lower = pl.ds(0, HALF), pl.ds(HALF, HALF)

    def row_copy(n):
        block, to, part, source = (
            (1, 3, upper, 0), (2, 1, lower, 0), (1, 3, lower, 0), (2, 1, upper, 0),
            (3, 3, upper, 1), (3, 1, lower, 2),
        )[n]
        return remote(xb.at[source, part], xb.at[block, part], XS + n, XR + n, along_y(to))

    for i in (2, 6):
        pl.semaphore_signal(line_z, inc=1, device_id=along_z(i), device_id_type=MESH)
    for n in range(4):
        row_copy(n).start()
    remote(w_qkv, w.at[c], WS, WR, sibling).start()

    loads[1].wait()
    loads[2].wait()
    row32 = lax.broadcasted_iota(jnp.int32, (32, 32), 0)
    col32 = lax.broadcasted_iota(jnp.int32, (32, 32), 1)
    plan_rows = jnp.sum(
        jnp.where(row32 == col32, plan_v[...].astype(F32), 0.0), axis=1, keepdims=True
    )
    hot = dest_v[...] == lax.broadcasted_iota(jnp.int32, (32, ROWS), 0)
    group = jnp.sum(jnp.where(hot, plan_rows, 0.0), axis=0, keepdims=True)
    line_g[0] = jnp.concatenate([group, group], axis=1)

    def group_copy(i):
        return remote(line_g.at[0], line_g.at[i], GX + i, GY + i, along_y(4 - i))

    for i in (2, 1, 3):
        group_copy(i).start()

    along = (0, 1, 3, 2)

    def project(start, count, s):
        rows = xb[start : start + count].reshape(count * ROWS, D)
        part = jnp.dot(rows, w[s], preferred_element_type=F32)
        for n in range(count):
            for p in range(3):
                two = part[n * ROWS : (n + 1) * ROWS, 128 * p : 128 * p + 128]
                first, last = two[:HALF], two[HALF:]
                spot = 6 * s + 2 * p
                sb[start + n, spot] = jnp.where(low, first, halves(last)).astype(BF)
                sb[start + n, spot + 1] = jnp.where(low, halves(first), last).astype(BF)

    def scatter(i, blocks):
        tz = plane_of(along[i])
        for s in blocks:
            sub = 3 * y + s
            kind, block = lax.div(sub, 4), lax.rem(sub, 4)
            ty = block + 1 - 2 * lax.rem(block, 2)
            for k in (2, 1, 3, 0):
                push(
                    sb.at[i, 4 * s + turn_x(k)], rb.at[kind, cls, pl.ds(slot * HALF, HALF)],
                    SBS, QR + kind, turn_x(k), ty, tz, cls,
                )

    loads[4].wait()
    project(0, 1, c)
    pl.semaphore_wait(line_z, 2)
    for partner in plane:
        pl.semaphore_signal(line_x, inc=1, device_id=partner, device_id_type=MESH)
    pl.semaphore_wait(line_x, len(plane))
    for i in (1, 2, 3):
        pl.semaphore_signal(line_y, inc=1, device_id=along_y(i), device_id_type=MESH)
    for n in (0, 1):
        row_copy(n).wait_recv()
        row_copy(4 + n).start()
    for i in (0, 1, 3, 2):
        if i:
            group_copy(i).wait_recv()
        tz = plane_of(i)
        for k in (2, 1, 3, 0):
            push(line_g.at[i], gb.at[cls, slot], GS, GR, turn_x(k), y, tz, cls)
    remote(w_qkv, w.at[1 - c], WS, WR, sibling).wait_recv()
    project(0, 1, 1 - c)
    scatter(0, (1,))
    pl.semaphore_wait(line_y, 3)
    scatter(0, (0, 2))
    for n in (2, 3):
        row_copy(n).wait_recv()
    for s in range(2):
        project(1, 2, s)
    scatter(1, (0, 2, 1))
    scatter(2, (0, 2, 1))
    for n in (4, 5):
        row_copy(n).wait_recv()
    for s in range(2):
        project(3, 1, s)
    scatter(3, (0, 2, 1))
    loads[5].wait()
    opposite = lax.rem(y + 2, 4)

    def quarter(ty, tx):
        return wo.at[c, ty, pl.ds(pl.multiple_of(tx * HALF, HALF), HALF)]

    def shard_copy(i):
        ref = quarter(y, x) if i == 2 else wo.at[c, y]
        return remote(ref, ref, OS + i, OR + i, along_y(4 - i))

    def quarter_copy(i):
        ref = quarter(opposite, x)
        return remote(ref, ref, QS + i, QV + i, along_x(i))

    for i in (2, 1, 3):
        shard_copy(i).start()

    def to_sibling(i):
        ty = lax.rem(y + i, 4)
        return remote(wo.at[c, ty], wo.at[c, ty], FS + i, FT + i, sibling)

    to_sibling(0).start()

    mine = [rb.at[1, c], rb.at[2, c], gb.at[c]]
    theirs = [rb.at[1, 1 - c], rb.at[2, 1 - c], gb.at[1 - c]]

    def swap(n, s):
        drain(mine[n], s)
        remote(mine[n], mine[n], PS + n, PR + n, sibling).start()

    lane = lax.broadcasted_iota(jnp.int32, (1, 128), 1)
    lane_group = jnp.where(lane < 64, lax.rem(lax.div(lane, 4), 8), -1).astype(F32)
    row = lax.rem(lax.broadcasted_iota(jnp.int32, (128, 128), 0), HALF)
    col = lax.broadcasted_iota(jnp.int32, (128, 128), 1)

    def group_columns(half, m):
        table = jnp.concatenate(
            [jnp.broadcast_to(gb[half, 4 * m + n], (HALF, 128)) for n in range(4)], axis=0
        )
        return [
            jnp.sum(jnp.where(col == row + base, table, 0.0), axis=1, keepdims=True)
            for base in (0, HALF)
        ]

    def mark_keys(half, m):
        for_low, for_high = group_columns(half, m)
        hit = jnp.where(lane < 32, for_low, for_high) == lane_group
        key_mark[half, 128 * m : 128 * m + 128, :] = jnp.where(hit, 1.0, 0.0).astype(BF)
        if half is not c:
            return
        group = jnp.concatenate([for_low, for_high], axis=0)
        miss = jnp.where(group == lane_group, 0.0, -(2.0**127))
        query_mark[0, m] = jnp.where(lane < 32, miss, 0.0).astype(BF)
        query_mark[1, m] = jnp.where((lane >= 32) & (lane < 64), miss, 0.0).astype(BF)

    swap(2, GR)
    for m in range(4):
        mark_keys(c, m)
    drain(theirs[2], PR + 2)
    for m in range(4):
        mark_keys(1 - c, m)
    swap(0, QR + 1)
    swap(1, QR + 2)
    drain(rb.at[0, c], QR)
    shard_copy(2).wait_recv()
    for i in (1, 2, 3):
        quarter_copy(i).start()

    def spread_values(half):
        vals = rb[2, half]
        turned = halves(vals)
        vd[half, 0:512, :] = jnp.where(low, vals, turned)
        vd[half, 512:1024, :] = jnp.where(low, turned, vals)

    owner_c = 1 - lax.rem(z, 2)
    owner_y = lax.div(lax.rem(z + 2 * owner_c, 8), 2)
    away = lax.rem(y + 4 - owner_y, 4)
    place = away + lax.div(away, 2) * (5 - 2 * away)
    scale = 0.125 * math.log2(math.e)

    def scores(m, half):
        q = rb[0, c, 128 * m : 128 * m + 128, :]
        turned = halves(q)
        none = jnp.zeros_like(q)
        q_low = jnp.concatenate([jnp.where(low, q, none), jnp.where(low, turned, none)], axis=0)
        q_high = jnp.concatenate([jnp.where(low, none, turned), jnp.where(low, none, q)], axis=0)
        keys = jnp.concatenate([rb[1, half], key_mark[half]], axis=1)
        both = [
            lax.dot_general(
                jnp.concatenate([part, query_mark[n, m]], axis=1), keys, NT,
                preferred_element_type=F32,
            )
            for n, part in enumerate((q_low, q_high))
        ]
        top = jnp.maximum(
            jnp.max(both[0], axis=1, keepdims=True), jnp.max(both[1], axis=1, keepdims=True)
        )
        return both[0], both[1], top

    def weigh(s_low, s_high, top, half):
        p_low = jnp.exp2((s_low - top) * scale)
        p_high = jnp.exp2((s_high - top) * scale)
        total = jnp.sum(p_low, axis=1, keepdims=True) + jnp.sum(p_high, axis=1, keepdims=True)
        mixed = jnp.dot(p_low.astype(BF), vd[half, 0:512, :], preferred_element_type=F32)
        mixed += jnp.dot(p_high.astype(BF), vd[half, 512:1024, :], preferred_element_type=F32)
        return total, mixed

    def first_part(m):
        s_low, s_high, top = scores(m, c)
        total, mixed = weigh(s_low, s_high, top, c)
        top_v[m] = top
        sum_v[m] = total
        acc[m] = mixed

    def second_part(m):
        s_low, s_high, top = scores(m, 1 - c)
        before = top_v[m]
        top = jnp.maximum(before, top)
        total, mixed = weigh(s_low, s_high, top, 1 - c)
        factor = jnp.exp2((before - top) * scale)
        context = (acc[m] * factor + mixed) / (sum_v[m] * factor + total)
        co[128 * m : 128 * m + 128, :] = jnp.where(low, context[:128], context[128:]).astype(BF)
        for k in (2, 1, 3, 0):
            push(
                co.at[pl.ds(128 * m + HALF * turn_x(k), HALF)],
                cb.at[place, lax.div(x, 2), lax.rem(x, 2)],
                CS, CR + lax.div(place, 3), turn_x(k), owner_y, 2 * m + c, owner_c,
            )

    spread_values(c)
    for m in range(3):
        first_part(m)
    drain(theirs[0], PR)
    drain(theirs[1], PR + 1)
    spread_values(1 - c)
    for m in range(3):
        second_part(m)
    first_part(3)
    second_part(3)

    for i in (1, 3, 2):
        if i == 2:
            for k in (1, 2, 3):
                quarter_copy(k).wait_recv()
        else:
            shard_copy(i).wait_recv()
        to_sibling(i).start()

    for n in range(6):
        row_copy(n).wait_send()
    for i in (1, 2, 3):
        shard_copy(i).wait_send()
        quarter_copy(i).wait_send()
    remote(w_qkv, w.at[c], WS, WR, sibling).wait_send()
    drain(sb, SBS)
    for n in range(3):
        remote(mine[n], mine[n], PS + n, PR + n, sibling).wait_send()
    drain(gb.at[c], GS)
    for i in (1, 2, 3):
        group_copy(i).wait_send()

    def gathered(p):
        both = []
        for tc in range(2):
            even, odd = cb[p, tc, 0], cb[p, tc, 1]
            both.append(
                jnp.concatenate(
                    [jnp.where(low, even, halves(odd)), jnp.where(low, halves(even), odd)], axis=0
                )
            )
        return jnp.concatenate(both, axis=1)

    def product(p, context, cols):
        ty = lax.rem(y + (0, 1, 3, 2)[p], 4)
        ty = ty + 1 - 2 * lax.rem(ty, 2)
        weights = wo[:, ty, :, cols].reshape(256, 256)
        return jnp.dot(context, weights, preferred_element_type=F32)

    drain(cb.at[pl.ds(0, 3)], CR)
    for i in range(4):
        ty = lax.rem(y + i, 4)
        remote(wo.at[c, ty], wo.at[1 - c, ty], FS + i, FT + i, sibling).wait_recv()
    contexts = [gathered(p) for p in range(3)]
    spans = [slice(256 * n, 256 * n + 256) for n in range(5)]
    for cols in spans:
        near[:, cols] = sum(product(p, contexts[p], cols) for p in range(3))
    drain(cb.at[3], CR + 1)
    context = gathered(3)
    leaving = []
    for n, cols in enumerate(spans):
        result[:, cols] = (near[:, cols] + product(3, context, cols)).astype(BF)
        piece = local(result.at[:, cols], out.at[0, :, cols], RS + n)
        piece.start()
        leaving.append(piece)

    for i in range(4):
        to_sibling(i).wait_send()
    drain(co, CS)
    for piece in leaving:
        piece.wait()


SCRATCH = [
    pltpu.VMEM((ROWS, D), BF),
    pltpu.VMEM((1, ROWS), jnp.int32),
    pltpu.VMEM((1, 32), jnp.int32),
    pltpu.VMEM((D,), F32),
    pltpu.VMEM((4, ROWS, D), BF),
    pltpu.VMEM((2, D, 384), BF),
    pltpu.VMEM((2, 4, 128, D), BF),
    pltpu.VMEM((4, 12, HALF, 128), BF),
    pltpu.VMEM((4, 1, 128), F32),
    pltpu.VMEM((3, 2, 512, 128), BF),
    pltpu.VMEM((2, 16, 1, 128), F32),
    pltpu.VMEM((2, 512, 128), BF),
    pltpu.VMEM((2, 4, 256, 128), BF),
    pltpu.VMEM((2, 1024, 128), BF),
    pltpu.VMEM((512, 128), BF),
    pltpu.VMEM((4, 2, 2, HALF, 128), BF),
    pltpu.VMEM((4, 256, 128), F32),
    pltpu.VMEM((4, 256, 1), F32),
    pltpu.VMEM((4, 256, 1), F32),
    pltpu.VMEM((ROWS, D), F32),
    pltpu.VMEM((ROWS, D), BF),
    pltpu.SemaphoreType.DMA((NSEM,)),
    pltpu.SemaphoreType.REGULAR,
    pltpu.SemaphoreType.REGULAR,
    pltpu.SemaphoreType.REGULAR,
]


def shards(frames, destination, plan, norm_gain, w_qkv, w_out):
    any_space = pl.BlockSpec(memory_space=pl.ANY)
    return pl.pallas_call(
        kernel,
        out_shape=jax.ShapeDtypeStruct((1, ROWS, D), BF),
        in_specs=[any_space] * 6,
        out_specs=any_space,
        scratch_shapes=SCRATCH,
        compiler_params=pltpu.CompilerParams(
            collective_id=0, has_side_effects=True, vmem_limit_bytes=60 * 2**20
        ),
        name="attend",
    )(frames, destination.reshape(1, ROWS), plan, norm_gain, w_qkv, w_out)


def solution(mesh):
    in_specs = (
        P("rep", "grp", None),
        P("rep", "grp", None),
        P("rep", None),
        P(),
        P(None, "rep"),
        P("rep", None),
    )
    out_specs = P("rep", "grp", None)
    return jax.shard_map(shards, mesh=mesh, in_specs=in_specs, out_specs=out_specs, check_vma=False)
```

```python
import math

import jax
import jax.numpy as jnp
from jax import lax
from jax.experimental import pallas as pl
from jax.experimental.pallas import tpu as pltpu
from jax.sharding import PartitionSpec as P

MESH = pl.DeviceIdType.MESH
NT = (((1,), (1,)), ((), ()))
BF = jnp.bfloat16
F32 = jnp.float32
D = 1280
ROWS = 64
HALF = 32
FR, DE, PL, GA, WL, WOL = 0, 1, 2, 3, 4, 5
XS, XR = 6, 12
WS, WR = 18, 19
OS, OR = 20, 24
QS, QV = 28, 32
FS, FT = 36, 40
SBS = 44
QR = 45
GS, GR = 48, 49
PS, PR = 50, 53
CS, CR = 56, 57
RS = 59
GX, GY = 64, 68
NSEM = 72


def halves(block):
    return jnp.concatenate([block[:, 64:], block[:, :64]], axis=1)


def kernel(
    frames, dest, plan, gain, w_qkv, w_out, out,
    raw, dest_v, plan_v, gain_v, xb, w, wo, sb, line_g, rb, gb, key_mark, query_mark, vd, co, cb, acc, top_v,
    sum_v, near, result, sem, line_x, line_y, line_z,
):
    g = lax.axis_index("grp")
    r = lax.axis_index("rep")
    x, z = lax.div(g, 8), lax.rem(g, 8)
    y, c = lax.div(r, 2), lax.rem(r, 2)
    cls = lax.rem(z, 2)
    slot = lax.div(z, 2) * 4 + x

    def at(tx, ty, tz, tc):
        return (tx * 8 + tz, ty * 2 + tc)

    def turn_x(i):
        return lax.rem(x + i, 4)

    def along_x(i):
        return at(turn_x(i), y, z, c)

    def along_y(i):
        return at(x, lax.rem(y + i, 4), z, c)

    def along_z(i):
        return at(x, y, lax.rem(z + i, 8), c)

    sibling = at(x, y, z, 1 - c)

    def remote(src, dst, ssem, rsem, target):
        return pltpu.make_async_remote_copy(
            src_ref=src, dst_ref=dst, send_sem=sem.at[ssem], recv_sem=sem.at[rsem],
            device_id=target, device_id_type=MESH,
        )

    def local(src, dst, s):
        return pltpu.make_async_copy(src, dst, sem.at[s])

    def push(src, dst, ssem, rsem, tx, ty, tz, tc):
        remote(src, dst, ssem, rsem, at(tx, ty, tz, tc)).start()

    def plane_of(i):
        return lax.rem(2 * lax.rem(y + i, 4) + 1 + 5 * c, 8)

    def drain(ref, s):
        local(ref, ref, s).wait()

    loads = [
        local(frames.at[0], raw, FR),
        local(dest, dest_v, DE),
        local(plan, plan_v, PL),
        local(gain, gain_v, GA),
        local(w_qkv, w.at[c], WL),
        local(w_out, wo.at[c, y], WOL),
    ]
    for load in loads:
        load.start()

    barrier = pltpu.get_barrier_semaphore()
    plane = [at(turn_x(i), y, z, c) for i in (1, 2, 3)]
    plane += [at(turn_x(i), y, z, 1 - c) for i in range(4)]
    partners = [along_y(i) for i in (1, 2, 3)] + plane
    partners += [along_z(i) for i in (1, 2, 6, 7)]
    for partner in partners:
        pl.semaphore_signal(barrier, inc=1, device_id=partner, device_id_type=MESH)

    low = lax.broadcasted_iota(jnp.int32, (1, 128), 1) < 64
    loads[0].wait()
    loads[3].wait()
    values = raw[...].astype(F32)
    mean = jnp.mean(values, axis=1, keepdims=True)
    centered = values - mean
    variance = jnp.mean(centered * centered, axis=1, keepdims=True)
    xb[0] = (centered * lax.rsqrt(variance + 1e-05) * gain_v[...][None, :]).astype(BF)

    pl.semaphore_wait(barrier, len(partners))

    upper, lower = pl.ds(0, HALF), pl.ds(HALF, HALF)

    def row_copy(n):
        block, to, part, source = (
            (1, 3, upper, 0), (2, 1, lower, 0), (1, 3, lower, 0), (2, 1, upper, 0),
            (3, 3, upper, 1), (3, 1, lower, 2),
        )[n]
        return remote(xb.at[source, part], xb.at[block, part], XS + n, XR + n, along_y(to))

    for i in (2, 6):
        pl.semaphore_signal(line_z, inc=1, device_id=along_z(i), device_id_type=MESH)
    for n in range(4):
        row_copy(n).start()
    remote(w_qkv, w.at[c], WS, WR, sibling).start()

    loads[1].wait()
    loads[2].wait()
    row32 = lax.broadcasted_iota(jnp.int32, (32, 32), 0)
    col32 = lax.broadcasted_iota(jnp.int32, (32, 32), 1)
    plan_rows = jnp.sum(
        jnp.where(row32 == col32, plan_v[...].astype(F32), 0.0), axis=1, keepdims=True
    )
    hot = dest_v[...] == lax.broadcasted_iota(jnp.int32, (32, ROWS), 0)
    group = jnp.sum(jnp.where(hot, plan_rows, 0.0), axis=0, keepdims=True)
    line_g[0] = jnp.concatenate([group, group], axis=1)

    def group_copy(i):
        return remote(line_g.at[0], line_g.at[i], GX + i, GY + i, along_y(4 - i))

    for i in (2, 1, 3):
        group_copy(i).start()

    along = (0, 1, 3, 2)

    def project(start, count, s):
        rows = xb[start : start + count].reshape(count * ROWS, D)
        part = jnp.dot(rows, w[s], preferred_element_type=F32)
        for n in range(count):
            for p in range(3):
                two = part[n * ROWS : (n + 1) * ROWS, 128 * p : 128 * p + 128]
                first, last = two[:HALF], two[HALF:]
                spot = 6 * s + 2 * p
                sb[start + n, spot] = jnp.where(low, first, halves(last)).astype(BF)
                sb[start + n, spot + 1] = jnp.where(low, halves(first), last).astype(BF)

    def scatter(i, blocks):
        tz = plane_of(along[i])
        for s in blocks:
            sub = 3 * y + s
            kind, block = lax.div(sub, 4), lax.rem(sub, 4)
            ty = block + 1 - 2 * lax.rem(block, 2)
            for k in (2, 1, 3, 0):
                push(
                    sb.at[i, 4 * s + turn_x(k)], rb.at[kind, cls, pl.ds(slot * HALF, HALF)],
                    SBS, QR + kind, turn_x(k), ty, tz, cls,
                )

    loads[4].wait()
    project(0, 1, c)
    pl.semaphore_wait(line_z, 2)
    for partner in plane:
        pl.semaphore_signal(line_x, inc=1, device_id=partner, device_id_type=MESH)
    pl.semaphore_wait(line_x, len(plane))
    for i in (1, 2, 3):
        pl.semaphore_signal(line_y, inc=1, device_id=along_y(i), device_id_type=MESH)
    for n in (0, 1):
        row_copy(n).wait_recv()
        row_copy(4 + n).start()
    for i in (0, 1, 3, 2):
        if i:
            group_copy(i).wait_recv()
        tz = plane_of(i)
        for k in (2, 1, 3, 0):
            push(line_g.at[i], gb.at[cls, slot], GS, GR, turn_x(k), y, tz, cls)
    remote(w_qkv, w.at[1 - c], WS, WR, sibling).wait_recv()
    project(0, 1, 1 - c)
    scatter(0, (1,))
    pl.semaphore_wait(line_y, 3)
    scatter(0, (0, 2))
    for n in (2, 3):
        row_copy(n).wait_recv()
    for s in range(2):
        project(1, 2, s)
    scatter(1, (0, 2, 1))
    scatter(2, (0, 2, 1))
    for n in (4, 5):
        row_copy(n).wait_recv()
    for s in range(2):
        project(3, 1, s)
    scatter(3, (0, 2, 1))
    loads[5].wait()
    opposite = lax.rem(y + 2, 4)

    def quarter(ty, tx):
        return wo.at[c, ty, pl.ds(pl.multiple_of(tx * HALF, HALF), HALF)]

    def shard_copy(i):
        ref = quarter(y, x) if i == 2 else wo.at[c, y]
        return remote(ref, ref, OS + i, OR + i, along_y(4 - i))

    def quarter_copy(i):
        ref = quarter(opposite, x)
        return remote(ref, ref, QS + i, QV + i, along_x(i))

    for i in (2, 1, 3):
        shard_copy(i).start()

    def to_sibling(i):
        ty = lax.rem(y + i, 4)
        return remote(wo.at[c, ty], wo.at[c, ty], FS + i, FT + i, sibling)

    to_sibling(0).start()

    mine = [rb.at[1, c], rb.at[2, c], gb.at[c]]
    theirs = [rb.at[1, 1 - c], rb.at[2, 1 - c], gb.at[1 - c]]

    def swap(n, s):
        drain(mine[n], s)
        remote(mine[n], mine[n], PS + n, PR + n, sibling).start()

    lane = lax.broadcasted_iota(jnp.int32, (1, 128), 1)
    lane_group = jnp.where(lane < 64, lax.rem(lax.div(lane, 4), 8), -1).astype(F32)
    row = lax.rem(lax.broadcasted_iota(jnp.int32, (128, 128), 0), HALF)
    col = lax.broadcasted_iota(jnp.int32, (128, 128), 1)

    def group_columns(half, m):
        table = jnp.concatenate(
            [jnp.broadcast_to(gb[half, 4 * m + n], (HALF, 128)) for n in range(4)], axis=0
        )
        return [
            jnp.sum(jnp.where(col == row + base, table, 0.0), axis=1, keepdims=True)
            for base in (0, HALF)
        ]

    def mark_keys(half, m):
        for_low, for_high = group_columns(half, m)
        hit = jnp.where(lane < 32, for_low, for_high) == lane_group
        key_mark[half, 128 * m : 128 * m + 128, :] = jnp.where(hit, 1.0, 0.0).astype(BF)
        if half is not c:
            return
        group = jnp.concatenate([for_low, for_high], axis=0)
        miss = jnp.where(group == lane_group, 0.0, -(2.0**127))
        query_mark[0, m] = jnp.where(lane < 32, miss, 0.0).astype(BF)
        query_mark[1, m] = jnp.where((lane >= 32) & (lane < 64), miss, 0.0).astype(BF)

    swap(2, GR)
    for m in range(4):
        mark_keys(c, m)
    drain(theirs[2], PR + 2)
    for m in range(4):
        mark_keys(1 - c, m)
    swap(0, QR + 1)
    swap(1, QR + 2)
    drain(rb.at[0, c], QR)

    def spread_values(half):
        vals = rb[2, half]
        turned = halves(vals)
        vd[half, 0:512, :] = jnp.where(low, vals, turned)
        vd[half, 512:1024, :] = jnp.where(low, turned, vals)

    owner_c = 1 - lax.rem(z, 2)
    owner_y = lax.div(lax.rem(z + 2 * owner_c, 8), 2)
    away = lax.rem(y + 4 - owner_y, 4)
    place = away + lax.div(away, 2) * (5 - 2 * away)
    scale = 0.125 * math.log2(math.e)

    def scores(m, half):
        q = rb[0, c, 128 * m : 128 * m + 128, :]
        turned = halves(q)
        none = jnp.zeros_like(q)
        q_low = jnp.concatenate([jnp.where(low, q, none), jnp.where(low, turned, none)], axis=0)
        q_high = jnp.concatenate([jnp.where(low, none, turned), jnp.where(low, none, q)], axis=0)
        keys = jnp.concatenate([rb[1, half], key_mark[half]], axis=1)
        both = [
            lax.dot_general(
                jnp.concatenate([part, query_mark[n, m]], axis=1), keys, NT,
                preferred_element_type=F32,
            )
            for n, part in enumerate((q_low, q_high))
        ]
        top = jnp.maximum(
            jnp.max(both[0], axis=1, keepdims=True), jnp.max(both[1], axis=1, keepdims=True)
        )
        return both[0], both[1], top

    def weigh(s_low, s_high, top, half):
        p_low = jnp.exp2((s_low - top) * scale)
        p_high = jnp.exp2((s_high - top) * scale)
        total = jnp.sum(p_low, axis=1, keepdims=True) + jnp.sum(p_high, axis=1, keepdims=True)
        mixed = jnp.dot(p_low.astype(BF), vd[half, 0:512, :], preferred_element_type=F32)
        mixed += jnp.dot(p_high.astype(BF), vd[half, 512:1024, :], preferred_element_type=F32)
        return total, mixed

    def first_part(m):
        s_low, s_high, top = scores(m, c)
        total, mixed = weigh(s_low, s_high, top, c)
        top_v[m] = top
        sum_v[m] = total
        acc[m] = mixed

    def second_part(m):
        s_low, s_high, top = scores(m, 1 - c)
        before = top_v[m]
        top = jnp.maximum(before, top)
        total, mixed = weigh(s_low, s_high, top, 1 - c)
        factor = jnp.exp2((before - top) * scale)
        context = (acc[m] * factor + mixed) / (sum_v[m] * factor + total)
        co[128 * m : 128 * m + 128, :] = jnp.where(low, context[:128], context[128:]).astype(BF)
        for k in (2, 1, 3, 0):
            push(
                co.at[pl.ds(128 * m + HALF * turn_x(k), HALF)],
                cb.at[place, lax.div(x, 2), lax.rem(x, 2)],
                CS, CR + lax.div(place, 3), turn_x(k), owner_y, 2 * m + c, owner_c,
            )

    spread_values(c)
    for m in range(4):
        first_part(m)
    drain(theirs[0], PR)
    drain(theirs[1], PR + 1)
    spread_values(1 - c)
    for m in range(4):
        second_part(m)
        if m == 1:
            shard_copy(2).wait_recv()
            for i in (1, 2, 3):
                quarter_copy(i).start()

    for i in (1, 3, 2):
        if i == 2:
            for k in (1, 2, 3):
                quarter_copy(k).wait_recv()
        else:
            shard_copy(i).wait_recv()
        to_sibling(i).start()

    for n in range(6):
        row_copy(n).wait_send()
    for i in (1, 2, 3):
        shard_copy(i).wait_send()
        quarter_copy(i).wait_send()
    remote(w_qkv, w.at[c], WS, WR, sibling).wait_send()
    drain(sb, SBS)
    for n in range(3):
        remote(mine[n], mine[n], PS + n, PR + n, sibling).wait_send()
    drain(gb.at[c], GS)
    for i in (1, 2, 3):
        group_copy(i).wait_send()

    def gathered(p):
        both = []
        for tc in range(2):
            even, odd = cb[p, tc, 0], cb[p, tc, 1]
            both.append(
                jnp.concatenate(
                    [jnp.where(low, even, halves(odd)), jnp.where(low, halves(even), odd)], axis=0
                )
            )
        return jnp.concatenate(both, axis=1)

    def product(p, context, cols):
        ty = lax.rem(y + (0, 1, 3, 2)[p], 4)
        ty = ty + 1 - 2 * lax.rem(ty, 2)
        weights = wo[:, ty, :, cols].reshape(256, 256)
        return jnp.dot(context, weights, preferred_element_type=F32)

    drain(cb.at[pl.ds(0, 3)], CR)
    for i in range(4):
        ty = lax.rem(y + i, 4)
        remote(wo.at[c, ty], wo.at[1 - c, ty], FS + i, FT + i, sibling).wait_recv()
    contexts = [gathered(p) for p in range(3)]
    spans = [slice(256 * n, 256 * n + 256) for n in range(5)]
    for cols in spans:
        near[:, cols] = sum(product(p, contexts[p], cols) for p in range(3))
    drain(cb.at[3], CR + 1)
    context = gathered(3)
    leaving = []
    for n, cols in enumerate(spans):
        result[:, cols] = (near[:, cols] + product(3, context, cols)).astype(BF)
        piece = local(result.at[:, cols], out.at[0, :, cols], RS + n)
        piece.start()
        leaving.append(piece)

    for i in range(4):
        to_sibling(i).wait_send()
    drain(co, CS)
    for piece in leaving:
        piece.wait()


SCRATCH = [
    pltpu.VMEM((ROWS, D), BF),
    pltpu.VMEM((1, ROWS), jnp.int32),
    pltpu.VMEM((1, 32), jnp.int32),
    pltpu.VMEM((D,), F32),
    pltpu.VMEM((4, ROWS, D), BF),
    pltpu.VMEM((2, D, 384), BF),
    pltpu.VMEM((2, 4, 128, D), BF),
    pltpu.VMEM((4, 12, HALF, 128), BF),
    pltpu.VMEM((4, 1, 128), F32),
    pltpu.VMEM((3, 2, 512, 128), BF),
    pltpu.VMEM((2, 16, 1, 128), F32),
    pltpu.VMEM((2, 512, 128), BF),
    pltpu.VMEM((2, 4, 256, 128), BF),
    pltpu.VMEM((2, 1024, 128), BF),
    pltpu.VMEM((512, 128), BF),
    pltpu.VMEM((4, 2, 2, HALF, 128), BF),
    pltpu.VMEM((4, 256, 128), F32),
    pltpu.VMEM((4, 256, 1), F32),
    pltpu.VMEM((4, 256, 1), F32),
    pltpu.VMEM((ROWS, D), F32),
    pltpu.VMEM((ROWS, D), BF),
    pltpu.SemaphoreType.DMA((NSEM,)),
    pltpu.SemaphoreType.REGULAR,
    pltpu.SemaphoreType.REGULAR,
    pltpu.SemaphoreType.REGULAR,
]


def shards(frames, destination, plan, norm_gain, w_qkv, w_out):
    any_space = pl.BlockSpec(memory_space=pl.ANY)
    return pl.pallas_call(
        kernel,
        out_shape=jax.ShapeDtypeStruct((1, ROWS, D), BF),
        in_specs=[any_space] * 6,
        out_specs=any_space,
        scratch_shapes=SCRATCH,
        compiler_params=pltpu.CompilerParams(
            collective_id=0, has_side_effects=True, vmem_limit_bytes=60 * 2**20
        ),
        name="attend",
    )(frames, destination.reshape(1, ROWS), plan, norm_gain, w_qkv, w_out)


def solution(mesh):
    in_specs = (
        P("rep", "grp", None),
        P("rep", "grp", None),
        P("rep", None),
        P(),
        P(None, "rep"),
        P("rep", None),
    )
    out_specs = P("rep", "grp", None)
    return jax.shard_map(shards, mesh=mesh, in_specs=in_specs, out_specs=out_specs, check_vma=False)
```

```python
import math

import jax
import jax.numpy as jnp
from jax import lax
from jax.experimental import pallas as pl
from jax.experimental.pallas import tpu as pltpu
from jax.sharding import PartitionSpec as P

MESH = pl.DeviceIdType.MESH
NT = (((1,), (1,)), ((), ()))
BF = jnp.bfloat16
F32 = jnp.float32
D = 1280
ROWS = 64
HALF = 32
FR, DE, PL, GA, WL, WOL = 0, 1, 2, 3, 4, 5
XS, XR = 6, 12
WS, WR = 18, 19
OS, OR = 20, 24
QS, QV = 28, 32
FS, FT = 36, 40
SBS = 44
QR = 45
GS, GR = 48, 49
PS, PR = 50, 53
CS, CR = 56, 57
RS = 59
GX, GY = 64, 68
NSEM = 72


def halves(block):
    return jnp.concatenate([block[:, 64:], block[:, :64]], axis=1)


def kernel(
    frames, dest, plan, gain, w_qkv, w_out, out,
    raw, dest_v, plan_v, gain_v, xb, w, wo, sb, line_g, rb, gb, key_mark, query_mark, vd, co, cb, acc, top_v,
    sum_v, near, result, sem, line_x, line_y, line_z,
):
    g = lax.axis_index("grp")
    r = lax.axis_index("rep")
    x, z = lax.div(g, 8), lax.rem(g, 8)
    y, c = lax.div(r, 2), lax.rem(r, 2)
    cls = lax.rem(z, 2)
    slot = lax.div(z, 2) * 4 + x

    def at(tx, ty, tz, tc):
        return (tx * 8 + tz, ty * 2 + tc)

    def turn_x(i):
        return lax.rem(x + i, 4)

    def along_x(i):
        return at(turn_x(i), y, z, c)

    def along_y(i):
        return at(x, lax.rem(y + i, 4), z, c)

    def along_z(i):
        return at(x, y, lax.rem(z + i, 8), c)

    sibling = at(x, y, z, 1 - c)

    def remote(src, dst, ssem, rsem, target):
        return pltpu.make_async_remote_copy(
            src_ref=src, dst_ref=dst, send_sem=sem.at[ssem], recv_sem=sem.at[rsem],
            device_id=target, device_id_type=MESH,
        )

    def local(src, dst, s):
        return pltpu.make_async_copy(src, dst, sem.at[s])

    def push(src, dst, ssem, rsem, tx, ty, tz, tc):
        remote(src, dst, ssem, rsem, at(tx, ty, tz, tc)).start()

    def plane_of(i):
        return lax.rem(2 * lax.rem(y + i, 4) + 1 + 5 * c, 8)

    def drain(ref, s):
        local(ref, ref, s).wait()

    loads = [
        local(frames.at[0], raw, FR),
        local(dest, dest_v, DE),
        local(plan, plan_v, PL),
        local(gain, gain_v, GA),
        local(w_qkv, w.at[c], WL),
        local(w_out, wo.at[c, y], WOL),
    ]
    for load in loads:
        load.start()

    barrier = pltpu.get_barrier_semaphore()
    plane = [at(turn_x(i), y, z, c) for i in (1, 2, 3)]
    plane += [at(turn_x(i), y, z, 1 - c) for i in range(4)]
    partners = [along_y(i) for i in (1, 2, 3)] + plane
    partners += [along_z(i) for i in (1, 2, 6, 7)]
    for partner in partners:
        pl.semaphore_signal(barrier, inc=1, device_id=partner, device_id_type=MESH)

    low = lax.broadcasted_iota(jnp.int32, (1, 128), 1) < 64
    loads[0].wait()
    loads[3].wait()
    values = raw[...].astype(F32)
    mean = jnp.mean(values, axis=1, keepdims=True)
    centered = values - mean
    variance = jnp.mean(centered * centered, axis=1, keepdims=True)
    xb[0] = (centered * lax.rsqrt(variance + 1e-05) * gain_v[...][None, :]).astype(BF)

    pl.semaphore_wait(barrier, len(partners))

    upper, lower = pl.ds(0, HALF), pl.ds(HALF, HALF)

    def row_copy(n):
        block, to, part, source = (
            (1, 3, upper, 0), (2, 1, lower, 0), (1, 3, lower, 0), (2, 1, upper, 0),
            (3, 3, upper, 1), (3, 1, lower, 2),
        )[n]
        return remote(xb.at[source, part], xb.at[block, part], XS + n, XR + n, along_y(to))

    for i in (2, 6):
        pl.semaphore_signal(line_z, inc=1, device_id=along_z(i), device_id_type=MESH)
    for n in range(4):
        row_copy(n).start()
    remote(w_qkv, w.at[c], WS, WR, sibling).start()

    loads[1].wait()
    loads[2].wait()
    row32 = lax.broadcasted_iota(jnp.int32, (32, 32), 0)
    col32 = lax.broadcasted_iota(jnp.int32, (32, 32), 1)
    plan_rows = jnp.sum(
        jnp.where(row32 == col32, plan_v[...].astype(F32), 0.0), axis=1, keepdims=True
    )
    hot = dest_v[...] == lax.broadcasted_iota(jnp.int32, (32, ROWS), 0)
    group = jnp.sum(jnp.where(hot, plan_rows, 0.0), axis=0, keepdims=True)
    line_g[0] = jnp.concatenate([group, group], axis=1)

    def group_copy(i):
        return remote(line_g.at[0], line_g.at[i], GX + i, GY + i, along_y(4 - i))

    for i in (2, 1, 3):
        group_copy(i).start()

    along = (0, 1, 3, 2)

    def project(start, count, s):
        rows = xb[start : start + count].reshape(count * ROWS, D)
        part = jnp.dot(rows, w[s], preferred_element_type=F32)
        for n in range(count):
            for p in range(3):
                two = part[n * ROWS : (n + 1) * ROWS, 128 * p : 128 * p + 128]
                first, last = two[:HALF], two[HALF:]
                spot = 6 * s + 2 * p
                sb[start + n, spot] = jnp.where(low, first, halves(last)).astype(BF)
                sb[start + n, spot + 1] = jnp.where(low, halves(first), last).astype(BF)

    def scatter(i, blocks):
        tz = plane_of(along[i])
        for s in blocks:
            sub = 3 * y + s
            kind, block = lax.div(sub, 4), lax.rem(sub, 4)
            ty = block + 1 - 2 * lax.rem(block, 2)
            for k in (2, 1, 3, 0):
                push(
                    sb.at[i, 4 * s + turn_x(k)], rb.at[kind, cls, pl.ds(slot * HALF, HALF)],
                    SBS, QR + kind, turn_x(k), ty, tz, cls,
                )

    loads[4].wait()
    project(0, 1, c)
    pl.semaphore_wait(line_z, 2)
    for partner in plane:
        pl.semaphore_signal(line_x, inc=1, device_id=partner, device_id_type=MESH)
    pl.semaphore_wait(line_x, len(plane))
    for i in (1, 2, 3):
        pl.semaphore_signal(line_y, inc=1, device_id=along_y(i), device_id_type=MESH)
    for n in (0, 1):
        row_copy(n).wait_recv()
        row_copy(4 + n).start()
    for i in (0, 1, 3, 2):
        if i:
            group_copy(i).wait_recv()
        tz = plane_of(i)
        for k in (2, 1, 3, 0):
            push(line_g.at[i], gb.at[cls, slot], GS, GR, turn_x(k), y, tz, cls)
    remote(w_qkv, w.at[1 - c], WS, WR, sibling).wait_recv()
    project(0, 1, 1 - c)
    opposite = lax.rem(y + 2, 4)

    def quarter(ty, tx):
        return wo.at[c, ty, pl.ds(pl.multiple_of(tx * HALF, HALF), HALF)]

    def shard_copy(i):
        ref = quarter(y, x) if i == 2 else wo.at[c, y]
        return remote(ref, ref, OS + i, OR + i, along_y(4 - i))

    def quarter_copy(i):
        ref = quarter(opposite, x)
        return remote(ref, ref, QS + i, QV + i, along_x(i))

    def to_sibling(i):
        ty = lax.rem(y + i, 4)
        return remote(wo.at[c, ty], wo.at[c, ty], FS + i, FT + i, sibling)

    scatter(0, (1,))
    pl.semaphore_wait(line_y, 3)
    scatter(0, (0, 2))
    loads[5].wait()
    shard_copy(2).start()
    for n in (2, 3):
        row_copy(n).wait_recv()
    for s in range(2):
        project(1, 2, s)
    scatter(1, (0, 2, 1))
    scatter(2, (0, 2, 1))
    for i in (1, 3):
        shard_copy(i).start()
    to_sibling(0).start()
    for n in (4, 5):
        row_copy(n).wait_recv()
    for s in range(2):
        project(3, 1, s)
    scatter(3, (0, 2, 1))
    mine = [rb.at[1, c], rb.at[2, c], gb.at[c]]
    theirs = [rb.at[1, 1 - c], rb.at[2, 1 - c], gb.at[1 - c]]

    def swap(n, s):
        drain(mine[n], s)
        remote(mine[n], mine[n], PS + n, PR + n, sibling).start()

    lane = lax.broadcasted_iota(jnp.int32, (1, 128), 1)
    lane_group = jnp.where(lane < 64, lax.rem(lax.div(lane, 4), 8), -1).astype(F32)
    row = lax.rem(lax.broadcasted_iota(jnp.int32, (128, 128), 0), HALF)
    col = lax.broadcasted_iota(jnp.int32, (128, 128), 1)

    def group_columns(half, m):
        table = jnp.concatenate(
            [jnp.broadcast_to(gb[half, 4 * m + n], (HALF, 128)) for n in range(4)], axis=0
        )
        return [
            jnp.sum(jnp.where(col == row + base, table, 0.0), axis=1, keepdims=True)
            for base in (0, HALF)
        ]

    def mark_keys(half, m):
        for_low, for_high = group_columns(half, m)
        hit = jnp.where(lane < 32, for_low, for_high) == lane_group
        key_mark[half, 128 * m : 128 * m + 128, :] = jnp.where(hit, 1.0, 0.0).astype(BF)
        if half is not c:
            return
        group = jnp.concatenate([for_low, for_high], axis=0)
        miss = jnp.where(group == lane_group, 0.0, -(2.0**127))
        query_mark[0, m] = jnp.where(lane < 32, miss, 0.0).astype(BF)
        query_mark[1, m] = jnp.where((lane >= 32) & (lane < 64), miss, 0.0).astype(BF)

    swap(2, GR)
    for m in range(4):
        mark_keys(c, m)
    drain(theirs[2], PR + 2)
    for m in range(4):
        mark_keys(1 - c, m)
    shard_copy(2).wait_recv()
    for i in (1, 2, 3):
        quarter_copy(i).start()
    swap(0, QR + 1)
    swap(1, QR + 2)
    drain(rb.at[0, c], QR)

    def spread_values(half):
        vals = rb[2, half]
        turned = halves(vals)
        vd[half, 0:512, :] = jnp.where(low, vals, turned)
        vd[half, 512:1024, :] = jnp.where(low, turned, vals)

    owner_c = 1 - lax.rem(z, 2)
    owner_y = lax.div(lax.rem(z + 2 * owner_c, 8), 2)
    away = lax.rem(y + 4 - owner_y, 4)
    place = away + lax.div(away, 2) * (5 - 2 * away)
    scale = 0.125 * math.log2(math.e)

    def scores(m, half):
        q = rb[0, c, 128 * m : 128 * m + 128, :]
        turned = halves(q)
        none = jnp.zeros_like(q)
        q_low = jnp.concatenate([jnp.where(low, q, none), jnp.where(low, turned, none)], axis=0)
        q_high = jnp.concatenate([jnp.where(low, none, turned), jnp.where(low, none, q)], axis=0)
        keys = jnp.concatenate([rb[1, half], key_mark[half]], axis=1)
        both = [
            lax.dot_general(
                jnp.concatenate([part, query_mark[n, m]], axis=1), keys, NT,
                preferred_element_type=F32,
            )
            for n, part in enumerate((q_low, q_high))
        ]
        top = jnp.maximum(
            jnp.max(both[0], axis=1, keepdims=True), jnp.max(both[1], axis=1, keepdims=True)
        )
        return both[0], both[1], top

    def weigh(s_low, s_high, top, half):
        p_low = jnp.exp2((s_low - top) * scale)
        p_high = jnp.exp2((s_high - top) * scale)
        total = jnp.sum(p_low, axis=1, keepdims=True) + jnp.sum(p_high, axis=1, keepdims=True)
        mixed = jnp.dot(p_low.astype(BF), vd[half, 0:512, :], preferred_element_type=F32)
        mixed += jnp.dot(p_high.astype(BF), vd[half, 512:1024, :], preferred_element_type=F32)
        return total, mixed

    def first_part(m):
        s_low, s_high, top = scores(m, c)
        total, mixed = weigh(s_low, s_high, top, c)
        top_v[m] = top
        sum_v[m] = total
        acc[m] = mixed

    def second_part(m):
        s_low, s_high, top = scores(m, 1 - c)
        before = top_v[m]
        top = jnp.maximum(before, top)
        total, mixed = weigh(s_low, s_high, top, 1 - c)
        factor = jnp.exp2((before - top) * scale)
        context = (acc[m] * factor + mixed) / (sum_v[m] * factor + total)
        co[128 * m : 128 * m + 128, :] = jnp.where(low, context[:128], context[128:]).astype(BF)
        for k in (2, 1, 3, 0):
            push(
                co.at[pl.ds(128 * m + HALF * turn_x(k), HALF)],
                cb.at[place, lax.div(x, 2), lax.rem(x, 2)],
                CS, CR + lax.div(place, 3), turn_x(k), owner_y, 2 * m + c, owner_c,
            )

    spread_values(c)
    for m in range(3):
        first_part(m)
    drain(theirs[0], PR)
    drain(theirs[1], PR + 1)
    spread_values(1 - c)
    for m in range(3):
        second_part(m)
        if m == 2:
            for k in (1, 2, 3):
                quarter_copy(k).wait_recv()
        else:
            shard_copy((1, 3)[m]).wait_recv()
        to_sibling((1, 3, 2)[m]).start()
    first_part(3)
    second_part(3)

    for n in range(6):
        row_copy(n).wait_send()
    for i in (1, 2, 3):
        shard_copy(i).wait_send()
        quarter_copy(i).wait_send()
    remote(w_qkv, w.at[c], WS, WR, sibling).wait_send()
    drain(sb, SBS)
    for n in range(3):
        remote(mine[n], mine[n], PS + n, PR + n, sibling).wait_send()
    drain(gb.at[c], GS)
    for i in (1, 2, 3):
        group_copy(i).wait_send()

    def gathered(p):
        both = []
        for tc in range(2):
            even, odd = cb[p, tc, 0], cb[p, tc, 1]
            both.append(
                jnp.concatenate(
                    [jnp.where(low, even, halves(odd)), jnp.where(low, halves(even), odd)], axis=0
                )
            )
        return jnp.concatenate(both, axis=1)

    def product(p, context, cols):
        ty = lax.rem(y + (0, 1, 3, 2)[p], 4)
        ty = ty + 1 - 2 * lax.rem(ty, 2)
        weights = wo[:, ty, :, cols].reshape(256, 256)
        return jnp.dot(context, weights, preferred_element_type=F32)

    drain(cb.at[pl.ds(0, 3)], CR)
    for i in range(4):
        ty = lax.rem(y + i, 4)
        remote(wo.at[c, ty], wo.at[1 - c, ty], FS + i, FT + i, sibling).wait_recv()
    contexts = [gathered(p) for p in range(3)]
    spans = [slice(256 * n, 256 * n + 256) for n in range(5)]
    for cols in spans:
        near[:, cols] = sum(product(p, contexts[p], cols) for p in range(3))
    drain(cb.at[3], CR + 1)
    context = gathered(3)
    leaving = []
    for n, cols in enumerate(spans):
        result[:, cols] = (near[:, cols] + product(3, context, cols)).astype(BF)
        piece = local(result.at[:, cols], out.at[0, :, cols], RS + n)
        piece.start()
        leaving.append(piece)

    for i in range(4):
        to_sibling(i).wait_send()
    drain(co, CS)
    for piece in leaving:
        piece.wait()


SCRATCH = [
    pltpu.VMEM((ROWS, D), BF),
    pltpu.VMEM((1, ROWS), jnp.int32),
    pltpu.VMEM((1, 32), jnp.int32),
    pltpu.VMEM((D,), F32),
    pltpu.VMEM((4, ROWS, D), BF),
    pltpu.VMEM((2, D, 384), BF),
    pltpu.VMEM((2, 4, 128, D), BF),
    pltpu.VMEM((4, 12, HALF, 128), BF),
    pltpu.VMEM((4, 1, 128), F32),
    pltpu.VMEM((3, 2, 512, 128), BF),
    pltpu.VMEM((2, 16, 1, 128), F32),
    pltpu.VMEM((2, 512, 128), BF),
    pltpu.VMEM((2, 4, 256, 128), BF),
    pltpu.VMEM((2, 1024, 128), BF),
    pltpu.VMEM((512, 128), BF),
    pltpu.VMEM((4, 2, 2, HALF, 128), BF),
    pltpu.VMEM((4, 256, 128), F32),
    pltpu.VMEM((4, 256, 1), F32),
    pltpu.VMEM((4, 256, 1), F32),
    pltpu.VMEM((ROWS, D), F32),
    pltpu.VMEM((ROWS, D), BF),
    pltpu.SemaphoreType.DMA((NSEM,)),
    pltpu.SemaphoreType.REGULAR,
    pltpu.SemaphoreType.REGULAR,
    pltpu.SemaphoreType.REGULAR,
]


def shards(frames, destination, plan, norm_gain, w_qkv, w_out):
    any_space = pl.BlockSpec(memory_space=pl.ANY)
    return pl.pallas_call(
        kernel,
        out_shape=jax.ShapeDtypeStruct((1, ROWS, D), BF),
        in_specs=[any_space] * 6,
        out_specs=any_space,
        scratch_shapes=SCRATCH,
        compiler_params=pltpu.CompilerParams(
            collective_id=0, has_side_effects=True, vmem_limit_bytes=60 * 2**20
        ),
        name="attend",
    )(frames, destination.reshape(1, ROWS), plan, norm_gain, w_qkv, w_out)


def solution(mesh):
    in_specs = (
        P("rep", "grp", None),
        P("rep", "grp", None),
        P("rep", None),
        P(),
        P(None, "rep"),
        P("rep", None),
    )
    out_specs = P("rep", "grp", None)
    return jax.shard_map(shards, mesh=mesh, in_specs=in_specs, out_specs=out_specs, check_vma=False)
```

```python
import math

import jax
import jax.numpy as jnp
from jax import lax
from jax.experimental import pallas as pl
from jax.experimental.pallas import tpu as pltpu
from jax.sharding import PartitionSpec as P

MESH = pl.DeviceIdType.MESH
NT = (((1,), (1,)), ((), ()))
BF = jnp.bfloat16
F32 = jnp.float32
D = 1280
ROWS = 64
HALF = 32
FR, DE, PL, GA, WL, WOL = 0, 1, 2, 3, 4, 5
XS, XR = 6, 12
WS, WR = 18, 19
OS, OR = 20, 24
QS, QV = 28, 32
FS, FT = 36, 40
SBS = 44
QR = 45
GS, GR = 48, 49
PS, PR = 50, 53
CS, CR = 56, 57
GX, GY = 64, 68
NSEM = 72


def halves(block):
    return jnp.concatenate([block[:, 64:], block[:, :64]], axis=1)


def kernel(
    frames, dest, plan, gain, w_qkv, w_out, out,
    raw, dest_v, plan_v, gain_v, xb, w, wo, sb, line_g, rb, gb, key_mark, query_mark, vd, co, cb, acc, top_v,
    sum_v, near, sem, line_x, line_y, line_z,
):
    g = lax.axis_index("grp")
    r = lax.axis_index("rep")
    x, z = lax.div(g, 8), lax.rem(g, 8)
    y, c = lax.div(r, 2), lax.rem(r, 2)
    cls = lax.rem(z, 2)
    slot = lax.div(z, 2) * 4 + x

    def at(tx, ty, tz, tc):
        return (tx * 8 + tz, ty * 2 + tc)

    def turn_x(i):
        return lax.rem(x + i, 4)

    def along_x(i):
        return at(turn_x(i), y, z, c)

    def along_y(i):
        return at(x, lax.rem(y + i, 4), z, c)

    def along_z(i):
        return at(x, y, lax.rem(z + i, 8), c)

    sibling = at(x, y, z, 1 - c)

    def remote(src, dst, ssem, rsem, target):
        return pltpu.make_async_remote_copy(
            src_ref=src, dst_ref=dst, send_sem=sem.at[ssem], recv_sem=sem.at[rsem],
            device_id=target, device_id_type=MESH,
        )

    def local(src, dst, s):
        return pltpu.make_async_copy(src, dst, sem.at[s])

    def push(src, dst, ssem, rsem, tx, ty, tz, tc):
        remote(src, dst, ssem, rsem, at(tx, ty, tz, tc)).start()

    def plane_of(i):
        return lax.rem(2 * lax.rem(y + i, 4) + 1 + 5 * c, 8)

    def drain(ref, s):
        local(ref, ref, s).wait()

    loads = [
        local(frames.at[0], raw, FR),
        local(dest, dest_v, DE),
        local(plan, plan_v, PL),
        local(gain, gain_v, GA),
        local(w_qkv, w.at[c], WL),
        local(w_out, wo.at[c, y], WOL),
    ]
    for load in loads:
        load.start()

    barrier = pltpu.get_barrier_semaphore()
    plane = [at(turn_x(i), y, z, c) for i in (1, 2, 3)]
    plane += [at(turn_x(i), y, z, 1 - c) for i in range(4)]
    partners = [along_y(i) for i in (1, 2, 3)] + plane
    partners += [along_z(i) for i in (1, 2, 6, 7)]
    for partner in partners:
        pl.semaphore_signal(barrier, inc=1, device_id=partner, device_id_type=MESH)

    low = lax.broadcasted_iota(jnp.int32, (1, 128), 1) < 64
    loads[0].wait()
    loads[3].wait()
    values = raw[...].astype(F32)
    mean = jnp.mean(values, axis=1, keepdims=True)
    centered = values - mean
    variance = jnp.mean(centered * centered, axis=1, keepdims=True)
    xb[0] = (centered * lax.rsqrt(variance + 1e-05) * gain_v[...][None, :]).astype(BF)

    pl.semaphore_wait(barrier, len(partners))

    upper, lower = pl.ds(0, HALF), pl.ds(HALF, HALF)

    def row_copy(n):
        block, to, part, source = (
            (1, 3, upper, 0), (2, 1, lower, 0), (1, 3, lower, 0), (2, 1, upper, 0),
            (3, 3, upper, 1), (3, 1, lower, 2),
        )[n]
        return remote(xb.at[source, part], xb.at[block, part], XS + n, XR + n, along_y(to))

    for i in (2, 6):
        pl.semaphore_signal(line_z, inc=1, device_id=along_z(i), device_id_type=MESH)
    for n in range(4):
        row_copy(n).start()
    remote(w_qkv, w.at[c], WS, WR, sibling).start()

    loads[1].wait()
    loads[2].wait()
    row32 = lax.broadcasted_iota(jnp.int32, (32, 32), 0)
    col32 = lax.broadcasted_iota(jnp.int32, (32, 32), 1)
    plan_rows = jnp.sum(
        jnp.where(row32 == col32, plan_v[...].astype(F32), 0.0), axis=1, keepdims=True
    )
    hot = dest_v[...] == lax.broadcasted_iota(jnp.int32, (32, ROWS), 0)
    group = jnp.sum(jnp.where(hot, plan_rows, 0.0), axis=0, keepdims=True)
    line_g[0] = jnp.concatenate([group, group], axis=1)

    def group_copy(i):
        return remote(line_g.at[0], line_g.at[i], GX + i, GY + i, along_y(4 - i))

    for i in (2, 1, 3):
        group_copy(i).start()

    along = (0, 1, 3, 2)

    def project(start, count, s):
        rows = xb[start : start + count].reshape(count * ROWS, D)
        part = jnp.dot(rows, w[s], preferred_element_type=F32)
        for n in range(count):
            for p in range(3):
                two = part[n * ROWS : (n + 1) * ROWS, 128 * p : 128 * p + 128]
                first, last = two[:HALF], two[HALF:]
                spot = 6 * s + 2 * p
                sb[start + n, spot] = jnp.where(low, first, halves(last)).astype(BF)
                sb[start + n, spot + 1] = jnp.where(low, halves(first), last).astype(BF)

    def scatter(i, blocks):
        tz = plane_of(along[i])
        for s in blocks:
            sub = 3 * y + s
            kind, block = lax.div(sub, 4), lax.rem(sub, 4)
            ty = block + 1 - 2 * lax.rem(block, 2)
            for k in (2, 1, 3, 0):
                push(
                    sb.at[i, 4 * s + turn_x(k)], rb.at[kind, cls, pl.ds(slot * HALF, HALF)],
                    SBS, QR + kind, turn_x(k), ty, tz, cls,
                )

    loads[4].wait()
    project(0, 1, c)
    pl.semaphore_wait(line_z, 2)
    for partner in plane:
        pl.semaphore_signal(line_x, inc=1, device_id=partner, device_id_type=MESH)
    pl.semaphore_wait(line_x, len(plane))
    for i in (1, 2, 3):
        pl.semaphore_signal(line_y, inc=1, device_id=along_y(i), device_id_type=MESH)
    for n in (0, 1):
        row_copy(n).wait_recv()
        row_copy(4 + n).start()
    for i in (0, 1, 3, 2):
        if i:
            group_copy(i).wait_recv()
        tz = plane_of(i)
        for k in (2, 1, 3, 0):
            push(line_g.at[i], gb.at[cls, slot], GS, GR, turn_x(k), y, tz, cls)
    remote(w_qkv, w.at[1 - c], WS, WR, sibling).wait_recv()
    project(0, 1, 1 - c)
    opposite = lax.rem(y + 2, 4)

    def quarter(ty, tx):
        return wo.at[c, ty, pl.ds(pl.multiple_of(tx * HALF, HALF), HALF)]

    def shard_copy(i):
        ref = quarter(y, x) if i == 2 else wo.at[c, y]
        return remote(ref, ref, OS + i, OR + i, along_y(4 - i))

    def quarter_copy(i):
        ref = quarter(opposite, x)
        return remote(ref, ref, QS + i, QV + i, along_x(i))

    def to_sibling(i):
        ty = lax.rem(y + i, 4)
        return remote(wo.at[c, ty], wo.at[c, ty], FS + i, FT + i, sibling)

    scatter(0, (1,))
    pl.semaphore_wait(line_y, 3)
    scatter(0, (0, 2))
    loads[5].wait()
    shard_copy(2).start()
    for n in (2, 3):
        row_copy(n).wait_recv()
    for s in range(2):
        project(1, 2, s)
    scatter(1, (0, 2, 1))
    scatter(2, (0, 2, 1))
    for n in (4, 5):
        row_copy(n).wait_recv()
    for s in range(2):
        project(3, 1, s)
    scatter(3, (0, 2, 1))
    for i in (1, 3):
        shard_copy(i).start()
    to_sibling(0).start()

    mine = [rb.at[1, c], rb.at[2, c], gb.at[c]]
    theirs = [rb.at[1, 1 - c], rb.at[2, 1 - c], gb.at[1 - c]]

    def swap(n, s):
        drain(mine[n], s)
        remote(mine[n], mine[n], PS + n, PR + n, sibling).start()

    lane = lax.broadcasted_iota(jnp.int32, (1, 128), 1)
    lane_group = jnp.where(lane < 64, lax.rem(lax.div(lane, 4), 8), -1).astype(F32)
    row = lax.rem(lax.broadcasted_iota(jnp.int32, (128, 128), 0), HALF)
    col = lax.broadcasted_iota(jnp.int32, (128, 128), 1)

    def group_columns(half, m):
        table = jnp.concatenate(
            [jnp.broadcast_to(gb[half, 4 * m + n], (HALF, 128)) for n in range(4)], axis=0
        )
        return [
            jnp.sum(jnp.where(col == row + base, table, 0.0), axis=1, keepdims=True)
            for base in (0, HALF)
        ]

    def mark_keys(half, m):
        for_low, for_high = group_columns(half, m)
        hit = jnp.where(lane < 32, for_low, for_high) == lane_group
        key_mark[half, 128 * m : 128 * m + 128, :] = jnp.where(hit, 1.0, 0.0).astype(BF)
        if half is not c:
            return
        group = jnp.concatenate([for_low, for_high], axis=0)
        miss = jnp.where(group == lane_group, 0.0, -(2.0**127))
        query_mark[0, m] = jnp.where(lane < 32, miss, 0.0).astype(BF)
        query_mark[1, m] = jnp.where((lane >= 32) & (lane < 64), miss, 0.0).astype(BF)

    swap(2, GR)
    for m in range(4):
        mark_keys(c, m)
    drain(theirs[2], PR + 2)
    for m in range(4):
        mark_keys(1 - c, m)
    shard_copy(2).wait_recv()
    for i in (1, 2, 3):
        quarter_copy(i).start()
    swap(0, QR + 1)
    swap(1, QR + 2)
    drain(rb.at[0, c], QR)

    def spread_values(half):
        vals = rb[2, half]
        turned = halves(vals)
        vd[half, 0:512, :] = jnp.where(low, vals, turned)
        vd[half, 512:1024, :] = jnp.where(low, turned, vals)

    owner_c = 1 - lax.rem(z, 2)
    owner_y = lax.div(lax.rem(z + 2 * owner_c, 8), 2)
    away = lax.rem(y + 4 - owner_y, 4)
    place = away + lax.div(away, 2) * (5 - 2 * away)
    scale = 0.125 * math.log2(math.e)

    def scores(m, half):
        q = rb[0, c, 128 * m : 128 * m + 128, :]
        turned = halves(q)
        none = jnp.zeros_like(q)
        q_low = jnp.concatenate([jnp.where(low, q, none), jnp.where(low, turned, none)], axis=0)
        q_high = jnp.concatenate([jnp.where(low, none, turned), jnp.where(low, none, q)], axis=0)
        keys = jnp.concatenate([rb[1, half], key_mark[half]], axis=1)
        both = [
            lax.dot_general(
                jnp.concatenate([part, query_mark[n, m]], axis=1), keys, NT,
                preferred_element_type=F32,
            )
            for n, part in enumerate((q_low, q_high))
        ]
        top = jnp.maximum(
            jnp.max(both[0], axis=1, keepdims=True), jnp.max(both[1], axis=1, keepdims=True)
        )
        return both[0], both[1], top

    def weigh(s_low, s_high, top, half):
        p_low = jnp.exp2((s_low - top) * scale)
        p_high = jnp.exp2((s_high - top) * scale)
        total = jnp.sum(p_low, axis=1, keepdims=True) + jnp.sum(p_high, axis=1, keepdims=True)
        mixed = jnp.dot(p_low.astype(BF), vd[half, 0:512, :], preferred_element_type=F32)
        mixed += jnp.dot(p_high.astype(BF), vd[half, 512:1024, :], preferred_element_type=F32)
        return total, mixed

    def first_part(m):
        s_low, s_high, top = scores(m, c)
        total, mixed = weigh(s_low, s_high, top, c)
        top_v[m] = top
        sum_v[m] = total
        acc[m] = mixed

    def second_part(m):
        s_low, s_high, top = scores(m, 1 - c)
        before = top_v[m]
        top = jnp.maximum(before, top)
        total, mixed = weigh(s_low, s_high, top, 1 - c)
        factor = jnp.exp2((before - top) * scale)
        context = (acc[m] * factor + mixed) / (sum_v[m] * factor + total)
        co[128 * m : 128 * m + 128, :] = jnp.where(low, context[:128], context[128:]).astype(BF)
        for k in (2, 1, 3, 0):
            push(
                co.at[pl.ds(128 * m + HALF * turn_x(k), HALF)],
                cb.at[place, lax.div(x, 2), lax.rem(x, 2)],
                CS, CR + lax.div(place, 3), turn_x(k), owner_y, 2 * m + c, owner_c,
            )

    spread_values(c)
    for m in range(3):
        first_part(m)
    drain(theirs[0], PR)
    drain(theirs[1], PR + 1)
    spread_values(1 - c)
    for m in range(3):
        second_part(m)
        if m == 0:
            for k in (1, 2, 3):
                quarter_copy(k).wait_recv()
            to_sibling(2).start()
    first_part(3)
    second_part(3)

    for i in (1, 3):
        shard_copy(i).wait_recv()
        to_sibling(i).start()

    for n in range(6):
        row_copy(n).wait_send()
    for i in (1, 2, 3):
        shard_copy(i).wait_send()
        quarter_copy(i).wait_send()
    remote(w_qkv, w.at[c], WS, WR, sibling).wait_send()
    drain(sb, SBS)
    for n in range(3):
        remote(mine[n], mine[n], PS + n, PR + n, sibling).wait_send()
    drain(gb.at[c], GS)
    for i in (1, 2, 3):
        group_copy(i).wait_send()

    def gathered(p):
        both = []
        for tc in range(2):
            even, odd = cb[p, tc, 0], cb[p, tc, 1]
            both.append(
                jnp.concatenate(
                    [jnp.where(low, even, halves(odd)), jnp.where(low, halves(even), odd)], axis=0
                )
            )
        return jnp.concatenate(both, axis=1)

    def product(p, context, cols):
        ty = lax.rem(y + (0, 1, 3, 2)[p], 4)
        ty = ty + 1 - 2 * lax.rem(ty, 2)
        weights = wo[:, ty, :, cols].reshape(256, 256)
        return jnp.dot(context, weights, preferred_element_type=F32)

    drain(cb.at[pl.ds(0, 3)], CR)
    for i in range(4):
        ty = lax.rem(y + i, 4)
        remote(wo.at[c, ty], wo.at[1 - c, ty], FS + i, FT + i, sibling).wait_recv()
    contexts = [gathered(p) for p in range(3)]
    spans = [slice(256 * n, 256 * n + 256) for n in range(5)]
    for cols in spans:
        near[:, cols] = sum(product(p, contexts[p], cols) for p in range(3))
    drain(cb.at[3], CR + 1)
    context = gathered(3)
    for cols in spans:
        out[0, :, cols] = (near[:, cols] + product(3, context, cols)).astype(BF)

    for i in range(4):
        to_sibling(i).wait_send()
    drain(co, CS)


SCRATCH = [
    pltpu.VMEM((ROWS, D), BF),
    pltpu.VMEM((1, ROWS), jnp.int32),
    pltpu.VMEM((1, 32), jnp.int32),
    pltpu.VMEM((D,), F32),
    pltpu.VMEM((4, ROWS, D), BF),
    pltpu.VMEM((2, D, 384), BF),
    pltpu.VMEM((2, 4, 128, D), BF),
    pltpu.VMEM((4, 12, HALF, 128), BF),
    pltpu.VMEM((4, 1, 128), F32),
    pltpu.VMEM((3, 2, 512, 128), BF),
    pltpu.VMEM((2, 16, 1, 128), F32),
    pltpu.VMEM((2, 512, 128), BF),
    pltpu.VMEM((2, 4, 256, 128), BF),
    pltpu.VMEM((2, 1024, 128), BF),
    pltpu.VMEM((512, 128), BF),
    pltpu.VMEM((4, 2, 2, HALF, 128), BF),
    pltpu.VMEM((4, 256, 128), F32),
    pltpu.VMEM((4, 256, 1), F32),
    pltpu.VMEM((4, 256, 1), F32),
    pltpu.VMEM((ROWS, D), F32),
    pltpu.SemaphoreType.DMA((NSEM,)),
    pltpu.SemaphoreType.REGULAR,
    pltpu.SemaphoreType.REGULAR,
    pltpu.SemaphoreType.REGULAR,
]


def shards(frames, destination, plan, norm_gain, w_qkv, w_out):
    any_space = pl.BlockSpec(memory_space=pl.ANY)
    return pl.pallas_call(
        kernel,
        out_shape=jax.ShapeDtypeStruct((1, ROWS, D), BF),
        in_specs=[any_space] * 6,
        out_specs=pl.BlockSpec(memory_space=pltpu.VMEM),
        scratch_shapes=SCRATCH,
        compiler_params=pltpu.CompilerParams(
            collective_id=0, has_side_effects=True, vmem_limit_bytes=55008 * 2**10
        ),
        name="attend",
    )(frames, destination.reshape(1, ROWS), plan, norm_gain, w_qkv, w_out)


def solution(mesh):
    in_specs = (
        P("rep", "grp", None),
        P("rep", "grp", None),
        P("rep", None),
        P(),
        P(None, "rep"),
        P("rep", None),
    )
    out_specs = P("rep", "grp", None)
    return jax.shard_map(shards, mesh=mesh, in_specs=in_specs, out_specs=out_specs, check_vma=False)
```

```python
import math

import jax
import jax.numpy as jnp
from jax import lax
from jax.experimental import pallas as pl
from jax.experimental.pallas import tpu as pltpu
from jax.sharding import PartitionSpec as P

MESH = pl.DeviceIdType.MESH
NT = (((1,), (1,)), ((), ()))
BF = jnp.bfloat16
F32 = jnp.float32
D = 1280
ROWS = 64
HALF = 32
FR, DE, PL, GA, WL, WOL = 0, 1, 2, 3, 4, 5
XS, XR = 6, 12
WS, WR = 18, 19
OS, OR = 20, 24
QS, QV = 28, 32
FS, FT = 36, 40
SBS = 44
QR = 45
GS, GR = 48, 49
PS, PR = 50, 53
CS, CR = 56, 57
GX, GY = 64, 68
NSEM = 72


def halves(block):
    return jnp.concatenate([block[:, 64:], block[:, :64]], axis=1)


def kernel(
    frames, dest, plan, gain, w_qkv, w_out, out,
    raw, dest_v, plan_v, gain_v, xb, w, wo, sb, line_g, rb, gb, key_mark, query_mark, vd, co, cb, acc, top_v,
    sum_v, near, spare, spare_g, sem, line_x, line_y, line_z,
):
    g = lax.axis_index("grp")
    r = lax.axis_index("rep")
    x, z = lax.div(g, 8), lax.rem(g, 8)
    y, c = lax.div(r, 2), lax.rem(r, 2)
    cls = lax.rem(z, 2)
    slot = lax.div(z, 2) * 4 + x

    def at(tx, ty, tz, tc):
        return (tx * 8 + tz, ty * 2 + tc)

    def turn_x(i):
        return lax.rem(x + i, 4)

    def along_x(i):
        return at(turn_x(i), y, z, c)

    def along_y(i):
        return at(x, lax.rem(y + i, 4), z, c)

    def along_z(i):
        return at(x, y, lax.rem(z + i, 8), c)

    sibling = at(x, y, z, 1 - c)

    def remote(src, dst, ssem, rsem, target):
        return pltpu.make_async_remote_copy(
            src_ref=src, dst_ref=dst, send_sem=sem.at[ssem], recv_sem=sem.at[rsem],
            device_id=target, device_id_type=MESH,
        )

    def local(src, dst, s):
        return pltpu.make_async_copy(src, dst, sem.at[s])

    def push(src, dst, ssem, rsem, tx, ty, tz, tc, dummy):
        if dummy is None:
            remote(src, dst, ssem, rsem, at(tx, ty, tz, tc)).start()
            return
        same = (ty == y) & (tz == z) & (tc == c)

        @pl.when(jnp.logical_not(same))
        def _():
            remote(src, dst, ssem, rsem, at(tx, ty, tz, tc)).start()

        @pl.when(same)
        def _():
            local(src, dst, rsem).start()
            local(src, dummy, ssem).start()

    def plane_of(i):
        return lax.rem(y + i, 4) + 4 * (1 - c)

    def drain(ref, s):
        local(ref, ref, s).wait()

    loads = [
        local(frames.at[0], raw, FR),
        local(dest, dest_v, DE),
        local(plan, plan_v, PL),
        local(gain, gain_v, GA),
        local(w_qkv, w.at[c], WL),
        local(w_out, wo.at[c, y], WOL),
    ]
    for load in loads:
        load.start()

    barrier = pltpu.get_barrier_semaphore()
    plane = [at(turn_x(i), y, z, c) for i in (1, 2, 3)]
    plane += [at(turn_x(i), y, z, 1 - c) for i in range(4)]
    partners = [along_y(i) for i in (1, 2, 3)] + plane
    partners += [along_z(i) for i in (1, 2, 6, 7)]
    for partner in partners:
        pl.semaphore_signal(barrier, inc=1, device_id=partner, device_id_type=MESH)

    low = lax.broadcasted_iota(jnp.int32, (1, 128), 1) < 64
    loads[0].wait()
    loads[3].wait()
    values = raw[...].astype(F32)
    mean = jnp.mean(values, axis=1, keepdims=True)
    centered = values - mean
    variance = jnp.mean(centered * centered, axis=1, keepdims=True)
    xb[0] = (centered * lax.rsqrt(variance + 1e-05) * gain_v[...][None, :]).astype(BF)

    pl.semaphore_wait(barrier, len(partners))

    upper, lower = pl.ds(0, HALF), pl.ds(HALF, HALF)

    def row_copy(n):
        block, to, part, source = (
            (1, 3, upper, 0), (2, 1, lower, 0), (1, 3, lower, 0), (2, 1, upper, 0),
            (3, 3, upper, 1), (3, 1, lower, 2),
        )[n]
        return remote(xb.at[source, part], xb.at[block, part], XS + n, XR + n, along_y(to))

    for i in (2, 6):
        pl.semaphore_signal(line_z, inc=1, device_id=along_z(i), device_id_type=MESH)
    for n in range(4):
        row_copy(n).start()
    remote(w_qkv, w.at[c], WS, WR, sibling).start()

    loads[1].wait()
    loads[2].wait()
    row32 = lax.broadcasted_iota(jnp.int32, (32, 32), 0)
    col32 = lax.broadcasted_iota(jnp.int32, (32, 32), 1)
    plan_rows = jnp.sum(
        jnp.where(row32 == col32, plan_v[...].astype(F32), 0.0), axis=1, keepdims=True
    )
    hot = dest_v[...] == lax.broadcasted_iota(jnp.int32, (32, ROWS), 0)
    group = jnp.sum(jnp.where(hot, plan_rows, 0.0), axis=0, keepdims=True)
    line_g[0] = jnp.concatenate([group, group], axis=1)

    def group_copy(i):
        return remote(line_g.at[0], line_g.at[i], GX + i, GY + i, along_y(4 - i))

    for i in (2, 1, 3):
        group_copy(i).start()

    along = (0, 1, 3, 2)

    def project(start, count, s):
        rows = xb[start : start + count].reshape(count * ROWS, D)
        part = jnp.dot(rows, w[s], preferred_element_type=F32)
        for n in range(count):
            for p in range(3):
                two = part[n * ROWS : (n + 1) * ROWS, 128 * p : 128 * p + 128]
                first, last = two[:HALF], two[HALF:]
                spot = 6 * s + 2 * p
                sb[start + n, spot] = jnp.where(low, first, halves(last)).astype(BF)
                sb[start + n, spot + 1] = jnp.where(low, halves(first), last).astype(BF)

    def scatter(i, blocks):
        tz = plane_of(along[i])
        for s in blocks:
            sub = 3 * y + s
            kind, block = lax.div(sub, 4), lax.rem(sub, 4)
            ty = block + 1 - 2 * lax.rem(block, 2)
            for k in (2, 1, 3, 0):
                push(
                    sb.at[i, 4 * s + turn_x(k)], rb.at[kind, cls, pl.ds(slot * HALF, HALF)],
                    SBS, QR + kind, turn_x(k), ty, tz, cls, None if k else spare.at[0],
                )

    loads[4].wait()
    project(0, 1, c)
    pl.semaphore_wait(line_z, 2)
    for partner in plane:
        pl.semaphore_signal(line_x, inc=1, device_id=partner, device_id_type=MESH)
    pl.semaphore_wait(line_x, len(plane))
    for i in (1, 2, 3):
        pl.semaphore_signal(line_y, inc=1, device_id=along_y(i), device_id_type=MESH)
    for n in (0, 1):
        row_copy(n).wait_recv()
        row_copy(4 + n).start()
    for i in (0, 1, 3, 2):
        if i:
            group_copy(i).wait_recv()
        tz = plane_of(i)
        for k in (2, 1, 3, 0):
            push(line_g.at[i], gb.at[cls, slot], GS, GR, turn_x(k), y, tz, cls,
                 None if k else spare_g)
    remote(w_qkv, w.at[1 - c], WS, WR, sibling).wait_recv()
    project(0, 1, 1 - c)
    opposite = lax.rem(y + 2, 4)

    def quarter(ty, tx):
        return wo.at[c, ty, pl.ds(pl.multiple_of(tx * HALF, HALF), HALF)]

    def shard_copy(i):
        ref = quarter(y, x) if i == 2 else wo.at[c, y]
        return remote(ref, ref, OS + i, OR + i, along_y(4 - i))

    def quarter_copy(i):
        ref = quarter(opposite, x)
        return remote(ref, ref, QS + i, QV + i, along_x(i))

    def to_sibling(i):
        ty = lax.rem(y + i, 4)
        return remote(wo.at[c, ty], wo.at[c, ty], FS + i, FT + i, sibling)

    scatter(0, (1,))
    pl.semaphore_wait(line_y, 3)
    scatter(0, (0, 2))
    loads[5].wait()
    shard_copy(2).start()
    for n in (2, 3):
        row_copy(n).wait_recv()
    for s in range(2):
        project(1, 2, s)
    scatter(1, (0, 2, 1))
    scatter(2, (0, 2, 1))
    for n in (4, 5):
        row_copy(n).wait_recv()
    for s in range(2):
        project(3, 1, s)
    scatter(3, (0, 2, 1))
    for i in (1, 3):
        shard_copy(i).start()
    to_sibling(0).start()

    mine = [rb.at[1, c], rb.at[2, c], gb.at[c]]
    theirs = [rb.at[1, 1 - c], rb.at[2, 1 - c], gb.at[1 - c]]

    def swap(n, s):
        drain(mine[n], s)
        remote(mine[n], mine[n], PS + n, PR + n, sibling).start()

    lane = lax.broadcasted_iota(jnp.int32, (1, 128), 1)
    lane_group = jnp.where(lane < 64, lax.rem(lax.div(lane, 4), 8), -1).astype(F32)
    row = lax.rem(lax.broadcasted_iota(jnp.int32, (128, 128), 0), HALF)
    col = lax.broadcasted_iota(jnp.int32, (128, 128), 1)

    def group_columns(half, m):
        table = jnp.concatenate(
            [jnp.broadcast_to(gb[half, 4 * m + n], (HALF, 128)) for n in range(4)], axis=0
        )
        return [
            jnp.sum(jnp.where(col == row + base, table, 0.0), axis=1, keepdims=True)
            for base in (0, HALF)
        ]

    def mark_keys(half, m):
        for_low, for_high = group_columns(half, m)
        hit = jnp.where(lane < 32, for_low, for_high) == lane_group
        key_mark[half, 128 * m : 128 * m + 128, :] = jnp.where(hit, 1.0, 0.0).astype(BF)
        if half is not c:
            return
        group = jnp.concatenate([for_low, for_high], axis=0)
        miss = jnp.where(group == lane_group, 0.0, -(2.0**127))
        query_mark[0, m] = jnp.where(lane < 32, miss, 0.0).astype(BF)
        query_mark[1, m] = jnp.where((lane >= 32) & (lane < 64), miss, 0.0).astype(BF)

    swap(2, GR)
    for m in range(4):
        mark_keys(c, m)
    drain(theirs[2], PR + 2)
    for m in range(4):
        mark_keys(1 - c, m)
    shard_copy(2).wait_recv()
    for i in (1, 2, 3):
        quarter_copy(i).start()
    swap(0, QR + 1)
    swap(1, QR + 2)
    drain(rb.at[0, c], QR)

    def spread_values(half):
        vals = rb[2, half]
        turned = halves(vals)
        vd[half, 0:512, :] = jnp.where(low, vals, turned)
        vd[half, 512:1024, :] = jnp.where(low, turned, vals)

    owner_y, owner_c = lax.rem(z, 4), 1 - lax.div(z, 4)
    away = lax.rem(y + 4 - owner_y, 4)
    place = away + lax.div(away, 2) * (5 - 2 * away)
    scale = 0.125 * math.log2(math.e)

    def scores(m, half):
        q = rb[0, c, 128 * m : 128 * m + 128, :]
        turned = halves(q)
        none = jnp.zeros_like(q)
        q_low = jnp.concatenate([jnp.where(low, q, none), jnp.where(low, turned, none)], axis=0)
        q_high = jnp.concatenate([jnp.where(low, none, turned), jnp.where(low, none, q)], axis=0)
        keys = jnp.concatenate([rb[1, half], key_mark[half]], axis=1)
        both = [
            lax.dot_general(
                jnp.concatenate([part, query_mark[n, m]], axis=1), keys, NT,
                preferred_element_type=F32,
            )
            for n, part in enumerate((q_low, q_high))
        ]
        top = jnp.maximum(
            jnp.max(both[0], axis=1, keepdims=True), jnp.max(both[1], axis=1, keepdims=True)
        )
        return both[0], both[1], top

    def weigh(s_low, s_high, top, half):
        p_low = jnp.exp2((s_low - top) * scale)
        p_high = jnp.exp2((s_high - top) * scale)
        total = jnp.sum(p_low, axis=1, keepdims=True) + jnp.sum(p_high, axis=1, keepdims=True)
        mixed = jnp.dot(p_low.astype(BF), vd[half, 0:512, :], preferred_element_type=F32)
        mixed += jnp.dot(p_high.astype(BF), vd[half, 512:1024, :], preferred_element_type=F32)
        return total, mixed

    def first_part(m):
        s_low, s_high, top = scores(m, c)
        total, mixed = weigh(s_low, s_high, top, c)
        top_v[m] = top
        sum_v[m] = total
        acc[m] = mixed

    def second_part(m):
        s_low, s_high, top = scores(m, 1 - c)
        before = top_v[m]
        top = jnp.maximum(before, top)
        total, mixed = weigh(s_low, s_high, top, 1 - c)
        factor = jnp.exp2((before - top) * scale)
        context = (acc[m] * factor + mixed) / (sum_v[m] * factor + total)
        co[128 * m : 128 * m + 128, :] = jnp.where(low, context[:128], context[128:]).astype(BF)
        for k in (2, 1, 3, 0):
            push(
                co.at[pl.ds(128 * m + HALF * turn_x(k), HALF)],
                cb.at[place, lax.div(x, 2), lax.rem(x, 2)],
                CS, CR + lax.div(place, 3), turn_x(k), owner_y, 2 * m + c, owner_c, None if k else spare.at[1],
            )

    spread_values(c)
    for m in range(3):
        first_part(m)
    drain(theirs[0], PR)
    drain(theirs[1], PR + 1)
    spread_values(1 - c)
    for m in range(3):
        second_part(m)
        if m == 0:
            for k in (1, 2, 3):
                quarter_copy(k).wait_recv()
            to_sibling(2).start()
    first_part(3)
    second_part(3)

    for i in (1, 3):
        shard_copy(i).wait_recv()
        to_sibling(i).start()

    for n in range(6):
        row_copy(n).wait_send()
    for i in (1, 2, 3):
        shard_copy(i).wait_send()
        quarter_copy(i).wait_send()
    remote(w_qkv, w.at[c], WS, WR, sibling).wait_send()
    drain(sb, SBS)
    for n in range(3):
        remote(mine[n], mine[n], PS + n, PR + n, sibling).wait_send()
    drain(gb.at[c], GS)
    for i in (1, 2, 3):
        group_copy(i).wait_send()

    def gathered(p):
        both = []
        for tc in range(2):
            even, odd = cb[p, tc, 0], cb[p, tc, 1]
            both.append(
                jnp.concatenate(
                    [jnp.where(low, even, halves(odd)), jnp.where(low, halves(even), odd)], axis=0
                )
            )
        return jnp.concatenate(both, axis=1)

    def product(p, context, cols):
        ty = lax.rem(y + (0, 1, 3, 2)[p], 4)
        ty = ty + 1 - 2 * lax.rem(ty, 2)
        weights = wo[:, ty, :, cols].reshape(256, 256)
        return jnp.dot(context, weights, preferred_element_type=F32)

    drain(cb.at[pl.ds(0, 3)], CR)
    for i in range(4):
        ty = lax.rem(y + i, 4)
        remote(wo.at[c, ty], wo.at[1 - c, ty], FS + i, FT + i, sibling).wait_recv()
    contexts = [gathered(p) for p in range(3)]
    spans = [slice(256 * n, 256 * n + 256) for n in range(5)]
    for cols in spans:
        near[:, cols] = sum(product(p, contexts[p], cols) for p in range(3))
    drain(cb.at[3], CR + 1)
    context = gathered(3)
    for cols in spans:
        out[0, :, cols] = (near[:, cols] + product(3, context, cols)).astype(BF)

    for i in range(4):
        to_sibling(i).wait_send()
    drain(co, CS)


SCRATCH = [
    pltpu.VMEM((ROWS, D), BF),
    pltpu.VMEM((1, ROWS), jnp.int32),
    pltpu.VMEM((1, 32), jnp.int32),
    pltpu.VMEM((D,), F32),
    pltpu.VMEM((4, ROWS, D), BF),
    pltpu.VMEM((2, D, 384), BF),
    pltpu.VMEM((2, 4, 128, D), BF),
    pltpu.VMEM((4, 12, HALF, 128), BF),
    pltpu.VMEM((4, 1, 128), F32),
    pltpu.VMEM((3, 2, 512, 128), BF),
    pltpu.VMEM((2, 16, 1, 128), F32),
    pltpu.VMEM((2, 512, 128), BF),
    pltpu.VMEM((2, 4, 256, 128), BF),
    pltpu.VMEM((2, 1024, 128), BF),
    pltpu.VMEM((512, 128), BF),
    pltpu.VMEM((4, 2, 2, HALF, 128), BF),
    pltpu.VMEM((4, 256, 128), F32),
    pltpu.VMEM((4, 256, 1), F32),
    pltpu.VMEM((4, 256, 1), F32),
    pltpu.VMEM((ROWS, D), F32),
    pltpu.VMEM((2, HALF, 128), BF),
    pltpu.VMEM((1, 128), F32),
    pltpu.SemaphoreType.DMA((NSEM,)),
    pltpu.SemaphoreType.REGULAR,
    pltpu.SemaphoreType.REGULAR,
    pltpu.SemaphoreType.REGULAR,
]


def shards(frames, destination, plan, norm_gain, w_qkv, w_out):
    any_space = pl.BlockSpec(memory_space=pl.ANY)
    return pl.pallas_call(
        kernel,
        out_shape=jax.ShapeDtypeStruct((1, ROWS, D), BF),
        in_specs=[any_space] * 6,
        out_specs=pl.BlockSpec(memory_space=pltpu.VMEM),
        scratch_shapes=SCRATCH,
        compiler_params=pltpu.CompilerParams(
            collective_id=0, has_side_effects=True, vmem_limit_bytes=55008 * 2**10
        ),
        name="attend",
    )(frames, destination.reshape(1, ROWS), plan, norm_gain, w_qkv, w_out)


def solution(mesh):
    in_specs = (
        P("rep", "grp", None),
        P("rep", "grp", None),
        P("rep", None),
        P(),
        P(None, "rep"),
        P("rep", None),
    )
    out_specs = P("rep", "grp", None)
    return jax.shard_map(shards, mesh=mesh, in_specs=in_specs, out_specs=out_specs, check_vma=False)
```

```python
import math

import jax
import jax.numpy as jnp
from jax import lax
from jax.experimental import pallas as pl
from jax.experimental.pallas import tpu as pltpu
from jax.sharding import PartitionSpec as P

MESH = pl.DeviceIdType.MESH
NT = (((1,), (1,)), ((), ()))
BF = jnp.bfloat16
F32 = jnp.float32
D = 1280
ROWS = 64
HALF = 32
FR, DE, PL, GA, WL, WOL = 0, 1, 2, 3, 4, 5
XS, XR = 6, 12
WS, WR = 18, 19
OS, OR = 20, 24
QS, QV = 28, 32
FS, FT = 36, 40
SBS = 44
QR = 45
GS, GR = 48, 49
PS, PR = 50, 53
CS, CR = 56, 57
GX, GY = 64, 68
NSEM = 72


def halves(block):
    return jnp.concatenate([block[:, 64:], block[:, :64]], axis=1)


def kernel(
    frames, dest, plan, gain, w_qkv, w_out, out,
    raw, dest_v, plan_v, gain_v, xb, w, wo, sb, line_g, rb, gb, key_mark, query_mark, vd, co, cb, acc, top_v,
    sum_v, near, spare, spare_g, sem, line_x, line_y, line_z,
):
    g = lax.axis_index("grp")
    r = lax.axis_index("rep")
    x, z = lax.div(g, 8), lax.rem(g, 8)
    y, c = lax.div(r, 2), lax.rem(r, 2)
    cls = lax.rem(z, 2)
    slot = lax.div(z, 2) * 4 + x

    def at(tx, ty, tz, tc):
        return (tx * 8 + tz, ty * 2 + tc)

    def turn_x(i):
        return lax.rem(x + i, 4)

    def along_x(i):
        return at(turn_x(i), y, z, c)

    def along_y(i):
        return at(x, lax.rem(y + i, 4), z, c)

    def along_z(i):
        return at(x, y, lax.rem(z + i, 8), c)

    sibling = at(x, y, z, 1 - c)

    def remote(src, dst, ssem, rsem, target):
        return pltpu.make_async_remote_copy(
            src_ref=src, dst_ref=dst, send_sem=sem.at[ssem], recv_sem=sem.at[rsem],
            device_id=target, device_id_type=MESH,
        )

    def local(src, dst, s):
        return pltpu.make_async_copy(src, dst, sem.at[s])

    def push(src, dst, ssem, rsem, tx, ty, tz, tc, dummy):
        if dummy is None:
            remote(src, dst, ssem, rsem, at(tx, ty, tz, tc)).start()
            return
        same = (ty == y) & (tz == z) & (tc == c)

        @pl.when(jnp.logical_not(same))
        def _():
            remote(src, dst, ssem, rsem, at(tx, ty, tz, tc)).start()

        @pl.when(same)
        def _():
            local(src, dst, rsem).start()
            local(src, dummy, ssem).start()

    def plane_of(i):
        return lax.rem(y + i + 1 - c, 4) + 4 * (1 - c)

    def drain(ref, s):
        local(ref, ref, s).wait()

    loads = [
        local(frames.at[0], raw, FR),
        local(dest, dest_v, DE),
        local(plan, plan_v, PL),
        local(gain, gain_v, GA),
        local(w_qkv, w.at[c], WL),
        local(w_out, wo.at[c, y], WOL),
    ]
    for load in loads:
        load.start()

    barrier = pltpu.get_barrier_semaphore()
    plane = [at(turn_x(i), y, z, c) for i in (1, 2, 3)]
    plane += [at(turn_x(i), y, z, 1 - c) for i in range(4)]
    partners = [along_y(i) for i in (1, 2, 3)] + plane
    partners += [along_z(i) for i in (1, 2, 6, 7)]
    for partner in partners:
        pl.semaphore_signal(barrier, inc=1, device_id=partner, device_id_type=MESH)

    low = lax.broadcasted_iota(jnp.int32, (1, 128), 1) < 64
    loads[0].wait()
    loads[3].wait()
    values = raw[...].astype(F32)
    mean = jnp.mean(values, axis=1, keepdims=True)
    centered = values - mean
    variance = jnp.mean(centered * centered, axis=1, keepdims=True)
    xb[0] = (centered * lax.rsqrt(variance + 1e-05) * gain_v[...][None, :]).astype(BF)

    pl.semaphore_wait(barrier, len(partners))

    upper, lower = pl.ds(0, HALF), pl.ds(HALF, HALF)

    def row_copy(n):
        block, to, part, source = (
            (1, 3, upper, 0), (2, 1, lower, 0), (1, 3, lower, 0), (2, 1, upper, 0),
            (3, 3, upper, 1), (3, 1, lower, 2),
        )[n]
        return remote(xb.at[source, part], xb.at[block, part], XS + n, XR + n, along_y(to))

    for i in (2, 6):
        pl.semaphore_signal(line_z, inc=1, device_id=along_z(i), device_id_type=MESH)
    for n in range(4):
        row_copy(n).start()
    remote(w_qkv, w.at[c], WS, WR, sibling).start()

    loads[1].wait()
    loads[2].wait()
    row32 = lax.broadcasted_iota(jnp.int32, (32, 32), 0)
    col32 = lax.broadcasted_iota(jnp.int32, (32, 32), 1)
    plan_rows = jnp.sum(
        jnp.where(row32 == col32, plan_v[...].astype(F32), 0.0), axis=1, keepdims=True
    )
    hot = dest_v[...] == lax.broadcasted_iota(jnp.int32, (32, ROWS), 0)
    group = jnp.sum(jnp.where(hot, plan_rows, 0.0), axis=0, keepdims=True)
    line_g[0] = jnp.concatenate([group, group], axis=1)

    def group_copy(i):
        return remote(line_g.at[0], line_g.at[i], GX + i, GY + i, along_y(4 - i))

    for i in (2, 1, 3):
        group_copy(i).start()

    along = (0, 1, 3, 2)

    def project(start, count, s):
        rows = xb[start : start + count].reshape(count * ROWS, D)
        part = jnp.dot(rows, w[s], preferred_element_type=F32)
        for n in range(count):
            for p in range(3):
                two = part[n * ROWS : (n + 1) * ROWS, 128 * p : 128 * p + 128]
                first, last = two[:HALF], two[HALF:]
                spot = 6 * s + 2 * p
                sb[start + n, spot] = jnp.where(low, first, halves(last)).astype(BF)
                sb[start + n, spot + 1] = jnp.where(low, halves(first), last).astype(BF)

    def scatter(i, blocks):
        tz = plane_of(along[i])
        for s in blocks:
            sub = 3 * y + s
            kind, block = lax.div(sub, 4), lax.rem(sub, 4)
            ty = block + 1 - 2 * lax.rem(block, 2)
            for k in (2, 1, 3, 0):
                push(
                    sb.at[i, 4 * s + turn_x(k)], rb.at[kind, cls, pl.ds(slot * HALF, HALF)],
                    SBS, QR + kind, turn_x(k), ty, tz, cls, None if k else spare.at[0],
                )

    loads[4].wait()
    project(0, 1, c)
    pl.semaphore_wait(line_z, 2)
    for partner in plane:
        pl.semaphore_signal(line_x, inc=1, device_id=partner, device_id_type=MESH)
    pl.semaphore_wait(line_x, len(plane))
    for i in (1, 2, 3):
        pl.semaphore_signal(line_y, inc=1, device_id=along_y(i), device_id_type=MESH)
    for n in (0, 1):
        row_copy(n).wait_recv()
        row_copy(4 + n).start()
    for i in (0, 1, 3, 2):
        if i:
            group_copy(i).wait_recv()
        tz = plane_of(i)
        for k in (2, 1, 3, 0):
            push(line_g.at[i], gb.at[cls, slot], GS, GR, turn_x(k), y, tz, cls,
                 None if k else spare_g)
    remote(w_qkv, w.at[1 - c], WS, WR, sibling).wait_recv()
    project(0, 1, 1 - c)
    opposite = lax.rem(y + 2, 4)

    def quarter(ty, tx):
        return wo.at[c, ty, pl.ds(pl.multiple_of(tx * HALF, HALF), HALF)]

    def shard_copy(i):
        ref = quarter(y, x) if i == 2 else wo.at[c, y]
        return remote(ref, ref, OS + i, OR + i, along_y(4 - i))

    def quarter_copy(i):
        ref = quarter(opposite, x)
        return remote(ref, ref, QS + i, QV + i, along_x(i))

    def to_sibling(i):
        ty = lax.rem(y + i, 4)
        return remote(wo.at[c, ty], wo.at[c, ty], FS + i, FT + i, sibling)

    scatter(0, (1,))
    pl.semaphore_wait(line_y, 3)
    scatter(0, (0, 2))
    loads[5].wait()
    shard_copy(2).start()
    for n in (2, 3):
        row_copy(n).wait_recv()
    for s in range(2):
        project(1, 2, s)
    scatter(1, (0, 2, 1))
    scatter(2, (0, 2, 1))
    for n in (4, 5):
        row_copy(n).wait_recv()
    for s in range(2):
        project(3, 1, s)
    scatter(3, (0, 2, 1))
    for i in (1, 3):
        shard_copy(i).start()
    to_sibling(0).start()

    mine = [rb.at[1, c], rb.at[2, c], gb.at[c]]
    theirs = [rb.at[1, 1 - c], rb.at[2, 1 - c], gb.at[1 - c]]

    def swap(n, s):
        drain(mine[n], s)
        remote(mine[n], mine[n], PS + n, PR + n, sibling).start()

    lane = lax.broadcasted_iota(jnp.int32, (1, 128), 1)
    lane_group = jnp.where(lane < 64, lax.rem(lax.div(lane, 4), 8), -1).astype(F32)
    row = lax.rem(lax.broadcasted_iota(jnp.int32, (128, 128), 0), HALF)
    col = lax.broadcasted_iota(jnp.int32, (128, 128), 1)

    def group_columns(half, m):
        table = jnp.concatenate(
            [jnp.broadcast_to(gb[half, 4 * m + n], (HALF, 128)) for n in range(4)], axis=0
        )
        return [
            jnp.sum(jnp.where(col == row + base, table, 0.0), axis=1, keepdims=True)
            for base in (0, HALF)
        ]

    def mark_keys(half, m):
        for_low, for_high = group_columns(half, m)
        hit = jnp.where(lane < 32, for_low, for_high) == lane_group
        key_mark[half, 128 * m : 128 * m + 128, :] = jnp.where(hit, 1.0, 0.0).astype(BF)
        if half is not c:
            return
        group = jnp.concatenate([for_low, for_high], axis=0)
        miss = jnp.where(group == lane_group, 0.0, -(2.0**127))
        query_mark[0, m] = jnp.where(lane < 32, miss, 0.0).astype(BF)
        query_mark[1, m] = jnp.where((lane >= 32) & (lane < 64), miss, 0.0).astype(BF)

    swap(2, GR)
    for m in range(4):
        mark_keys(c, m)
    drain(theirs[2], PR + 2)
    for m in range(4):
        mark_keys(1 - c, m)
    shard_copy(2).wait_recv()
    for i in (1, 2, 3):
        quarter_copy(i).start()
    swap(0, QR + 1)
    swap(1, QR + 2)
    drain(rb.at[0, c], QR)

    def spread_values(half):
        vals = rb[2, half]
        turned = halves(vals)
        vd[half, 0:512, :] = jnp.where(low, vals, turned)
        vd[half, 512:1024, :] = jnp.where(low, turned, vals)

    owner_y, owner_c = lax.rem(z + 3 * lax.div(z, 4), 4), 1 - lax.div(z, 4)
    away = lax.rem(y + 4 - owner_y, 4)
    place = away + lax.div(away, 2) * (5 - 2 * away)
    scale = 0.125 * math.log2(math.e)

    def scores(m, half):
        q = rb[0, c, 128 * m : 128 * m + 128, :]
        turned = halves(q)
        none = jnp.zeros_like(q)
        q_low = jnp.concatenate([jnp.where(low, q, none), jnp.where(low, turned, none)], axis=0)
        q_high = jnp.concatenate([jnp.where(low, none, turned), jnp.where(low, none, q)], axis=0)
        keys = jnp.concatenate([rb[1, half], key_mark[half]], axis=1)
        both = [
            lax.dot_general(
                jnp.concatenate([part, query_mark[n, m]], axis=1), keys, NT,
                preferred_element_type=F32,
            )
            for n, part in enumerate((q_low, q_high))
        ]
        top = jnp.maximum(
            jnp.max(both[0], axis=1, keepdims=True), jnp.max(both[1], axis=1, keepdims=True)
        )
        return both[0], both[1], top

    def weigh(s_low, s_high, top, half):
        p_low = jnp.exp2((s_low - top) * scale)
        p_high = jnp.exp2((s_high - top) * scale)
        total = jnp.sum(p_low, axis=1, keepdims=True) + jnp.sum(p_high, axis=1, keepdims=True)
        mixed = jnp.dot(p_low.astype(BF), vd[half, 0:512, :], preferred_element_type=F32)
        mixed += jnp.dot(p_high.astype(BF), vd[half, 512:1024, :], preferred_element_type=F32)
        return total, mixed

    def first_part(m):
        s_low, s_high, top = scores(m, c)
        total, mixed = weigh(s_low, s_high, top, c)
        top_v[m] = top
        sum_v[m] = total
        acc[m] = mixed

    def second_part(m):
        s_low, s_high, top = scores(m, 1 - c)
        before = top_v[m]
        top = jnp.maximum(before, top)
        total, mixed = weigh(s_low, s_high, top, 1 - c)
        factor = jnp.exp2((before - top) * scale)
        context = (acc[m] * factor + mixed) / (sum_v[m] * factor + total)
        co[128 * m : 128 * m + 128, :] = jnp.where(low, context[:128], context[128:]).astype(BF)
        for k in (2, 1, 3, 0):
            push(
                co.at[pl.ds(128 * m + HALF * turn_x(k), HALF)],
                cb.at[place, lax.div(x, 2), lax.rem(x, 2)],
                CS, CR + lax.div(place, 3), turn_x(k), owner_y, 2 * m + c, owner_c, None if k else spare.at[1],
            )

    spread_values(c)
    for m in range(3):
        first_part(m)
    drain(theirs[0], PR)
    drain(theirs[1], PR + 1)
    spread_values(1 - c)
    for m in range(3):
        second_part(m)
        if m == 0:
            for k in (1, 2, 3):
                quarter_copy(k).wait_recv()
            to_sibling(2).start()
    first_part(3)
    second_part(3)

    for i in (1, 3):
        shard_copy(i).wait_recv()
        to_sibling(i).start()

    for n in range(6):
        row_copy(n).wait_send()
    for i in (1, 2, 3):
        shard_copy(i).wait_send()
        quarter_copy(i).wait_send()
    remote(w_qkv, w.at[c], WS, WR, sibling).wait_send()
    drain(sb, SBS)
    for n in range(3):
        remote(mine[n], mine[n], PS + n, PR + n, sibling).wait_send()
    drain(gb.at[c], GS)
    for i in (1, 2, 3):
        group_copy(i).wait_send()

    def gathered(p):
        both = []
        for tc in range(2):
            even, odd = cb[p, tc, 0], cb[p, tc, 1]
            both.append(
                jnp.concatenate(
                    [jnp.where(low, even, halves(odd)), jnp.where(low, halves(even), odd)], axis=0
                )
            )
        return jnp.concatenate(both, axis=1)

    def product(p, context, cols):
        ty = lax.rem(y + (0, 1, 3, 2)[p], 4)
        ty = ty + 1 - 2 * lax.rem(ty, 2)
        weights = wo[:, ty, :, cols].reshape(256, 256)
        return jnp.dot(context, weights, preferred_element_type=F32)

    drain(cb.at[pl.ds(0, 3)], CR)
    for i in range(4):
        ty = lax.rem(y + i, 4)
        remote(wo.at[c, ty], wo.at[1 - c, ty], FS + i, FT + i, sibling).wait_recv()
    contexts = [gathered(p) for p in range(3)]
    spans = [slice(256 * n, 256 * n + 256) for n in range(5)]
    for cols in spans:
        near[:, cols] = sum(product(p, contexts[p], cols) for p in range(3))
    drain(cb.at[3], CR + 1)
    context = gathered(3)
    for cols in spans:
        out[0, :, cols] = (near[:, cols] + product(3, context, cols)).astype(BF)

    for i in range(4):
        to_sibling(i).wait_send()
    drain(co, CS)


SCRATCH = [
    pltpu.VMEM((ROWS, D), BF),
    pltpu.VMEM((1, ROWS), jnp.int32),
    pltpu.VMEM((1, 32), jnp.int32),
    pltpu.VMEM((D,), F32),
    pltpu.VMEM((4, ROWS, D), BF),
    pltpu.VMEM((2, D, 384), BF),
    pltpu.VMEM((2, 4, 128, D), BF),
    pltpu.VMEM((4, 12, HALF, 128), BF),
    pltpu.VMEM((4, 1, 128), F32),
    pltpu.VMEM((3, 2, 512, 128), BF),
    pltpu.VMEM((2, 16, 1, 128), F32),
    pltpu.VMEM((2, 512, 128), BF),
    pltpu.VMEM((2, 4, 256, 128), BF),
    pltpu.VMEM((2, 1024, 128), BF),
    pltpu.VMEM((512, 128), BF),
    pltpu.VMEM((4, 2, 2, HALF, 128), BF),
    pltpu.VMEM((4, 256, 128), F32),
    pltpu.VMEM((4, 256, 1), F32),
    pltpu.VMEM((4, 256, 1), F32),
    pltpu.VMEM((ROWS, D), F32),
    pltpu.VMEM((2, HALF, 128), BF),
    pltpu.VMEM((1, 128), F32),
    pltpu.SemaphoreType.DMA((NSEM,)),
    pltpu.SemaphoreType.REGULAR,
    pltpu.SemaphoreType.REGULAR,
    pltpu.SemaphoreType.REGULAR,
]


def shards(frames, destination, plan, norm_gain, w_qkv, w_out):
    any_space = pl.BlockSpec(memory_space=pl.ANY)
    return pl.pallas_call(
        kernel,
        out_shape=jax.ShapeDtypeStruct((1, ROWS, D), BF),
        in_specs=[any_space] * 6,
        out_specs=pl.BlockSpec(memory_space=pltpu.VMEM),
        scratch_shapes=SCRATCH,
        compiler_params=pltpu.CompilerParams(
            collective_id=0, has_side_effects=True, vmem_limit_bytes=55008 * 2**10
        ),
        name="attend",
    )(frames, destination.reshape(1, ROWS), plan, norm_gain, w_qkv, w_out)


def solution(mesh):
    in_specs = (
        P("rep", "grp", None),
        P("rep", "grp", None),
        P("rep", None),
        P(),
        P(None, "rep"),
        P("rep", None),
    )
    out_specs = P("rep", "grp", None)
    return jax.shard_map(shards, mesh=mesh, in_specs=in_specs, out_specs=out_specs, check_vma=False)
```
